32 devices in a mesh: lon: 4 (over y, core), lat: 4 (over z), lev: 2 (over x).
Axes of the slice: x: 2, y: 2, z: 4, core: 2. Of those that a mesh axis runs over, the one named last changes fastest.
Arguments:
- fields: float32 [4, 8, 32, 7200], P(None, 'lev', 'lat', 'lon'), may hold values from -6 to 6
- surface: float32 [32, 7200], P('lat', 'lon'), may hold values from -3 to 3
- filter_rows: int32 [16], replicated, may hold values from 0 to 31, as said below
- keep_counts: int32 [16], replicated, may hold values from 1 to 128
Outputs:
- advanced: float32 [4, 8, 32, 7200], P(None, 'lev', 'lat', 'lon')
The draws below stay inside these ranges and needn't reach their ends.
Inputs may be any that keep to these rules, and one draw needn't show every extreme that they name: `filter_rows`: 16 distinct rows in increasing order: exactly 4 of the 8 rows of each aligned block of 8 rows, row 0 and row 31 among them.
All inputs are finite; a program needn't handle non-finite values.
Results may differ from the reference program's by a relative error of at most 0.0001.
Values sent between devices are 32-bit elements; how exact they have to be, the bound alone decides.
No kernel may reach another device: no remote copies, remote signals or barrier semaphores. Data moves between devices by JAX's collectives and lax.ppermute only.
A program may use at most 64 MiB of HBM per device.

```python
import jax
import jax.numpy as jnp
from jax import lax

NLON = 7200
LAT_DEV = 8
KMAX = 128
STEPS = 2
NLAT = 32
LEV = 8
NF = 16


def band_choice(key, band, bands):
    scores = jax.random.permutation(jax.random.fold_in(key, 100 + band), LAT_DEV).astype(jnp.int32)
    local = jnp.arange(LAT_DEV, dtype=jnp.int32)
    if band == 0:
        scores = jnp.where(local == 0, -1, scores)
    if band == bands - 1:
        scores = jnp.where(local == LAT_DEV - 1, -1, scores)
    chosen = jnp.argsort(scores, stable=True)[:LAT_DEV // 2].astype(jnp.int32)
    return jnp.sort(chosen).astype(jnp.int32) + band * LAT_DEV


def draw_filter_rows(key, part):
    bands = NLAT // LAT_DEV
    return jnp.concatenate([band_choice(key, band, bands) for band in range(bands)]).astype(jnp.int32)


def draw_keep_counts(key, part):
    counts = jax.random.randint(jax.random.fold_in(key, 21), (NF,), 1, KMAX + 1)
    where_full = jax.random.randint(jax.random.fold_in(key, 22), (), 0, NF)
    return jnp.where(jnp.arange(NF) == where_full, KMAX, counts).astype(jnp.int32)


def block_scale(own_key, shape, split, smallest, top_value):
    loudness = 1.0
    for dim, shards_of in split:
        steps = jax.random.uniform(jax.random.fold_in(jax.random.fold_in(own_key, 6), dim), (shards_of,), jnp.float32, smallest / len(split), top_value / len(split))
        loudness = loudness * jnp.repeat(jnp.exp(steps), shape[dim] // shards_of).reshape((-1,) + (1,) * (len(shape) - 1 - dim))
    return loudness


def normal_values(rng, shape, deviation, bound, shards=(), kind=jnp.bfloat16):
    drawn = deviation * jax.random.normal(rng, shape, jnp.float32)
    if shards:
        drawn = drawn * block_scale(rng, shape, shards, -0.22, 0.18)
    return jnp.clip(drawn, -bound, bound).astype(kind)


def setup_inputs(seed: int = 0) -> dict:
    splits = jax.random.split(jax.random.key(seed), 5)
    return {
        "fields": normal_values(splits[0], (4, LEV, NLAT, NLON), 1.0, 6.0, ((1, 2), (2, 4), (3, 4)), jnp.float32),
        "surface": normal_values(splits[1], (NLAT, NLON), 0.5, 3.0, ((0, 4), (1, 4)), jnp.float32),
        "filter_rows": draw_filter_rows(jax.random.fold_in(splits[4], 71), 0),
        "keep_counts": draw_keep_counts(jax.random.fold_in(splits[4], 71), 0),
    }


GRAVITY_SCALE = 0.05
BUOYANCY = 0.5
CORIOLIS = 0.3
ZONAL_COEF = 0.08
NORTH_COEF = 0.2
DAMPING = 0.25
FIRST_LAT = -70.0
ROW_STEP = 0.05
PRECISE = lax.Precision.HIGHEST


def row_geometry(row_index):
    based = row_index.astype(jnp.float32)
    to_radian = jnp.pi / 180.0
    middle = (FIRST_LAT + (based + 0.5) * ROW_STEP) * to_radian
    northern = (FIRST_LAT + (based + 1.0) * ROW_STEP) * to_radian
    southern = (FIRST_LAT + based * ROW_STEP) * to_radian
    return (jnp.cos(middle), jnp.cos(northern), jnp.cos(southern),
            CORIOLIS * jnp.sin(middle), CORIOLIS * jnp.sin(northern))


def layer_weight(values):
    return GRAVITY_SCALE * (1.0 + values[2]) * (1.0 + BUOYANCY * values[3])


def advance(padded, geometry):
    cos_mid, cos_north, cos_south, cor_mid, cor_north = [g[:, None] for g in geometry]
    height = padded.shape[-2] - 2
    width = padded.shape[-1] - 2

    def part(which, row_shift, col_shift):
        return padded[which, ..., 1 + row_shift:1 + row_shift + height, 1 + col_shift:1 + col_shift + width]

    zonal = ZONAL_COEF / cos_mid
    uwind_mid, uwind_west, uwind_north, uwind_corner = part(0, 0, 0), part(0, 0, -1), part(0, 1, 0), part(0, 1, -1)
    vwind_mid, vwind_east, vwind_south, vwind_corner = part(1, 0, 0), part(1, 0, 1), part(1, -1, 0), part(1, -1, 1)
    depth_mid, depth_east, depth_west = part(2, 0, 0), part(2, 0, 1), part(2, 0, -1)
    depth_north, depth_south = part(2, 1, 0), part(2, -1, 0)
    heat_mid, heat_east, heat_west = part(3, 0, 0), part(3, 0, 1), part(3, 0, -1)
    heat_north, heat_south = part(3, 1, 0), part(3, -1, 0)
    geopot_mid, geopot_east, geopot_north = part(4, 0, 0), part(4, 0, 1), part(4, 1, 0)
    uwind_new = uwind_mid + cor_mid * 0.25 * (vwind_mid + vwind_east + vwind_south + vwind_corner) - zonal * (geopot_east - geopot_mid)
    vwind_new = vwind_mid - cor_north * 0.25 * (uwind_mid + uwind_west + uwind_north + uwind_corner) - NORTH_COEF * (geopot_north - geopot_mid)
    flux_east = uwind_mid * (2.0 + depth_mid + depth_east) * 0.5
    flux_west = uwind_west * (2.0 + depth_west + depth_mid) * 0.5
    flux_north = vwind_mid * (2.0 + depth_mid + depth_north) * 0.5
    flux_south = vwind_south * (2.0 + depth_south + depth_mid) * 0.5
    depth_new = depth_mid - zonal * (flux_east - flux_west) - NORTH_COEF * (cos_north * flux_north - cos_south * flux_south) / cos_mid
    heat_new = heat_mid - 0.25 * (uwind_mid + uwind_west) * zonal * (heat_east - heat_west) - 0.25 * (vwind_mid + vwind_south) * NORTH_COEF * (heat_north - heat_south)
    return jnp.stack([uwind_new, vwind_new, depth_new, heat_new])


def wave_table(lon_start, count, wave_start, wave_count):
    longitude = lon_start + jnp.arange(count, dtype=jnp.int32)
    wavenumber = wave_start + jnp.arange(wave_count, dtype=jnp.int32)
    angles = ((longitude[:, None] * wavenumber[None, :]) % NLON).astype(jnp.float32) * (2.0 * jnp.pi / NLON)
    return jnp.concatenate([jnp.cos(angles), jnp.sin(angles)], 1)


def mode_weights(keep, wave_start, wave_count):
    wavenumber = wave_start + jnp.arange(wave_count, dtype=jnp.int32)
    scaled = jnp.where(wavenumber == 0, 1.0, 2.0).astype(jnp.float32) / NLON
    kept = jnp.where(wavenumber[None, :] < keep[:, None], scaled[None, :], jnp.zeros((), jnp.float32))
    return jnp.concatenate([kept, kept], 1)


def one_step(fields, surface, filter_rows, keep_counts):
    weight = layer_weight(fields)
    below = jnp.flip(jnp.cumsum(jnp.flip(weight, 0), 0), 0) - weight
    geopot = surface[None] + below + 0.5 * weight
    geometry = row_geometry(jnp.arange(NLAT, dtype=jnp.int32))

    def level_step(level):
        layer = lax.dynamic_index_in_dim(fields, level, 1, keepdims=False)
        stacked = jnp.concatenate([layer, lax.dynamic_index_in_dim(geopot, level, 0, keepdims=True)], 0)
        wrapped = jnp.concatenate([stacked[..., -1:], stacked, stacked[..., :1]], 2)
        padded = jnp.pad(wrapped, ((0, 0), (1, 1), (0, 0)))
        return advance(padded, geometry)

    updated = jnp.transpose(lax.map(level_step, jnp.arange(LEV, dtype=jnp.int32)), (1, 0, 2, 3))
    picked = updated[:, :, filter_rows, :].reshape(4 * LEV, NF, NLON)
    waves = wave_table(0, NLON, 0, KMAX)
    spectra = jnp.einsum("vrn,nk->vrk", picked, waves, precision=PRECISE)
    smooth = jnp.einsum("vrk,nk->vrn", spectra * mode_weights(keep_counts, 0, KMAX), waves, precision=PRECISE)
    change = (DAMPING - 1.0) * (picked - smooth)
    return updated.at[:, :, filter_rows, :].add(change.reshape(4, LEV, NF, NLON))


def reference(fields, surface, filter_rows, keep_counts):
    for count in range(STEPS):
        fields = one_step(fields, surface, filter_rows, keep_counts)
    return fields
```

```python
import functools

import jax
import jax.numpy as jnp
import ml_dtypes
import numpy as np
from jax import lax
from jax.experimental import pallas as pl
from jax.experimental.pallas import tpu as pltpu
from jax.sharding import PartitionSpec as P

KMAX = 128
GRAVITY_SCALE = 0.05
BUOYANCY = 0.5
CORIOLIS = 0.3
ZONAL_COEF = 0.08
NORTH_COEF = 0.2
DAMPING = 0.25
FIRST_LAT = -70.0
ROW_STEP = 0.05
LANES = 128
VMEM_LIMIT = 24 * 1024 * 1024


def layer_weight(h, t):
    return GRAVITY_SCALE * (1.0 + h) * (1.0 + BUOYANCY * t)


def east(x):
    return pltpu.roll(x, x.shape[1] - 1, 1)


def west(x):
    return pltpu.roll(x, 1, 1)


def rows_up(x):
    return pltpu.roll(x, x.shape[0] - 1, 0)


def rows_down(x):
    return pltpu.roll(x, 1, 0)


def row_iota(x):
    return lax.broadcasted_iota(jnp.int32, x.shape, 0)


def with_last(x, row):
    return jnp.where(row_iota(x) == x.shape[0] - 1, jnp.broadcast_to(row, x.shape), rows_up(x))


def with_first(x, row):
    return jnp.where(row_iota(x) == 0, jnp.broadcast_to(row, x.shape), rows_down(x))


def wide(geom, k, lo, hi, width):
    return jnp.concatenate([geom[k, lo:hi, :]] * (width // LANES), 1)


class Sizes:
    def __init__(self, mesh, fields_shape, filter_count):
        _, levels, rows, columns = fields_shape
        self.n_lon, self.n_lat, self.n_lev = (mesh.shape[a] for a in ("lon", "lat", "lev"))
        self.L = levels // self.n_lev
        self.R = rows // self.n_lat
        self.C = columns // self.n_lon
        self.N = columns
        self.W = -(-(self.C + 4) // LANES) * LANES
        self.slots = filter_count // self.n_lat
        self.filters = filter_count
        self.planes = 4 * self.L + 1
        self.base = (self.C - 1) // LANES * LANES
        self.tiles = self.W // LANES
        self.extra = -(-self.tiles // self.R)
        self.lat_rows = -(-(7 * self.L + 1) // 8) * 8
        assert self.R == 2 * self.L and self.n_lon % 2 == 0
        assert 2 <= self.C - self.base <= LANES - 2 and 2 * self.planes <= LANES


def pack_edges(z, fhead, ftail, shead, stail, m1, m2):
    lane = lax.broadcasted_iota(jnp.int32, (z.R, LANES), 1)
    left = jnp.zeros((z.R, LANES), jnp.float32)
    right = left
    first = z.C - 2 - z.base
    for p in range(z.planes):
        f, l = divmod(p, z.L)
        head = fhead[f, l] if p < 4 * z.L else shead[...]
        tail = ftail[f, l] if p < 4 * z.L else stail[...]
        here = (lane >= 2 * p) & (lane < 2 * p + 2)
        left = jnp.where(here, pltpu.roll(head, 2 * p, 1) if p else head, left)
        shift = (2 * p - first) % LANES
        right = jnp.where(here, pltpu.roll(tail, shift, 1) if shift else tail, right)
    even = lax.axis_index("lon") % 2 == 0

    @pl.when(even)
    def _():
        m1[...] = right
        m2[...] = left

    @pl.when(jnp.logical_not(even))
    def _():
        m1[...] = left
        m2[...] = right


def widen(z, fields, surface, r1, r2, x, m1, m2, sums, from_right, from_left):
    lon_even = lax.axis_index("lon") % 2 == 0

    @pl.when(lon_even)
    def _():
        from_right[...] = r1[...]
        from_left[...] = r2[...]

    @pl.when(jnp.logical_not(lon_even))
    def _():
        from_right[...] = r2[...]
        from_left[...] = r1[...]

    lane = lax.broadcasted_iota(jnp.int32, (z.R, LANES), 1)
    last = z.C - z.base
    fr, fl = from_right[...], from_left[...]
    for p in range(z.planes):
        f, l = divmod(p, z.L)
        if p < 4 * z.L:
            x[p, :, 0 : z.C] = fields[f, l]
        else:
            x[p, :, 0 : z.C] = surface[...]
        for start in range(z.base, z.W, LANES):
            if start == z.base:
                tile = jnp.where(lane < last, x[p, :, start : start + LANES], 0.0)
                shift = (last - 2 * p) % LANES
                moved = pltpu.roll(fr, shift, 1) if shift else fr
                tile = jnp.where((lane >= last) & (lane < last + 2), moved, tile)
            else:
                tile = jnp.zeros((z.R, LANES), jnp.float32)
            if start == z.W - LANES:
                moved = pltpu.roll(fl, LANES - 2 - 2 * p, 1)
                tile = jnp.where(lane >= LANES - 2, moved, tile)
            x[p, :, start : start + LANES] = tile

    lat_even = lax.axis_index("lat") % 2 == 0
    near1 = jnp.where(lat_even, z.R - 1, 0)
    far1 = jnp.where(lat_even, z.R - 2, 1)
    for msg, near, far in ((m1, near1, far1), (m2, z.R - 1 - near1, z.R - 1 - far1)):
        for p in range(4 * z.L):
            msg[p : p + 1, :] = x[p, pl.ds(near, 1), :]
        for p in range(z.L, 4 * z.L):
            to = 3 * z.L + p
            msg[to : to + 1, :] = x[p, pl.ds(far, 1), :]
        to = 7 * z.L
        msg[to : to + 1, :] = x[4 * z.L, pl.ds(near, 1), :]
        if z.lat_rows > to + 1:
            msg[to + 1 :, :] = jnp.zeros((z.lat_rows - to - 1, z.W), jnp.float32)
    total = layer_weight(x[2 * z.L], x[3 * z.L])
    for l in range(1, z.L):
        total = total + layer_weight(x[2 * z.L + l], x[3 * z.L + l])
    sums[...] = total


def put_column_sums(z, msg, total, south, north):
    if total is not None:
        msg[:, 0 : z.W] = total
    for d, row in enumerate((south, north)):
        for t in range(z.tiles):
            at = z.W + (d * z.extra + t // z.R) * LANES
            msg[t % z.R : t % z.R + 1, at : at + LANES] = row[:, t * LANES : (t + 1) * LANES]


def ring_sum(z, w):
    south = w[0:1]
    north = w[z.L : z.L + 1]
    for l in range(1, z.L):
        south = south + w[l : l + 1]
        north = north + w[z.L + l : z.L + l + 1]
    return south, north


def halo_rows(z, sums, r1, r2, ring, ring_surface, msg):
    lat_even = lax.axis_index("lat") % 2 == 0

    def place(d, source):
        for k in range(7):
            ring[k, d * z.L : (d + 1) * z.L, :] = source[k * z.L : (k + 1) * z.L, :]
        ring_surface[d * z.L : (d + 1) * z.L, :] = jnp.broadcast_to(
            source[7 * z.L : 7 * z.L + 1, :], (z.L, z.W)
        )

    @pl.when(lat_even)
    def _():
        place(0, r2)
        place(1, r1)

    @pl.when(jnp.logical_not(lat_even))
    def _():
        place(0, r1)
        place(1, r2)

    south, north = ring_sum(z, layer_weight(ring[2], ring[3]))
    put_column_sums(z, msg, sums[...], south, north)


def in_band(z, shape):
    lat = lax.axis_index("lat")
    row = lax.broadcasted_iota(jnp.int32, shape, 0)
    south = jnp.where(lat > 0, 1.0, 0.0)
    north = jnp.where(lat < z.n_lat - 1, 1.0, 0.0)
    return jnp.where(row < z.L, south, north)


def ring_geopot(z, h, t):
    w = layer_weight(h, t)
    row = row_iota(w)
    level = jnp.where(row < z.L, row, row - z.L)
    q = 0.5 * w
    for s in range(1, z.L):
        q = q + jnp.where(level < z.L - s, pltpu.roll(w, 2 * z.L - s, 0), 0.0)
    return q * in_band(z, w.shape)


def tendencies(coef, u, v, h, t, un, vs, hn, hs, tn, ts, q, qn, which="uvht"):
    zonal, cor, corn, north, south = coef
    out = {}
    if "u" in which:
        a = v + vs
        out["u"] = u + cor * (a + east(a)) - zonal * (east(q) - q)
    if "v" in which:
        b = u + un
        out["v"] = v - corn * (b + west(b)) - NORTH_COEF * (qn - q)
    if "h" in which:
        flux = u * (2.0 + h + east(h)) * 0.5
        out["h"] = (
            h
            - zonal * (flux - west(flux))
            - (north * (v * (2.0 + h + hn) * 0.5) - south * (vs * (2.0 + hs + h) * 0.5))
        )
    if "t" in which:
        out["t"] = (
            t
            - 0.25 * (u + west(u)) * zonal * (east(t) - west(t))
            - (0.25 * NORTH_COEF) * (v + vs) * (tn - ts)
        )
    return out


def advance_tile(z, geom, get, un_row, vs_row, h_ring, t_ring, q_ring, put, qput=None):
    coef = [wide(geom, k, 0, z.R, z.W) for k in range(5)]
    below = None
    for l in reversed(range(z.L)):
        u, v, h, t = (get(f, l) for f in range(4))
        w = layer_weight(h, t)
        q = 0.5 * w if below is None else below + 0.5 * w
        below = w if below is None else below + w
        s, n = l, z.L + l
        new = tendencies(
            coef, u, v, h, t,
            with_last(u, un_row(l)), with_first(v, vs_row(l)),
            with_last(h, h_ring[n : n + 1, :]), with_first(h, h_ring[s : s + 1, :]),
            with_last(t, t_ring[n : n + 1, :]), with_first(t, t_ring[s : s + 1, :]),
            q, with_last(q, q_ring[n : n + 1, :]),
        )
        for f, name in enumerate("uvht"):
            put(f, l, new[name])
        if qput is not None:
            qput(l, q)


def first_step(z, x, ring, geom, y, yring, inner, q_ring):
    L = z.L
    q_ring[...] = ring_geopot(z, ring[2], ring[3])

    def get(f, l):
        return x[f * L + l]

    def put(f, l, value):
        y[f * L + l] = value

    def qput(l, q):
        inner[3, l : l + 1, :] = q[0:1]

    inner[3, L:, :] = jnp.zeros((L, z.W), jnp.float32)
    advance_tile(
        z, geom, get,
        lambda l: ring[0, L + l : L + l + 1, :], lambda l: ring[1, l : l + 1, :],
        ring.at[2], ring.at[3], q_ring, put, qput,
    )
    for l in range(L):
        inner[0, l : l + 1, :] = x[l, 0:1, :]
        inner[0, L + l : L + l + 1, :] = x[L + l, z.R - 1 : z.R, :]
        for k, f in ((1, 2), (2, 3)):
            inner[k, l : l + 1, :] = x[f * L + l, 0:1, :]
            inner[k, L + l : L + l + 1, :] = x[f * L + l, z.R - 1 : z.R, :]
    south = lax.broadcasted_iota(jnp.int32, (2 * L, z.W), 0) < L
    coef = [wide(geom, k, z.R, z.R + 2 * L, z.W) for k in range(5)]
    u, v, h, t = (ring[k] for k in range(4))
    new = tendencies(
        coef, u, v, h, t,
        inner[0], jnp.where(south, ring[4], inner[0]),
        jnp.where(south, inner[1], ring[5]), jnp.where(south, ring[5], inner[1]),
        jnp.where(south, inner[2], ring[6]), jnp.where(south, ring[6], inner[2]),
        q_ring[...], inner[3],
    )
    mask = in_band(z, (2 * L, z.W))
    yring[0] = jnp.where(south, new["v"], new["u"]) * mask
    yring[1] = new["h"] * mask
    yring[2] = new["t"] * mask


def level_part(z, surface, ring_surface, got):
    live = jnp.where(lax.axis_index("lev") < z.n_lev - 1, 1.0, 0.0)
    lat = lax.axis_index("lat")
    tile = surface + live * got[:, 0 : z.W]
    rows = []
    for d in range(2):
        there = jnp.where(lat > 0, 1.0, 0.0) if d == 0 else jnp.where(lat < z.n_lat - 1, 1.0, 0.0)
        parts = []
        for t in range(z.tiles):
            at = z.W + (d * z.extra + t // z.R) * LANES
            parts.append(got[t % z.R : t % z.R + 1, at : at + LANES])
        sums = jnp.concatenate(parts, 1)
        rows.append(there * (ring_surface[d * z.L : d * z.L + 1, :] + live * sums))
    return tile, rows[0], rows[1]


def split(x):
    high = x.astype(jnp.bfloat16)
    return high, (x - high.astype(jnp.float32)).astype(jnp.bfloat16)


def dot(a, b, dims):
    return lax.dot_general(a, b, (dims, ((), ())), preferred_element_type=jnp.float32)


def product(x, wh, wl, dims):
    high, low = split(x)
    return dot(high, wh[...], dims) + dot(low, wh[...], dims) + dot(high, wl[...], dims)


def spectra(z, x, wh, wl, phase):
    lane = lax.broadcasted_iota(jnp.int32, (x.shape[0], z.W - z.base), 1)
    tail = jnp.where(lane < z.C - z.base, x[:, z.base :], 0.0)
    if z.base:
        x = jnp.concatenate([x[:, : z.base], tail], 1)
    else:
        x = tail
    s = product(x, wh, wl, ((1,), (0,)))
    a, b = s[:, :KMAX], s[:, KMAX:]
    c, d = phase[0:1, :], phase[1:2, :]
    return jnp.concatenate([a * c - b * d, a * d + b * c], 1)


def slot_row(z, rows, s):
    lat = lax.axis_index("lat")
    return rows[lat * z.slots + s] - lat * z.R


def pick_spectra(z, full, rows, out):
    for s in range(z.slots):
        at = slot_row(z, rows, s)
        for p in range(4 * z.L):
            to = p * z.slots + s
            out[to : to + 1, :] = full[pl.ds(p * z.R + at, 1), :]


def first_spectra(z, y, yring, surface, ring_surface, got, geom, wh, wl, phase, rows, state, sring, out, full):
    L = z.L
    g, gs, gn = level_part(z, surface[...], ring_surface, got)
    du = wide(geom, 0, 0, z.R, z.W) * (east(g) - g)
    dv = NORTH_COEF * (with_last(g, gn) - g)
    for l in range(L):
        state[l] = y[l] - du
        state[L + l] = y[L + l] - dv
    for p in range(2 * L, 4 * L):
        state[p] = y[p]
    south = lax.broadcasted_iota(jnp.int32, (2 * L, z.W), 0) < L
    shape = (2 * L, z.W)
    du_north = wide(geom, 0, z.R, z.R + 2 * L, z.W) * jnp.broadcast_to(east(jnp.broadcast_to(gn, shape)) - gn, shape)
    dv_south = NORTH_COEF * jnp.broadcast_to(g[0:1] - gs, shape)
    sring[0] = yring[0] - jnp.where(south, dv_south, du_north) * in_band(z, shape)
    sring[1] = yring[1]
    sring[2] = yring[2]
    m = 4 * L * z.R
    everything = jnp.concatenate(
        [state[...].reshape(m, z.W), sring[...].reshape(6 * L, z.W)], 0
    )
    full[...] = spectra(z, everything, wh, wl, phase)
    pick_spectra(z, full, rows, out)
    out[4 * L * z.slots :, :] = full[m:, :]


def second_spectra(z, y, surface, ring_surface, got, geom, wh, wl, phase, rows, state, out, full):
    L = z.L
    g, _, gn = level_part(z, surface[...], ring_surface, got)
    du = wide(geom, 0, 0, z.R, z.W) * (east(g) - g)
    dv = NORTH_COEF * (with_last(g, gn) - g)
    for l in range(L):
        state[l] = y[l] - du
        state[L + l] = y[L + l] - dv
    for p in range(2 * L, 4 * L):
        state[p] = y[p]
    full[...] = spectra(z, state[...].reshape(4 * L * z.R, z.W), wh, wl, phase)
    pick_spectra(z, full, rows, out)


def mode_weight(z, keep):
    k = lax.broadcasted_iota(jnp.int32, keep.shape, 1)
    k = jnp.where(k < KMAX, k, k - KMAX)
    scale = jnp.where(k == 0, 1.0 / z.N, 2.0 / z.N)
    return jnp.where(k < keep, scale, 0.0)


def tile_keep(z, rows, keeps, width):
    lat = lax.axis_index("lat")
    r = lax.broadcasted_iota(jnp.int32, (z.R, width), 0)
    keep = jnp.zeros((z.R, width), jnp.int32)
    for s in range(z.slots):
        keep = jnp.where(r == slot_row(z, rows, s), keeps[lat * z.slots + s], keep)
    return keep


def ring_keep(z, rows, keeps, width):
    lat = lax.axis_index("lat")
    before = jnp.maximum(lat * z.slots - 1, 0)
    after = jnp.minimum((lat + 1) * z.slots, z.filters - 1)
    south = jnp.where((lat > 0) & (rows[before] == lat * z.R - 1), keeps[before], 0)
    north = jnp.where((lat < z.n_lat - 1) & (rows[after] == (lat + 1) * z.R), keeps[after], 0)
    r = lax.broadcasted_iota(jnp.int32, (2 * z.L, width), 0)
    return jnp.where(r < z.L, south, north)


def damping(keep):
    return jnp.where(keep > 0, 1.0 - DAMPING, 0.0)


def local_modes(total, phase):
    a, b = total[:, :KMAX], total[:, KMAX:]
    c, d = phase[0:1, :], phase[1:2, :]
    return jnp.concatenate([a * c + b * d, b * c - a * d], 1)


def tile_modes(z, modes, rows, weight, planes):
    r = lax.broadcasted_iota(jnp.int32, (z.R, 2 * KMAX), 0)
    out = []
    for p in planes:
        tile = jnp.zeros((z.R, 2 * KMAX), jnp.float32)
        for s in range(z.slots):
            row = modes[p * z.slots + s : p * z.slots + s + 1, :]
            tile = jnp.where(r == slot_row(z, rows, s), jnp.broadcast_to(row, tile.shape), tile)
        out.append(tile * weight)
    return out


def smooth(modes, wh, wl):
    return product(modes, wh, wl, ((1,), (1,)))


def filter_mass(z, state, sring, part, got, wh, wl, phase, rows, keeps, ht, htring, uvmodes, msg):
    L, m = z.L, 4 * z.L * z.slots
    modes = local_modes(part[...] + got[...], phase)
    keep = tile_keep(z, rows, keeps, 2 * KMAX)
    rkeep = ring_keep(z, rows, keeps, 2 * KMAX)
    weight, rweight = mode_weight(z, keep), mode_weight(z, rkeep)
    ring = [modes[m + k * 2 * L : m + (k + 1) * 2 * L] * rweight for k in range(3)]
    tiles = tile_modes(z, modes, rows, weight, range(4 * L))
    uvmodes[...] = jnp.concatenate(tiles[: 2 * L] + [ring[0]], 0)
    s = smooth(jnp.concatenate(tiles[2 * L :] + ring[1:], 0), wh, wl)
    damp = jnp.broadcast_to(damping(keep[:, 0:1]), (z.R, z.W))
    rdamp = jnp.broadcast_to(damping(rkeep[:, 0:1]), (2 * L, z.W))
    for p in range(2 * L):
        x = state[2 * L + p]
        ht[p] = x + damp * (s[p * z.R : (p + 1) * z.R] - x)
    for k in range(2):
        x = sring[1 + k]
        at = 2 * L * z.R + k * 2 * L
        htring[k] = x + rdamp * (s[at : at + 2 * L] - x)
    total = layer_weight(ht[0], ht[L])
    for l in range(1, L):
        total = total + layer_weight(ht[l], ht[L + l])
    south, north = ring_sum(z, layer_weight(htring[0], htring[1]))
    put_column_sums(z, msg, total, south, north)


def second_step(z, state, sring, uvmodes, ht, htring, geom, wh, wl, rows, keeps, y, uv, uvring, q_ring):
    L = z.L
    s = smooth(uvmodes[...], wh, wl)
    damp = jnp.broadcast_to(damping(tile_keep(z, rows, keeps, LANES)[:, 0:1]), (z.R, z.W))
    rdamp = jnp.broadcast_to(damping(ring_keep(z, rows, keeps, LANES)[:, 0:1]), (2 * L, z.W))
    for p in range(2 * L):
        x = state[p]
        uv[p] = x + damp * (s[p * z.R : (p + 1) * z.R] - x)
    x = sring[0]
    uvring[...] = x + rdamp * (s[2 * L * z.R :] - x)
    q_ring[...] = ring_geopot(z, htring[0], htring[1])

    def get(f, l):
        return uv[f * L + l] if f < 2 else ht[(f - 2) * L + l]

    def put(f, l, value):
        y[f * L + l] = value

    advance_tile(
        z, geom, get,
        lambda l: uvring[L + l : L + l + 1, :], lambda l: uvring[l : l + 1, :],
        htring.at[0], htring.at[1], q_ring, put,
    )


def filter_all(z, state, part, got, wh, wl, phase, rows, keeps, out):
    L = z.L
    modes = local_modes(part[...] + got[...], phase)
    keep = tile_keep(z, rows, keeps, 2 * KMAX)
    tiles = tile_modes(z, modes, rows, mode_weight(z, keep), range(4 * L))
    s = smooth(jnp.concatenate(tiles, 0), wh, wl)
    damp = jnp.broadcast_to(damping(keep[:, 0:1]), (z.R, z.W))
    for p in range(4 * L):
        f, l = divmod(p, L)
        x = state[p]
        new = x + damp * (s[p * z.R : (p + 1) * z.R] - x)
        out[f, l] = new[:, : z.C]


def local(z, wave_high, wave_low, fields, surface, filter_rows, keep_counts):
    L, R, W = z.L, z.R, z.W
    f32 = jnp.float32
    vmem = pl.BlockSpec(memory_space=pltpu.VMEM)
    smem = pl.BlockSpec(memory_space=pltpu.SMEM)

    def call(kernel, outs, ins, scratch=(), flops=1_000_000):
        size = sum(int(np.prod(s)) for s in outs) * 4 + sum(i.size * i.dtype.itemsize for i in ins)
        return pl.pallas_call(
            functools.partial(kernel, z),
            out_shape=[jax.ShapeDtypeStruct(s, f32) for s in outs],
            in_specs=[smem if i.dtype == jnp.int32 else vmem for i in ins],
            out_specs=[vmem] * len(outs),
            scratch_shapes=[pltpu.VMEM(s, f32) for s in scratch],
            compiler_params=pltpu.CompilerParams(vmem_limit_bytes=VMEM_LIMIT),
            cost_estimate=pl.CostEstimate(flops=flops, bytes_accessed=size, transcendentals=0),
            name=kernel.__name__,
        )(*ins)

    lat, lon = lax.axis_index("lat"), lax.axis_index("lon")
    index = lax.broadcasted_iota(jnp.int32, (R + 2 * L, LANES), 0)
    index = jnp.where(index < R, index, jnp.where(index < R + L, -1, R))
    based = (lat * R + index).astype(f32)
    to_radian = jnp.pi / 180.0
    middle = (FIRST_LAT + (based + 0.5) * ROW_STEP) * to_radian
    northern = (FIRST_LAT + (based + 1.0) * ROW_STEP) * to_radian
    southern = (FIRST_LAT + based * ROW_STEP) * to_radian
    cos_mid = jnp.cos(middle)
    geom = jnp.stack(
        [
            ZONAL_COEF / cos_mid,
            (0.25 * CORIOLIS) * jnp.sin(middle),
            (0.25 * CORIOLIS) * jnp.sin(northern),
            NORTH_COEF * jnp.cos(northern) / cos_mid,
            NORTH_COEF * jnp.cos(southern) / cos_mid,
        ]
    )
    turn = (lon * z.C * jnp.arange(KMAX, dtype=jnp.int32)) % z.N
    angle = turn.astype(f32) * (2.0 * jnp.pi / z.N)
    phase = jnp.stack([jnp.cos(angle), jnp.sin(angle)])

    def swaps(n):
        one = [(i, i ^ 1) for i in range(n)]
        return one

    lon_one = [(i, i ^ 1) for i in range(z.n_lon)]
    lon_two = [(i, (((i + 1) % z.n_lon ^ 1) - 1) % z.n_lon) for i in range(z.n_lon)]
    lat_one = [(i, i ^ 1) for i in range(z.n_lat) if i ^ 1 < z.n_lat]
    lat_two = [(i, ((i + 1) ^ 1) - 1) for i in range(1, z.n_lat) if ((i + 1) ^ 1) - 1 < z.n_lat]

    def from_below(column):
        if z.n_lev == 2:
            return lax.ppermute(column, "lev", [(0, 1), (1, 0)])
        place = lax.axis_index("lev")
        total = jnp.zeros_like(column)
        for s in range(1, z.n_lev):
            got = lax.ppermute(column, "lev", [(i, i - s) for i in range(s, z.n_lev)])
            total = total + jnp.where(place + s < z.n_lev, got, 0.0)
        return total

    def over_lon(part):
        got, step = None, 1
        while step < z.n_lon:
            if got is not None:
                part = part + got
            got = lax.ppermute(part, "lon", [(i, i ^ step) for i in range(z.n_lon)])
            step *= 2
        return part, got

    head = lambda i: (0, 0, 0, 0)
    tail = lambda i: (0, 0, 0, z.base // LANES)
    edge = pl.BlockSpec((R, LANES), lambda i: (0, 0))
    e1, e2 = pl.pallas_call(
        functools.partial(pack_edges, z),
        grid=(1,),
        out_shape=[jax.ShapeDtypeStruct((R, LANES), f32)] * 2,
        in_specs=[
            pl.BlockSpec((4, L, R, LANES), head),
            pl.BlockSpec((4, L, R, LANES), tail),
            edge,
            pl.BlockSpec((R, LANES), lambda i: (0, z.base // LANES)),
        ],
        out_specs=[edge] * 2,
        name="pack_edges",
    )(fields, fields, surface, surface)
    e1 = lax.ppermute(e1, "lon", lon_one)
    e2 = lax.ppermute(e2, "lon", lon_two)

    x, m1, m2, sums = call(
        widen,
        [(z.planes, R, W), (z.lat_rows, W), (z.lat_rows, W), (R, W)],
        [fields, surface, e1, e2],
        [(R, LANES)] * 2,
    )
    m1 = lax.ppermute(m1, "lat", lat_one)
    m2 = lax.ppermute(m2, "lat", lat_two)

    sent = (R, W + 2 * z.extra * LANES)
    ring, ring_surface, msg = call(
        halo_rows, [(7, 2 * L, W), (2 * L, W), sent], [sums, m1, m2]
    )
    got = from_below(msg)
    y, yring = call(
        first_step,
        [(4 * L, R, W), (3, 2 * L, W)],
        [x, ring, geom],
        [(4, 2 * L, W), (2 * L, W)],
        flops=10_000_000,
    )
    m = 4 * L * R
    surface_tile = x[4 * L]
    state, sring, part = call(
        first_spectra,
        [(4 * L, R, W), (3, 2 * L, W), (4 * L * z.slots + 6 * L, 2 * KMAX)],
        [y, yring, surface_tile, ring_surface, got, geom, wave_high, wave_low, phase, filter_rows],
        [(m + 6 * L, 2 * KMAX)],
    )
    part, got = over_lon(part)
    ht, htring, uvmodes, msg = call(
        filter_mass,
        [(2 * L, R, W), (2, 2 * L, W), (2 * L * R + 2 * L, 2 * KMAX), sent],
        [state, sring, part, got, wave_high, wave_low, phase, filter_rows, keep_counts],
    )
    got = from_below(msg)
    (y,) = call(
        second_step,
        [(4 * L, R, W)],
        [state, sring, uvmodes, ht, htring, geom, wave_high, wave_low, filter_rows, keep_counts],
        [(2 * L, R, W), (2 * L, W), (2 * L, W)],
        flops=10_000_000,
    )
    state, part = call(
        second_spectra,
        [(4 * L, R, W), (4 * L * z.slots, 2 * KMAX)],
        [y, surface_tile, ring_surface, got, geom, wave_high, wave_low, phase, filter_rows],
        [(m, 2 * KMAX)],
    )
    part, got = over_lon(part)
    (out,) = call(
        filter_all,
        [(4, L, R, z.C)],
        [state, part, got, wave_high, wave_low, phase, filter_rows, keep_counts],
    )
    return out


def wave_tables(z):
    lane = np.arange(z.W)
    j = np.where(lane >= z.W - 2, lane - z.W, lane)
    angle = 2.0 * np.pi * ((j[:, None] * np.arange(KMAX)[None, :]) % z.N) / z.N
    table = np.concatenate([np.cos(angle), np.sin(angle)], 1).astype(np.float32)
    high = table.astype(ml_dtypes.bfloat16)
    low = (table - high.astype(np.float32)).astype(ml_dtypes.bfloat16)
    return high, low


def solution(mesh):
    def run(fields, surface, filter_rows, keep_counts):
        z = Sizes(mesh, fields.shape, filter_rows.shape[0])
        high, low = wave_tables(z)

        def body(fields, surface, filter_rows, keep_counts):
            return local(
                z, jnp.asarray(high), jnp.asarray(low), fields, surface, filter_rows, keep_counts
            )

        spec = P(None, "lev", "lat", "lon")
        return jax.shard_map(
            body,
            mesh=mesh,
            in_specs=(spec, P("lat", "lon"), P(), P()),
            out_specs=spec,
            check_vma=False,
        )(fields, surface, filter_rows, keep_counts)

    return run
```

```python
import functools

import jax
import jax.numpy as jnp
import ml_dtypes
import numpy as np
from jax import lax
from jax.experimental import pallas as pl
from jax.experimental.pallas import tpu as pltpu
from jax.sharding import PartitionSpec as P

KMAX = 128
GRAVITY_SCALE = 0.05
BUOYANCY = 0.5
CORIOLIS = 0.3
ZONAL_COEF = 0.08
NORTH_COEF = 0.2
DAMPING = 0.25
FIRST_LAT = -70.0
ROW_STEP = 0.05
LANES = 128
VMEM_LIMIT = 24 * 1024 * 1024


def layer_weight(h, t):
    return GRAVITY_SCALE * (1.0 + h) * (1.0 + BUOYANCY * t)


def east(x):
    return pltpu.roll(x, x.shape[1] - 1, 1)


def west(x):
    return pltpu.roll(x, 1, 1)


def rows_up(x):
    return pltpu.roll(x, x.shape[0] - 1, 0)


def rows_down(x):
    return pltpu.roll(x, 1, 0)


def row_iota(x):
    return lax.broadcasted_iota(jnp.int32, x.shape, 0)


def with_last(x, row):
    return jnp.where(row_iota(x) == x.shape[0] - 1, jnp.broadcast_to(row, x.shape), rows_up(x))


def with_first(x, row):
    return jnp.where(row_iota(x) == 0, jnp.broadcast_to(row, x.shape), rows_down(x))


def wide(geom, k, lo, hi, width):
    return jnp.concatenate([geom[k, lo:hi, :]] * (width // LANES), 1)


class Sizes:
    def __init__(self, mesh, fields_shape, filter_count):
        _, levels, rows, columns = fields_shape
        self.n_lon, self.n_lat, self.n_lev = (mesh.shape[a] for a in ("lon", "lat", "lev"))
        self.L = levels // self.n_lev
        self.R = rows // self.n_lat
        self.C = columns // self.n_lon
        self.N = columns
        self.W = -(-(self.C + 4) // LANES) * LANES
        self.slots = filter_count // self.n_lat
        self.filters = filter_count
        self.planes = 4 * self.L + 1
        self.base = (self.C - 1) // LANES * LANES
        self.tiles = self.W // LANES
        self.extra = -(-self.tiles // self.R)
        self.lat_rows = -(-(7 * self.L + 1) // 8) * 8
        width = -(-self.base // LANES // 3) * LANES if self.base else self.W
        cuts = [c for c in range(0, self.base + 1, width)] if self.base else [0]
        if self.C - cuts[-1] <= LANES and len(cuts) > 1:
            cuts.pop()
        self.chunks = list(zip(cuts, cuts[1:] + [self.C]))
        assert self.R == 2 * self.L and self.n_lon % 2 == 0
        assert 2 <= self.C - self.base <= LANES - 2 and 2 * self.planes <= LANES


def pack_edges(z, fhead, ftail, shead, stail, m1, m2):
    lane = lax.broadcasted_iota(jnp.int32, (z.R, LANES), 1)
    left = jnp.zeros((z.R, LANES), jnp.float32)
    right = left
    first = z.C - 2 - z.base
    for p in range(z.planes):
        f, l = divmod(p, z.L)
        head = fhead[f, l] if p < 4 * z.L else shead[...]
        tail = ftail[f, l] if p < 4 * z.L else stail[...]
        here = (lane >= 2 * p) & (lane < 2 * p + 2)
        left = jnp.where(here, pltpu.roll(head, 2 * p, 1) if p else head, left)
        shift = (2 * p - first) % LANES
        right = jnp.where(here, pltpu.roll(tail, shift, 1) if shift else tail, right)
    even = lax.axis_index("lon") % 2 == 0

    @pl.when(even)
    def _():
        m1[...] = right
        m2[...] = left

    @pl.when(jnp.logical_not(even))
    def _():
        m1[...] = left
        m2[...] = right


def widen(z, fields, surface, r1, r2, rows, keeps, x, m1, m2, sums, from_right, from_left):
    lon_even = lax.axis_index("lon") % 2 == 0

    @pl.when(lon_even)
    def _():
        from_right[...] = r1[...]
        from_left[...] = r2[...]

    @pl.when(jnp.logical_not(lon_even))
    def _():
        from_right[...] = r2[...]
        from_left[...] = r1[...]

    lane = lax.broadcasted_iota(jnp.int32, (z.R, LANES), 1)
    last = z.C - z.base
    fr, fl = from_right[...], from_left[...]
    for p in range(z.planes):
        f, l = divmod(p, z.L)
        if p < 4 * z.L:
            x[p, :, 0 : z.C] = fields[f, l]
        else:
            x[p, :, 0 : z.C] = surface[...]
        for start in range(z.base, z.W, LANES):
            if start == z.base:
                tile = jnp.where(lane < last, x[p, :, start : start + LANES], 0.0)
                shift = (last - 2 * p) % LANES
                moved = pltpu.roll(fr, shift, 1) if shift else fr
                tile = jnp.where((lane >= last) & (lane < last + 2), moved, tile)
            else:
                tile = jnp.zeros((z.R, LANES), jnp.float32)
            if start == z.W - LANES:
                moved = pltpu.roll(fl, LANES - 2 - 2 * p, 1)
                tile = jnp.where(lane >= LANES - 2, moved, tile)
            x[p, :, start : start + LANES] = tile

    lat_even = lax.axis_index("lat") % 2 == 0
    near1 = jnp.where(lat_even, z.R - 1, 0)
    far1 = jnp.where(lat_even, z.R - 2, 1)
    for msg, near, far in ((m1, near1, far1), (m2, z.R - 1 - near1, z.R - 1 - far1)):
        for p in range(4 * z.L):
            msg[p : p + 1, :] = x[p, pl.ds(near, 1), :]
        for p in range(z.L, 4 * z.L):
            to = 3 * z.L + p
            msg[to : to + 1, :] = x[p, pl.ds(far, 1), :]
        to = 7 * z.L
        msg[to : to + 1, :] = x[4 * z.L, pl.ds(near, 1), :]
        if z.lat_rows > to + 1:
            msg[to + 1 :, :] = jnp.zeros((z.lat_rows - to - 1, z.W), jnp.float32)
    total = layer_weight(x[2 * z.L], x[3 * z.L])
    for l in range(1, z.L):
        total = total + layer_weight(x[2 * z.L + l], x[3 * z.L + l])
    sums[...] = total


def put_column_sums(z, msg, total, south, north):
    if total is not None:
        msg[:, 0 : z.W] = total
    for d, row in enumerate((south, north)):
        for t in range(z.tiles):
            at = z.W + (d * z.extra + t // z.R) * LANES
            msg[t % z.R : t % z.R + 1, at : at + LANES] = row[:, t * LANES : (t + 1) * LANES]


def ring_sum(z, w):
    south = w[0:1]
    north = w[z.L : z.L + 1]
    for l in range(1, z.L):
        south = south + w[l : l + 1]
        north = north + w[z.L + l : z.L + l + 1]
    return south, north


def halo_rows(z, sums, r1, r2, ring, ring_surface, msg):
    lat_even = lax.axis_index("lat") % 2 == 0

    def place(d, source):
        for k in range(7):
            ring[k, d * z.L : (d + 1) * z.L, :] = source[k * z.L : (k + 1) * z.L, :]
        ring_surface[d * z.L : (d + 1) * z.L, :] = jnp.broadcast_to(
            source[7 * z.L : 7 * z.L + 1, :], (z.L, z.W)
        )

    @pl.when(lat_even)
    def _():
        place(0, r2)
        place(1, r1)

    @pl.when(jnp.logical_not(lat_even))
    def _():
        place(0, r1)
        place(1, r2)

    south, north = ring_sum(z, layer_weight(ring[2], ring[3]))
    put_column_sums(z, msg, sums[...], south, north)


def in_band(z, shape):
    lat = lax.axis_index("lat")
    row = lax.broadcasted_iota(jnp.int32, shape, 0)
    south = jnp.where(lat > 0, 1.0, 0.0)
    north = jnp.where(lat < z.n_lat - 1, 1.0, 0.0)
    return jnp.where(row < z.L, south, north)


def ring_geopot(z, h, t):
    w = layer_weight(h, t)
    row = row_iota(w)
    level = jnp.where(row < z.L, row, row - z.L)
    q = 0.5 * w
    for s in range(1, z.L):
        q = q + jnp.where(level < z.L - s, pltpu.roll(w, 2 * z.L - s, 0), 0.0)
    return q * in_band(z, w.shape)


def tendencies(coef, u, v, h, t, un, vs, hn, hs, tn, ts, q, qn, which="uvht"):
    zonal, cor, corn, north, south = coef
    out = {}
    if "u" in which:
        a = v + vs
        out["u"] = u + cor * (a + east(a)) - zonal * (east(q) - q)
    if "v" in which:
        b = u + un
        out["v"] = v - corn * (b + west(b)) - NORTH_COEF * (qn - q)
    if "h" in which:
        flux = u * (2.0 + h + east(h)) * 0.5
        out["h"] = (
            h
            - zonal * (flux - west(flux))
            - (north * (v * (2.0 + h + hn) * 0.5) - south * (vs * (2.0 + hs + h) * 0.5))
        )
    if "t" in which:
        out["t"] = (
            t
            - 0.25 * (u + west(u)) * zonal * (east(t) - west(t))
            - (0.25 * NORTH_COEF) * (v + vs) * (tn - ts)
        )
    return out


def advance_tile(z, geom, get, un_row, vs_row, h_ring, t_ring, q_ring, put, qput=None):
    coef = [wide(geom, k, 0, z.R, z.W) for k in range(5)]
    below = None
    for l in reversed(range(z.L)):
        u, v, h, t = (get(f, l) for f in range(4))
        w = layer_weight(h, t)
        q = 0.5 * w if below is None else below + 0.5 * w
        below = w if below is None else below + w
        s, n = l, z.L + l
        new = tendencies(
            coef, u, v, h, t,
            with_last(u, un_row(l)), with_first(v, vs_row(l)),
            with_last(h, h_ring[n : n + 1, :]), with_first(h, h_ring[s : s + 1, :]),
            with_last(t, t_ring[n : n + 1, :]), with_first(t, t_ring[s : s + 1, :]),
            q, with_last(q, q_ring[n : n + 1, :]),
        )
        for f, name in enumerate("uvht"):
            put(f, l, new[name])
        if qput is not None:
            qput(l, q)


def first_step(z, x, ring, geom, y, yring, inner, q_ring):
    L = z.L
    q_ring[...] = ring_geopot(z, ring[2], ring[3])

    def get(f, l):
        return x[f * L + l]

    def put(f, l, value):
        y[f * L + l] = value

    def qput(l, q):
        inner[3, l : l + 1, :] = q[0:1]

    inner[3, L:, :] = jnp.zeros((L, z.W), jnp.float32)
    advance_tile(
        z, geom, get,
        lambda l: ring[0, L + l : L + l + 1, :], lambda l: ring[1, l : l + 1, :],
        ring.at[2], ring.at[3], q_ring, put, qput,
    )
    for l in range(L):
        inner[0, l : l + 1, :] = x[l, 0:1, :]
        inner[0, L + l : L + l + 1, :] = x[L + l, z.R - 1 : z.R, :]
        for k, f in ((1, 2), (2, 3)):
            inner[k, l : l + 1, :] = x[f * L + l, 0:1, :]
            inner[k, L + l : L + l + 1, :] = x[f * L + l, z.R - 1 : z.R, :]
    south = lax.broadcasted_iota(jnp.int32, (2 * L, z.W), 0) < L
    coef = [wide(geom, k, z.R, z.R + 2 * L, z.W) for k in range(5)]
    u, v, h, t = (ring[k] for k in range(4))
    new = tendencies(
        coef, u, v, h, t,
        inner[0], jnp.where(south, ring[4], inner[0]),
        jnp.where(south, inner[1], ring[5]), jnp.where(south, ring[5], inner[1]),
        jnp.where(south, inner[2], ring[6]), jnp.where(south, ring[6], inner[2]),
        q_ring[...], inner[3],
    )
    mask = in_band(z, (2 * L, z.W))
    yring[0] = jnp.where(south, new["v"], new["u"]) * mask
    yring[1] = new["h"] * mask
    yring[2] = new["t"] * mask


def level_part(z, surface, ring_surface, got):
    live = jnp.where(lax.axis_index("lev") < z.n_lev - 1, 1.0, 0.0)
    lat = lax.axis_index("lat")
    tile = surface + live * got[:, 0 : z.W]
    rows = []
    for d in range(2):
        there = jnp.where(lat > 0, 1.0, 0.0) if d == 0 else jnp.where(lat < z.n_lat - 1, 1.0, 0.0)
        parts = []
        for t in range(z.tiles):
            at = z.W + (d * z.extra + t // z.R) * LANES
            parts.append(got[t % z.R : t % z.R + 1, at : at + LANES])
        sums = jnp.concatenate(parts, 1)
        rows.append(there * (ring_surface[d * z.L : d * z.L + 1, :] + live * sums))
    return tile, rows[0], rows[1]


def split(x):
    high = x.astype(jnp.bfloat16)
    return high, (x - high.astype(jnp.float32)).astype(jnp.bfloat16)


def dot(a, b, dims):
    return lax.dot_general(a, b, (dims, ((), ())), preferred_element_type=jnp.float32)


def product(x, wh, wl, dims):
    high, low = split(x)
    return dot(high, wh[...], dims) + dot(low, wh[...], dims) + dot(high, wl[...], dims)


def spectra(z, x, wh, wl, phase):
    lane = lax.broadcasted_iota(jnp.int32, (x.shape[0], z.W - z.base), 1)
    tail = jnp.where(lane < z.C - z.base, x[:, z.base :], 0.0)
    if z.base:
        x = jnp.concatenate([x[:, : z.base], tail], 1)
    else:
        x = tail
    s = product(x, wh, wl, ((1,), (0,)))
    a, b = s[:, :KMAX], s[:, KMAX:]
    c, d = phase[0:1, :], phase[1:2, :]
    return jnp.concatenate([a * c - b * d, a * d + b * c], 1)


def slot_row(z, rows, s):
    lat = lax.axis_index("lat")
    return rows[lat * z.slots + s] - lat * z.R


def pick_spectra(z, full, rows, out):
    for s in range(z.slots):
        at = slot_row(z, rows, s)
        for p in range(4 * z.L):
            to = p * z.slots + s
            out[to : to + 1, :] = full[pl.ds(p * z.R + at, 1), :]


def first_spectra(z, y, yring, surface, ring_surface, got, geom, wh, wl, phase, rows, state, sring, out, full):
    L = z.L
    g, gs, gn = level_part(z, surface[...], ring_surface, got)
    du = wide(geom, 0, 0, z.R, z.W) * (east(g) - g)
    dv = NORTH_COEF * (with_last(g, gn) - g)
    for l in range(L):
        state[l] = y[l] - du
        state[L + l] = y[L + l] - dv
    for p in range(2 * L, 4 * L):
        state[p] = y[p]
    south = lax.broadcasted_iota(jnp.int32, (2 * L, z.W), 0) < L
    shape = (2 * L, z.W)
    du_north = wide(geom, 0, z.R, z.R + 2 * L, z.W) * jnp.broadcast_to(east(jnp.broadcast_to(gn, shape)) - gn, shape)
    dv_south = NORTH_COEF * jnp.broadcast_to(g[0:1] - gs, shape)
    sring[0] = yring[0] - jnp.where(south, dv_south, du_north) * in_band(z, shape)
    sring[1] = yring[1]
    sring[2] = yring[2]
    m = 4 * L * z.R
    everything = jnp.concatenate(
        [state[...].reshape(m, z.W), sring[...].reshape(6 * L, z.W)], 0
    )
    full[...] = spectra(z, everything, wh, wl, phase)
    pick_spectra(z, full, rows, out)
    out[4 * L * z.slots :, :] = full[m:, :]


def second_spectra(z, y, surface, ring_surface, got, geom, wh, wl, phase, rows, state, out, full):
    L = z.L
    g, _, gn = level_part(z, surface[...], ring_surface, got)
    du = wide(geom, 0, 0, z.R, z.W) * (east(g) - g)
    dv = NORTH_COEF * (with_last(g, gn) - g)
    for l in range(L):
        state[l] = y[l] - du
        state[L + l] = y[L + l] - dv
    for p in range(2 * L, 4 * L):
        state[p] = y[p]
    full[...] = spectra(z, state[...].reshape(4 * L * z.R, z.W), wh, wl, phase)
    pick_spectra(z, full, rows, out)


def mode_weight(z, keep):
    k = lax.broadcasted_iota(jnp.int32, keep.shape, 1)
    k = jnp.where(k < KMAX, k, k - KMAX)
    scale = jnp.where(k == 0, 1.0 / z.N, 2.0 / z.N)
    return jnp.where(k < keep, scale, 0.0)


def tile_keep(z, rows, keeps, width):
    lat = lax.axis_index("lat")
    r = lax.broadcasted_iota(jnp.int32, (z.R, width), 0)
    keep = jnp.zeros((z.R, width), jnp.int32)
    for s in range(z.slots):
        keep = jnp.where(r == slot_row(z, rows, s), keeps[lat * z.slots + s], keep)
    return keep


def ring_keep(z, rows, keeps, width):
    lat = lax.axis_index("lat")
    before = jnp.maximum(lat * z.slots - 1, 0)
    after = jnp.minimum((lat + 1) * z.slots, z.filters - 1)
    south = jnp.where((lat > 0) & (rows[before] == lat * z.R - 1), keeps[before], 0)
    north = jnp.where((lat < z.n_lat - 1) & (rows[after] == (lat + 1) * z.R), keeps[after], 0)
    r = lax.broadcasted_iota(jnp.int32, (2 * z.L, width), 0)
    return jnp.where(r < z.L, south, north)


def damping(keep):
    return jnp.where(keep > 0, 1.0 - DAMPING, 0.0)


def local_modes(total, phase):
    a, b = total[:, :KMAX], total[:, KMAX:]
    c, d = phase[0:1, :], phase[1:2, :]
    return jnp.concatenate([a * c + b * d, b * c - a * d], 1)


def tile_modes(z, modes, rows, weight, planes):
    r = lax.broadcasted_iota(jnp.int32, (z.R, 2 * KMAX), 0)
    out = []
    for p in planes:
        tile = jnp.zeros((z.R, 2 * KMAX), jnp.float32)
        for s in range(z.slots):
            row = modes[p * z.slots + s : p * z.slots + s + 1, :]
            tile = jnp.where(r == slot_row(z, rows, s), jnp.broadcast_to(row, tile.shape), tile)
        out.append(tile * weight)
    return out


def smooth(modes, wh, wl):
    return product(modes, wh, wl, ((1,), (1,)))


def filter_mass(z, state, sring, part, got, wh, wl, phase, rows, keeps, ht, htring, uvmodes, msg):
    L, m = z.L, 4 * z.L * z.slots
    modes = local_modes(part[...] + got[...], phase)
    keep = tile_keep(z, rows, keeps, 2 * KMAX)
    rkeep = ring_keep(z, rows, keeps, 2 * KMAX)
    weight, rweight = mode_weight(z, keep), mode_weight(z, rkeep)
    ring = [modes[m + k * 2 * L : m + (k + 1) * 2 * L] * rweight for k in range(3)]
    tiles = tile_modes(z, modes, rows, weight, range(4 * L))
    uvmodes[...] = jnp.concatenate(tiles[: 2 * L] + [ring[0]], 0)
    s = smooth(jnp.concatenate(tiles[2 * L :] + ring[1:], 0), wh, wl)
    damp = jnp.broadcast_to(damping(keep[:, 0:1]), (z.R, z.W))
    rdamp = jnp.broadcast_to(damping(rkeep[:, 0:1]), (2 * L, z.W))
    for p in range(2 * L):
        x = state[2 * L + p]
        ht[p] = x + damp * (s[p * z.R : (p + 1) * z.R] - x)
    for k in range(2):
        x = sring[1 + k]
        at = 2 * L * z.R + k * 2 * L
        htring[k] = x + rdamp * (s[at : at + 2 * L] - x)
    total = layer_weight(ht[0], ht[L])
    for l in range(1, L):
        total = total + layer_weight(ht[l], ht[L + l])
    south, north = ring_sum(z, layer_weight(htring[0], htring[1]))
    put_column_sums(z, msg, total, south, north)


def second_step(z, state, sring, uvmodes, ht, htring, geom, wh, wl, rows, keeps, y, uv, uvring, q_ring):
    L = z.L
    s = smooth(uvmodes[...], wh, wl)
    damp = jnp.broadcast_to(damping(tile_keep(z, rows, keeps, LANES)[:, 0:1]), (z.R, z.W))
    rdamp = jnp.broadcast_to(damping(ring_keep(z, rows, keeps, LANES)[:, 0:1]), (2 * L, z.W))
    for p in range(2 * L):
        x = state[p]
        uv[p] = x + damp * (s[p * z.R : (p + 1) * z.R] - x)
    x = sring[0]
    uvring[...] = x + rdamp * (s[2 * L * z.R :] - x)
    q_ring[...] = ring_geopot(z, htring[0], htring[1])

    def get(f, l):
        return uv[f * L + l] if f < 2 else ht[(f - 2) * L + l]

    def put(f, l, value):
        y[f * L + l] = value

    advance_tile(
        z, geom, get,
        lambda l: uvring[L + l : L + l + 1, :], lambda l: uvring[l : l + 1, :],
        htring.at[0], htring.at[1], q_ring, put,
    )


def filter_all(z, state, part, got, wh, wl, phase, rows, keeps, out, held, sem):
    L = z.L
    modes = local_modes(part[...] + got[...], phase)
    keep = tile_keep(z, rows, keeps, 2 * KMAX)
    tiles = tile_modes(z, modes, rows, mode_weight(z, keep), range(4 * L))
    high, low = split(jnp.concatenate(tiles, 0))
    damp = damping(keep[:, 0:1])
    across = ((1,), (1,))
    copies = []
    for i, (lo, hi) in enumerate(z.chunks):
        top = min(-(-hi // LANES) * LANES, z.W)
        w, v = wh[lo:top, :], wl[lo:top, :]
        s = dot(high, w, across) + dot(low, w, across) + dot(high, v, across)
        d = jnp.broadcast_to(damp, (z.R, top - lo))
        for p in range(4 * L):
            x = state[p, :, lo:top]
            new = x + d * (s[p * z.R : (p + 1) * z.R] - x)
            held[p // L, p % L, :, lo:hi] = new[:, : hi - lo]
        copies.append(
            pltpu.make_async_copy(held.at[:, :, :, lo:hi], out.at[:, :, :, lo:hi], sem.at[i])
        )
        copies[-1].start()
    for copy in copies:
        copy.wait()


def local(z, wave_high, wave_low, fields, surface, filter_rows, keep_counts):
    L, R, W = z.L, z.R, z.W
    f32 = jnp.float32
    vmem = pl.BlockSpec(memory_space=pltpu.VMEM)
    smem = pl.BlockSpec(memory_space=pltpu.SMEM)

    def call(kernel, outs, ins, scratch=(), flops=1_000_000):
        size = sum(int(np.prod(s)) for s in outs) * 4 + sum(i.size * i.dtype.itemsize for i in ins)
        return pl.pallas_call(
            functools.partial(kernel, z),
            out_shape=[jax.ShapeDtypeStruct(s, f32) for s in outs],
            in_specs=[smem if i.dtype == jnp.int32 else vmem for i in ins],
            out_specs=[vmem] * len(outs),
            scratch_shapes=[pltpu.VMEM(s, f32) for s in scratch],
            compiler_params=pltpu.CompilerParams(vmem_limit_bytes=VMEM_LIMIT),
            cost_estimate=pl.CostEstimate(flops=flops, bytes_accessed=size, transcendentals=0),
            name=kernel.__name__,
        )(*ins)

    lat, lon = lax.axis_index("lat"), lax.axis_index("lon")
    index = lax.broadcasted_iota(jnp.int32, (R + 2 * L, LANES), 0)
    index = jnp.where(index < R, index, jnp.where(index < R + L, -1, R))
    based = (lat * R + index).astype(f32)
    to_radian = jnp.pi / 180.0
    middle = (FIRST_LAT + (based + 0.5) * ROW_STEP) * to_radian
    northern = (FIRST_LAT + (based + 1.0) * ROW_STEP) * to_radian
    southern = (FIRST_LAT + based * ROW_STEP) * to_radian
    cos_mid = jnp.cos(middle)
    geom = jnp.stack(
        [
            ZONAL_COEF / cos_mid,
            (0.25 * CORIOLIS) * jnp.sin(middle),
            (0.25 * CORIOLIS) * jnp.sin(northern),
            NORTH_COEF * jnp.cos(northern) / cos_mid,
            NORTH_COEF * jnp.cos(southern) / cos_mid,
        ]
    )
    turn = (lon * z.C * jnp.arange(KMAX, dtype=jnp.int32)) % z.N
    angle = turn.astype(f32) * (2.0 * jnp.pi / z.N)
    phase = jnp.stack([jnp.cos(angle), jnp.sin(angle)])

    lon_one = [(i, i ^ 1) for i in range(z.n_lon)]
    lon_two = [(i, (((i + 1) % z.n_lon ^ 1) - 1) % z.n_lon) for i in range(z.n_lon)]
    lat_one = [(i, i ^ 1) for i in range(z.n_lat) if i ^ 1 < z.n_lat]
    lat_two = [(i, ((i + 1) ^ 1) - 1) for i in range(1, z.n_lat) if ((i + 1) ^ 1) - 1 < z.n_lat]

    def from_below(column):
        if z.n_lev == 2:
            return lax.ppermute(column, "lev", [(0, 1), (1, 0)])
        place = lax.axis_index("lev")
        total = jnp.zeros_like(column)
        for s in range(1, z.n_lev):
            got = lax.ppermute(column, "lev", [(i, i - s) for i in range(s, z.n_lev)])
            total = total + jnp.where(place + s < z.n_lev, got, 0.0)
        return total

    def over_lon(part):
        got, step = None, 1
        while step < z.n_lon:
            if got is not None:
                part = part + got
            got = lax.ppermute(part, "lon", [(i, i ^ step) for i in range(z.n_lon)])
            step *= 2
        return part, got

    head = lambda i: (0, 0, 0, 0)
    tail = lambda i: (0, 0, 0, z.base // LANES)
    edge = pl.BlockSpec((R, LANES), lambda i: (0, 0))
    e1, e2 = pl.pallas_call(
        functools.partial(pack_edges, z),
        grid=(1,),
        out_shape=[jax.ShapeDtypeStruct((R, LANES), f32)] * 2,
        in_specs=[
            pl.BlockSpec((4, L, R, LANES), head),
            pl.BlockSpec((4, L, R, LANES), tail),
            edge,
            pl.BlockSpec((R, LANES), lambda i: (0, z.base // LANES)),
        ],
        out_specs=[edge] * 2,
        name="pack_edges",
    )(fields, fields, surface, surface)
    e1 = lax.ppermute(e1, "lon", lon_one)
    e2 = lax.ppermute(e2, "lon", lon_two)

    x, m1, m2, sums = call(
        widen,
        [(z.planes, R, W), (z.lat_rows, W), (z.lat_rows, W), (R, W)],
        [fields, surface, e1, e2, filter_rows, keep_counts],
        [(R, LANES)] * 2,
    )
    m1 = lax.ppermute(m1, "lat", lat_one)
    m2 = lax.ppermute(m2, "lat", lat_two)

    sent = (R, W + 2 * z.extra * LANES)
    ring, ring_surface, msg = call(
        halo_rows, [(7, 2 * L, W), (2 * L, W), sent], [sums, m1, m2]
    )
    got = from_below(msg)
    y, yring = call(
        first_step,
        [(4 * L, R, W), (3, 2 * L, W)],
        [x, ring, geom],
        [(4, 2 * L, W), (2 * L, W)],
        flops=10_000_000,
    )
    m = 4 * L * R
    surface_tile = x[4 * L]
    state, sring, part = call(
        first_spectra,
        [(4 * L, R, W), (3, 2 * L, W), (4 * L * z.slots + 6 * L, 2 * KMAX)],
        [y, yring, surface_tile, ring_surface, got, geom, wave_high, wave_low, phase, filter_rows],
        [(m + 6 * L, 2 * KMAX)],
    )
    part, got = over_lon(part)
    ht, htring, uvmodes, msg = call(
        filter_mass,
        [(2 * L, R, W), (2, 2 * L, W), (2 * L * R + 2 * L, 2 * KMAX), sent],
        [state, sring, part, got, wave_high, wave_low, phase, filter_rows, keep_counts],
    )
    got = from_below(msg)
    (y,) = call(
        second_step,
        [(4 * L, R, W)],
        [state, sring, uvmodes, ht, htring, geom, wave_high, wave_low, filter_rows, keep_counts],
        [(2 * L, R, W), (2 * L, W), (2 * L, W)],
        flops=10_000_000,
    )
    state, part = call(
        second_spectra,
        [(4 * L, R, W), (4 * L * z.slots, 2 * KMAX)],
        [y, surface_tile, ring_surface, got, geom, wave_high, wave_low, phase, filter_rows],
        [(m, 2 * KMAX)],
    )
    part, got = over_lon(part)
    return pl.pallas_call(
        functools.partial(filter_all, z),
        out_shape=jax.ShapeDtypeStruct((4, L, R, z.C), f32),
        in_specs=[vmem] * 6 + [smem] * 2,
        out_specs=pl.BlockSpec(memory_space=pl.ANY),
        scratch_shapes=[
            pltpu.VMEM((4, L, R, z.C), f32),
            pltpu.SemaphoreType.DMA((len(z.chunks),)),
        ],
        compiler_params=pltpu.CompilerParams(vmem_limit_bytes=VMEM_LIMIT),
        name="filter_all",
    )(state, part, got, wave_high, wave_low, phase, filter_rows, keep_counts)


def wave_tables(z):
    lane = np.arange(z.W)
    j = np.where(lane >= z.W - 2, lane - z.W, lane)
    angle = 2.0 * np.pi * ((j[:, None] * np.arange(KMAX)[None, :]) % z.N) / z.N
    table = np.concatenate([np.cos(angle), np.sin(angle)], 1).astype(np.float32)
    high = table.astype(ml_dtypes.bfloat16)
    low = (table - high.astype(np.float32)).astype(ml_dtypes.bfloat16)
    return high, low


def solution(mesh):
    def run(fields, surface, filter_rows, keep_counts):
        z = Sizes(mesh, fields.shape, filter_rows.shape[0])
        high, low = wave_tables(z)

        def body(fields, surface, filter_rows, keep_counts):
            return local(
                z, jnp.asarray(high), jnp.asarray(low), fields, surface, filter_rows, keep_counts
            )

        spec = P(None, "lev", "lat", "lon")
        return jax.shard_map(
            body,
            mesh=mesh,
            in_specs=(spec, P("lat", "lon"), P(), P()),
            out_specs=spec,
            check_vma=False,
        )(fields, surface, filter_rows, keep_counts)

    return run
```

```python
import functools

import jax
import jax.numpy as jnp
import ml_dtypes
import numpy as np
from jax import lax
from jax.experimental import pallas as pl
from jax.experimental.pallas import tpu as pltpu
from jax.sharding import PartitionSpec as P

KMAX = 128
GRAVITY_SCALE = 0.05
BUOYANCY = 0.5
CORIOLIS = 0.3
ZONAL_COEF = 0.08
NORTH_COEF = 0.2
DAMPING = 0.25
FIRST_LAT = -70.0
ROW_STEP = 0.05
LANES = 128
VMEM_LIMIT = 24 * 1024 * 1024


def layer_weight(h, t):
    return GRAVITY_SCALE * (1.0 + h) * (1.0 + BUOYANCY * t)


def east(x):
    return pltpu.roll(x, x.shape[1] - 1, 1)


def west(x):
    return pltpu.roll(x, 1, 1)


def rows_up(x):
    return pltpu.roll(x, x.shape[0] - 1, 0)


def rows_down(x):
    return pltpu.roll(x, 1, 0)


def row_iota(x):
    return lax.broadcasted_iota(jnp.int32, x.shape, 0)


def with_last(x, row):
    return jnp.where(row_iota(x) == x.shape[0] - 1, jnp.broadcast_to(row, x.shape), rows_up(x))


def with_first(x, row):
    return jnp.where(row_iota(x) == 0, jnp.broadcast_to(row, x.shape), rows_down(x))


def wide(geom, k, lo, hi, width):
    return jnp.concatenate([geom[k, lo:hi, :]] * (width // LANES), 1)


class Sizes:
    def __init__(self, mesh, fields_shape, filter_count):
        _, levels, rows, columns = fields_shape
        self.n_lon, self.n_lat, self.n_lev = (mesh.shape[a] for a in ("lon", "lat", "lev"))
        self.L = levels // self.n_lev
        self.R = rows // self.n_lat
        self.C = columns // self.n_lon
        self.N = columns
        self.W = -(-(self.C + 4) // LANES) * LANES
        self.slots = filter_count // self.n_lat
        self.filters = filter_count
        self.planes = 4 * self.L + 1
        self.base = (self.C - 1) // LANES * LANES
        self.tiles = self.W // LANES
        self.extra = -(-self.tiles // self.R)
        self.lat_rows = -(-(7 * self.L + 1) // 8) * 8
        width = -(-self.base // LANES // 3) * LANES if self.base else self.W
        cuts = [c for c in range(0, self.base + 1, width)] if self.base else [0]
        if self.C - cuts[-1] <= LANES and len(cuts) > 1:
            cuts.pop()
        self.chunks = list(zip(cuts, cuts[1:] + [self.C]))
        self.bits = (self.R - self.slots).bit_length()
        assert self.R == 2 * self.slots and self.n_lon <= KMAX
        assert self.R == 2 * self.L and self.n_lon % 2 == 0
        assert 2 <= self.C - self.base <= LANES - 2 and 2 * self.planes <= LANES


def edge_tiles(z, count, head, tail, width):
    lane = lax.broadcasted_iota(jnp.int32, (z.R, LANES), 1)
    left = jnp.zeros((z.R, LANES), jnp.float32)
    right = left
    first = z.C - width - z.base
    for p in range(count):
        here = (lane >= width * p) & (lane < width * (p + 1))
        left = jnp.where(here, moved(head(p), width * p), left)
        right = jnp.where(here, moved(tail(p), width * p - first), right)
    return left, right


def moved(x, shift):
    shift = shift % x.shape[1]
    return pltpu.roll(x, shift, 1) if shift else x


def by_parity(axis, first, second, even, odd):
    is_even = lax.axis_index(axis) % 2 == 0

    @pl.when(is_even)
    def _():
        first[...] = even
        second[...] = odd

    @pl.when(jnp.logical_not(is_even))
    def _():
        first[...] = odd
        second[...] = even


def patch(z, ref, p, count, width, from_right, from_left):
    lane = lax.broadcasted_iota(jnp.int32, (z.R, LANES), 1)
    last = z.C - z.base
    right = moved(from_right, last - width * p)
    left = moved(from_left, LANES - width - width * p)
    for start in sorted({z.base, z.W - LANES}):
        tile = ref[:, start : start + LANES]
        if start == z.base:
            tile = jnp.where((lane >= last) & (lane < last + width), right, tile)
        if start == z.W - LANES:
            tile = jnp.where(lane >= LANES - width, left, tile)
        ref[:, start : start + LANES] = tile


def place_tiles(z, fields, surface, x, m1, m2, e1, e2):
    lane = lax.broadcasted_iota(jnp.int32, (z.R, LANES), 1)
    for p in range(z.planes):
        f, l = divmod(p, z.L)
        x[p, :, 0 : z.C] = fields[f, l] if p < 4 * z.L else surface[...]
        x[p, :, z.base : z.base + LANES] = jnp.where(
            lane < z.C - z.base, x[p, :, z.base : z.base + LANES], 0.0
        )
        if z.base + LANES < z.W:
            x[p, :, z.base + LANES :] = jnp.zeros((z.R, z.W - z.base - LANES), jnp.float32)
    lat_even = lax.axis_index("lat") % 2 == 0
    near1 = jnp.where(lat_even, z.R - 1, 0)
    far1 = jnp.where(lat_even, z.R - 2, 1)
    for msg, near, far in ((m1, near1, far1), (m2, z.R - 1 - near1, z.R - 1 - far1)):
        for p in range(4 * z.L):
            msg[p : p + 1, :] = x[p, pl.ds(near, 1), :]
        for p in range(z.L, 4 * z.L):
            to = 3 * z.L + p
            msg[to : to + 1, :] = x[p, pl.ds(far, 1), :]
        to = 7 * z.L
        msg[to : to + 1, :] = x[4 * z.L, pl.ds(near, 1), :]
        if z.lat_rows > to + 1:
            msg[to + 1 :, :] = jnp.zeros((z.lat_rows - to - 1, z.W), jnp.float32)
    left, right = edge_tiles(
        z,
        z.planes,
        lambda p: x[p, :, 0:LANES],
        lambda p: x[p, :, z.base : z.base + LANES],
        2,
    )
    by_parity("lon", e1, e2, right, left)


def widen(z, x_in, r1, r2, x, sums, from_right, from_left):
    del x_in
    by_parity("lon", from_right, from_left, r1[...], r2[...])
    right, left = from_right[...], from_left[...]
    for p in range(z.planes):
        patch(z, x.at[p], p, z.planes, 2, right, left)
    total = layer_weight(x[2 * z.L], x[3 * z.L])
    for l in range(1, z.L):
        total = total + layer_weight(x[2 * z.L + l], x[3 * z.L + l])
    sums[...] = total


def put_column_sums(z, msg, total, south, north):
    if total is not None:
        msg[:, 0 : z.W] = total
    for d, row in enumerate((south, north)):
        for t in range(z.tiles):
            at = z.W + (d * z.extra + t // z.R) * LANES
            msg[t % z.R : t % z.R + 1, at : at + LANES] = row[:, t * LANES : (t + 1) * LANES]


def ring_sum(z, w):
    south = w[0:1]
    north = w[z.L : z.L + 1]
    for l in range(1, z.L):
        south = south + w[l : l + 1]
        north = north + w[z.L + l : z.L + l + 1]
    return south, north


def halo_rows(z, sums, r1, r2, ring, ring_surface, msg, c1, c2):
    lat_even = lax.axis_index("lat") % 2 == 0

    def place(d, source):
        for k in range(7):
            ring[k, d * z.L : (d + 1) * z.L, :] = source[k * z.L : (k + 1) * z.L, :]
        ring_surface[d * z.L : (d + 1) * z.L, :] = jnp.broadcast_to(
            source[7 * z.L : 7 * z.L + 1, :], (z.L, z.W)
        )

    @pl.when(lat_even)
    def _():
        place(0, r2)
        place(1, r1)

    @pl.when(jnp.logical_not(lat_even))
    def _():
        place(0, r1)
        place(1, r2)

    def row(k, lo):
        return ring[k, :, lo : lo + LANES] if k < 4 else ring_surface[:, lo : lo + LANES]

    left, right = edge_tiles(z, 5, lambda k: row(k, 0), lambda k: row(k, z.base), 1)
    by_parity("lon", c1, c2, right, left)
    south, north = ring_sum(z, layer_weight(ring[2], ring[3]))
    put_column_sums(z, msg, sums[...], south, north)


def in_band(z, shape):
    lat = lax.axis_index("lat")
    row = lax.broadcasted_iota(jnp.int32, shape, 0)
    south = jnp.where(lat > 0, 1.0, 0.0)
    north = jnp.where(lat < z.n_lat - 1, 1.0, 0.0)
    return jnp.where(row < z.L, south, north)


def ring_geopot(z, h, t):
    w = layer_weight(h, t)
    row = row_iota(w)
    level = jnp.where(row < z.L, row, row - z.L)
    q = 0.5 * w
    for s in range(1, z.L):
        q = q + jnp.where(level < z.L - s, pltpu.roll(w, 2 * z.L - s, 0), 0.0)
    return q * in_band(z, w.shape)


def tendencies(coef, u, v, h, t, un, vs, hn, hs, tn, ts, q, qn, which="uvht"):
    zonal, cor, corn, north, south = coef
    out = {}
    if "u" in which:
        a = v + vs
        out["u"] = u + cor * (a + east(a)) - zonal * (east(q) - q)
    if "v" in which:
        b = u + un
        out["v"] = v - corn * (b + west(b)) - NORTH_COEF * (qn - q)
    if "h" in which:
        flux = u * (2.0 + h + east(h)) * 0.5
        out["h"] = (
            h
            - zonal * (flux - west(flux))
            - (north * (v * (2.0 + h + hn) * 0.5) - south * (vs * (2.0 + hs + h) * 0.5))
        )
    if "t" in which:
        out["t"] = (
            t
            - 0.25 * (u + west(u)) * zonal * (east(t) - west(t))
            - (0.25 * NORTH_COEF) * (v + vs) * (tn - ts)
        )
    return out


def advance_tile(z, geom, get, un_row, vs_row, h_ring, t_ring, q_ring, put, qput=None):
    coef = [wide(geom, k, 0, z.R, z.W) for k in range(5)]
    below = None
    for l in reversed(range(z.L)):
        u, v, h, t = (get(f, l) for f in range(4))
        w = layer_weight(h, t)
        q = 0.5 * w if below is None else below + 0.5 * w
        below = w if below is None else below + w
        s, n = l, z.L + l
        new = tendencies(
            coef, u, v, h, t,
            with_last(u, un_row(l)), with_first(v, vs_row(l)),
            with_last(h, h_ring[n : n + 1, :]), with_first(h, h_ring[s : s + 1, :]),
            with_last(t, t_ring[n : n + 1, :]), with_first(t, t_ring[s : s + 1, :]),
            q, with_last(q, q_ring[n : n + 1, :]),
        )
        for f, name in enumerate("uvht"):
            put(f, l, new[name])
        if qput is not None:
            qput(l, q)


def first_step(
    z, x, ring_in, surface_in, r1, r2, geom, y, yring, ring_surface, ring, inner, q_ring, from_right, from_left
):
    L = z.L
    by_parity("lon", from_right, from_left, r1[...], r2[...])
    right, left = from_right[...], from_left[...]
    ring[...] = ring_in[...]
    ring_surface[...] = surface_in[...]
    for k in range(5):
        patch(z, ring.at[k] if k < 4 else ring_surface, k, 5, 1, right, left)
    q_ring[...] = ring_geopot(z, ring[2], ring[3])

    def get(f, l):
        return x[f * L + l]

    def put(f, l, value):
        y[f * L + l] = value

    def qput(l, q):
        inner[3, l : l + 1, :] = q[0:1]

    inner[3, L:, :] = jnp.zeros((L, z.W), jnp.float32)
    advance_tile(
        z, geom, get,
        lambda l: ring[0, L + l : L + l + 1, :], lambda l: ring[1, l : l + 1, :],
        ring.at[2], ring.at[3], q_ring, put, qput,
    )
    for l in range(L):
        inner[0, l : l + 1, :] = x[l, 0:1, :]
        inner[0, L + l : L + l + 1, :] = x[L + l, z.R - 1 : z.R, :]
        for k, f in ((1, 2), (2, 3)):
            inner[k, l : l + 1, :] = x[f * L + l, 0:1, :]
            inner[k, L + l : L + l + 1, :] = x[f * L + l, z.R - 1 : z.R, :]
    south = lax.broadcasted_iota(jnp.int32, (2 * L, z.W), 0) < L
    coef = [wide(geom, k, z.R, z.R + 2 * L, z.W) for k in range(5)]
    u, v, h, t = (ring[k] for k in range(4))
    new = tendencies(
        coef, u, v, h, t,
        inner[0], jnp.where(south, ring[4], inner[0]),
        jnp.where(south, inner[1], ring[5]), jnp.where(south, ring[5], inner[1]),
        jnp.where(south, inner[2], ring[6]), jnp.where(south, ring[6], inner[2]),
        q_ring[...], inner[3],
    )
    mask = in_band(z, (2 * L, z.W))
    yring[0] = jnp.where(south, new["v"], new["u"]) * mask
    yring[1] = new["h"] * mask
    yring[2] = new["t"] * mask


def level_part(z, surface, ring_surface, got):
    live = jnp.where(lax.axis_index("lev") < z.n_lev - 1, 1.0, 0.0)
    lat = lax.axis_index("lat")
    tile = surface + live * got[:, 0 : z.W]
    rows, beneath = [], []
    for d in range(2):
        there = jnp.where(lat > 0, 1.0, 0.0) if d == 0 else jnp.where(lat < z.n_lat - 1, 1.0, 0.0)
        parts = []
        for t in range(z.tiles):
            at = z.W + (d * z.extra + t // z.R) * LANES
            parts.append(got[t % z.R : t % z.R + 1, at : at + LANES])
        sums = jnp.concatenate(parts, 1)
        sums = jnp.where(lax.broadcasted_iota(jnp.int32, sums.shape, 1) < z.C, sums, 0.0)
        beneath.append(there * live * sums)
        rows.append(there * ring_surface[d * z.L : d * z.L + 1, :] + beneath[d])
    return tile, rows[0], rows[1], beneath[1]


def split(x):
    high = x.astype(jnp.bfloat16)
    return high, (x - high.astype(jnp.float32)).astype(jnp.bfloat16)


def dot(a, b, dims):
    return lax.dot_general(a, b, (dims, ((), ())), preferred_element_type=jnp.float32)


def product(x, wh, wl, dims):
    high, low = split(x)
    return dot(high, wh[...], dims) + dot(low, wh[...], dims) + dot(high, wl[...], dims)


def masked(z, x):
    tail = x[:, z.base :]
    lane = lax.broadcasted_iota(jnp.int32, tail.shape, 1)
    tail = jnp.where(lane < z.C - z.base, tail, 0.0)
    return jnp.concatenate([x[:, : z.base], tail], 1) if z.base else tail


def spectra(z, x, wh, wl, phase):
    s = product(x, wh, wl, ((1,), (0,)))
    a, b = s[:, :KMAX], s[:, KMAX:]
    c, d = phase[0:1, :], phase[1:2, :]
    return jnp.concatenate([a * c - b * d, a * d + b * c], 1)


def twice(x):
    return jnp.concatenate([x, x], 1)


def code_bit(code, k):
    return twice((code >> k) & 1) == 1


def compress(z, tile, code):
    for b in range(z.bits):
        tile = jnp.where(code_bit(code, b), pltpu.roll(tile, z.R - (1 << b), 0), tile)
    return tile


def expand(z, tile, code):
    for b in reversed(range(z.bits)):
        tile = jnp.where(code_bit(code, z.bits + b), pltpu.roll(tile, 1 << b, 0), tile)
    return tile


def pick_spectra(z, full, code, out):
    code = code[0 : z.R, :]
    row = lax.broadcasted_iota(jnp.int32, (z.R, 2 * KMAX), 0)
    for i in range(2 * z.L):
        a = compress(z, full[2 * i * z.R : (2 * i + 1) * z.R], code)
        b = compress(z, full[(2 * i + 1) * z.R : (2 * i + 2) * z.R], code)
        out[i * z.R : (i + 1) * z.R, :] = jnp.where(row < z.slots, a, pltpu.roll(b, z.slots, 0))


def first_spectra(z, y, yring, surface, ring_surface, got, geom, wh, wl, phase, code, state, sring, out):
    L = z.L
    g, gs, gn, beneath = level_part(z, surface[...], ring_surface, got)
    du = wide(geom, 0, 0, z.R, z.W) * (east(g) - g)
    dv = NORTH_COEF * (with_last(g, gn) - g)
    for l in range(L):
        state[l] = y[l] - du
        state[L + l] = y[L + l] - dv
    for p in range(2 * L, 4 * L):
        state[p] = y[p]
    shape = (2 * L, z.W)
    south = lax.broadcasted_iota(jnp.int32, shape, 0) < L
    zonal = wide(geom, 0, z.R, z.R + 2 * L, z.W)
    gn = jnp.broadcast_to(gn, shape)
    du_north = zonal * (east(gn) - gn)
    dv_south = NORTH_COEF * jnp.broadcast_to(g[0:1] - gs, shape)
    uv = yring[0] - jnp.where(south, dv_south, du_north) * in_band(z, shape)
    sring[0] = uv
    sring[1] = yring[1]
    sring[2] = yring[2]
    lane = lax.broadcasted_iota(jnp.int32, shape, 1)
    corner = jnp.broadcast_to(beneath[:, 0:1], shape)
    given = jnp.where((lane == z.W - 1) & jnp.logical_not(south), -zonal * corner, masked(z, uv))
    m = 4 * L * z.R
    everything = jnp.concatenate(
        [
            masked(z, state[...].reshape(m, z.W)),
            given,
            masked(z, sring[1]),
            masked(z, sring[2]),
        ],
        0,
    )
    full = spectra(z, everything, wh, wl, phase)
    pick_spectra(z, full, code, out)
    at = 4 * L * z.slots
    out[at : at + 6 * L, :] = full[m:, :]
    wide_shape = (2 * L, 2 * KMAX)
    lane = lax.broadcasted_iota(jnp.int32, wide_shape, 1)
    lon = lax.axis_index("lon")
    ends = jnp.where(south[:, 0:1], uv[:, 0:1], uv[:, z.C - 1 : z.C])
    out[at + 6 * L :, :] = jnp.where(
        lane == lon,
        jnp.broadcast_to(ends, wide_shape),
        jnp.where(lane == KMAX + lon, jnp.broadcast_to(beneath[:, 0:1], wide_shape), 0.0),
    )


def second_spectra(z, y, surface, ring_surface, got, geom, wh, wl, phase, code, state, out):
    L = z.L
    g, _, gn, _ = level_part(z, surface[...], ring_surface, got)
    du = wide(geom, 0, 0, z.R, z.W) * (east(g) - g)
    dv = NORTH_COEF * (with_last(g, gn) - g)
    for l in range(L):
        state[l] = y[l] - du
        state[L + l] = y[L + l] - dv
    for p in range(2 * L, 4 * L):
        state[p] = y[p]
    full = spectra(z, masked(z, state[...].reshape(4 * L * z.R, z.W)), wh, wl, phase)
    pick_spectra(z, full, code, out)


def mode_weight(z, keep):
    keep = twice(keep)
    k = lax.broadcasted_iota(jnp.int32, keep.shape, 1)
    k = jnp.where(k < KMAX, k, k - KMAX)
    scale = jnp.where(k == 0, 1.0 / z.N, 2.0 / z.N)
    return jnp.where(k < keep, scale, 0.0)


def keeps(z, code):
    keep = code[...] >> (2 * z.bits)
    return keep[0 : z.R], keep[z.R :]


def damping(z, keep, width):
    value = jnp.where(keep > 0, 1.0 - DAMPING, 0.0)
    return jnp.concatenate([value] * (width // LANES), 1)


def local_modes(total, phase):
    a, b = total[:, :KMAX], total[:, KMAX:]
    c, d = phase[0:1, :], phase[1:2, :]
    return jnp.concatenate([a * c + b * d, b * c - a * d], 1)


def tile_modes(z, modes, code, weight):
    code = code[0 : z.R, :]
    out = []
    for i in range(2 * z.L):
        pair = modes[i * z.R : (i + 1) * z.R]
        out.append(expand(z, pair, code) * weight)
        out.append(expand(z, pltpu.roll(pair, z.R - z.slots, 0), code) * weight)
    return out


def smooth(modes, wh, wl):
    return product(modes, wh, wl, ((1,), (1,)))


def filter_mass(z, state, sring, part, got, wh, wl, phase, code, ht, htring, uvmodes, msg):
    L, m = z.L, 4 * z.L * z.slots
    total = part[...] + got[...]
    modes = local_modes(total, phase)
    keep, rkeep = keeps(z, code)
    weight, rweight = mode_weight(z, keep), mode_weight(z, rkeep)
    ring = [modes[m + k * 2 * L : m + (k + 1) * 2 * L] * rweight for k in range(3)]
    tiles = tile_modes(z, modes, code, weight)
    uvmodes[...] = jnp.concatenate(tiles[: 2 * L] + [ring[0], total[m + 6 * L :]], 0)
    s = smooth(jnp.concatenate(tiles[2 * L :] + ring[1:], 0), wh, wl)
    damp, rdamp = damping(z, keep, z.W), damping(z, rkeep, z.W)
    for p in range(2 * L):
        x = state[2 * L + p]
        ht[p] = x + damp * (s[p * z.R : (p + 1) * z.R] - x)
    for k in range(2):
        x = sring[1 + k]
        at = 2 * L * z.R + k * 2 * L
        htring[k] = x + rdamp * (s[at : at + 2 * L] - x)
    total = layer_weight(ht[0], ht[L])
    for l in range(1, L):
        total = total + layer_weight(ht[l], ht[L + l])
    south, north = ring_sum(z, layer_weight(htring[0], htring[1]))
    put_column_sums(z, msg, total, south, north)


def ring_corners(z, uv, gathered, geom):
    shape = uv.shape
    lon = lax.axis_index("lon")
    right = jnp.where(lon == z.n_lon - 1, 0, lon + 1)
    left = jnp.where(lon == 0, z.n_lon - 1, lon - 1)
    place = lax.broadcasted_iota(jnp.int32, gathered.shape, 1)

    def of(lane):
        value = jnp.sum(jnp.where(place == lane, gathered, 0.0), 1, keepdims=True)
        return jnp.broadcast_to(value, shape)

    south = lax.broadcasted_iota(jnp.int32, shape, 0) < z.L
    north = jnp.logical_not(south)
    lane = lax.broadcasted_iota(jnp.int32, shape, 1)
    zonal = wide(geom, 0, z.R, z.R + 2 * z.L, z.W)
    uv = jnp.where((lane == z.C) & south, of(right), uv)
    uv = jnp.where((lane == z.W - 1) & north, of(left) - zonal * of(KMAX + lon), uv)
    corner = of(KMAX + right)
    uv = jnp.where((lane == z.C - 1) & north, uv - zonal * corner, uv)
    row = lax.broadcasted_iota(jnp.int32, shape, 0)
    above = jnp.where((lane == z.C) & (row == z.R - 1), NORTH_COEF * corner, 0.0)
    return uv, above


def second_step(z, state, sring, uvmodes, ht, htring, geom, wh, wl, code, y, uv, uvring, q_ring):
    L = z.L
    m = 2 * L * z.R
    s = smooth(uvmodes[0 : m + 2 * L, :], wh, wl)
    keep, rkeep = keeps(z, code)
    damp, rdamp = damping(z, keep, z.W), damping(z, rkeep, z.W)
    x, above = ring_corners(z, sring[0], uvmodes[m + 2 * L :, :], geom)
    for p in range(2 * L):
        old = state[p] if p < L else state[p] - above
        uv[p] = old + damp * (s[p * z.R : (p + 1) * z.R] - old)
    uvring[...] = x + rdamp * (s[m:] - x)
    q_ring[...] = ring_geopot(z, htring[0], htring[1])

    def get(f, l):
        return uv[f * L + l] if f < 2 else ht[(f - 2) * L + l]

    def put(f, l, value):
        y[f * L + l] = value

    advance_tile(
        z, geom, get,
        lambda l: uvring[L + l : L + l + 1, :], lambda l: uvring[l : l + 1, :],
        htring.at[0], htring.at[1], q_ring, put,
    )


def filter_all(z, state, part, got, wh, wl, phase, code, out, held, sem):
    L = z.L
    modes = local_modes(part[...] + got[...], phase)
    keep, _ = keeps(z, code)
    high, low = split(jnp.concatenate(tile_modes(z, modes, code, mode_weight(z, keep)), 0))
    across = ((1,), (1,))
    copies = []
    for i, (lo, hi) in enumerate(z.chunks):
        top = min(-(-hi // LANES) * LANES, z.W)
        w, v = wh[lo:top, :], wl[lo:top, :]
        s = dot(high, w, across) + dot(low, w, across) + dot(high, v, across)
        d = damping(z, keep, top - lo)
        for p in range(4 * L):
            x = state[p, :, lo:top]
            new = x + d * (s[p * z.R : (p + 1) * z.R] - x)
            held[p // L, p % L, :, lo:hi] = new[:, : hi - lo]
        copies.append(
            pltpu.make_async_copy(held.at[:, :, :, lo:hi], out.at[:, :, :, lo:hi], sem.at[i])
        )
        copies[-1].start()
    for copy in copies:
        copy.wait()


def local(z, wave_high, wave_low, fields, surface, filter_rows, keep_counts):
    L, R, W = z.L, z.R, z.W
    f32 = jnp.float32
    vmem = pl.BlockSpec(memory_space=pltpu.VMEM)

    def call(kernel, outs, ins, scratch=(), flops=1_000_000, aliases={}):
        size = sum(int(np.prod(s)) for s in outs) * 4 + sum(i.size * i.dtype.itemsize for i in ins)
        return pl.pallas_call(
            functools.partial(kernel, z),
            out_shape=[jax.ShapeDtypeStruct(s, f32) for s in outs],
            in_specs=[vmem] * len(ins),
            out_specs=[vmem] * len(outs),
            scratch_shapes=[pltpu.VMEM(s, f32) for s in scratch],
            input_output_aliases=aliases,
            compiler_params=pltpu.CompilerParams(vmem_limit_bytes=VMEM_LIMIT),
            cost_estimate=pl.CostEstimate(flops=flops, bytes_accessed=size, transcendentals=0),
            name=kernel.__name__,
        )(*ins)

    lat, lon = lax.axis_index("lat"), lax.axis_index("lon")
    index = lax.broadcasted_iota(jnp.int32, (R + 2 * L, LANES), 0)
    index = jnp.where(index < R, index, jnp.where(index < R + L, -1, R))
    based = (lat * R + index).astype(f32)
    to_radian = jnp.pi / 180.0
    middle = (FIRST_LAT + (based + 0.5) * ROW_STEP) * to_radian
    northern = (FIRST_LAT + (based + 1.0) * ROW_STEP) * to_radian
    southern = (FIRST_LAT + based * ROW_STEP) * to_radian
    cos_mid = jnp.cos(middle)
    geom = jnp.stack(
        [
            ZONAL_COEF / cos_mid,
            (0.25 * CORIOLIS) * jnp.sin(middle),
            (0.25 * CORIOLIS) * jnp.sin(northern),
            NORTH_COEF * jnp.cos(northern) / cos_mid,
            NORTH_COEF * jnp.cos(southern) / cos_mid,
        ]
    )
    turn = (lon * z.C * jnp.arange(KMAX, dtype=jnp.int32)) % z.N
    angle = turn.astype(f32) * (2.0 * jnp.pi / z.N)
    phase = jnp.stack([jnp.cos(angle), jnp.sin(angle)])

    code = row_code(z, lat, filter_rows, keep_counts)

    lon_one = [(i, i ^ 1) for i in range(z.n_lon)]
    lon_two = [(i, (((i + 1) % z.n_lon ^ 1) - 1) % z.n_lon) for i in range(z.n_lon)]
    lat_one = [(i, i ^ 1) for i in range(z.n_lat) if i ^ 1 < z.n_lat]
    lat_two = [(i, ((i + 1) ^ 1) - 1) for i in range(1, z.n_lat) if ((i + 1) ^ 1) - 1 < z.n_lat]

    def from_below(column):
        if z.n_lev == 2:
            return lax.ppermute(column, "lev", [(0, 1), (1, 0)])
        place = lax.axis_index("lev")
        total = jnp.zeros_like(column)
        for s in range(1, z.n_lev):
            got = lax.ppermute(column, "lev", [(i, i - s) for i in range(s, z.n_lev)])
            total = total + jnp.where(place + s < z.n_lev, got, 0.0)
        return total

    def over_lon(part):
        got, step = None, 1
        while step < z.n_lon:
            if got is not None:
                part = part + got
            got = lax.ppermute(part, "lon", [(i, i ^ step) for i in range(z.n_lon)])
            step *= 2
        return part, got

    tile = (R, LANES)
    x, m1, m2, e1, e2 = call(
        place_tiles,
        [(z.planes, R, W), (z.lat_rows, W), (z.lat_rows, W), tile, tile],
        [fields, surface],
    )
    m1 = lax.ppermute(m1, "lat", lat_one)
    m2 = lax.ppermute(m2, "lat", lat_two)
    e1 = lax.ppermute(e1, "lon", lon_one)
    e2 = lax.ppermute(e2, "lon", lon_two)
    x, sums = call(
        widen, [(z.planes, R, W), (R, W)], [x, e1, e2], [tile] * 2, aliases={0: 0}
    )

    sent = (R, W + 2 * z.extra * LANES)
    ring, ring_surface, msg, c1, c2 = call(
        halo_rows, [(7, 2 * L, W), (2 * L, W), sent, tile, tile], [sums, m1, m2]
    )
    c1 = lax.ppermute(c1, "lon", lon_one)
    c2 = lax.ppermute(c2, "lon", lon_two)
    got = from_below(msg)
    y, yring, ring_surface = call(
        first_step,
        [(4 * L, R, W), (3, 2 * L, W), (2 * L, W)],
        [x, ring, ring_surface, c1, c2, geom],
        [(7, 2 * L, W), (4, 2 * L, W), (2 * L, W), tile, tile],
        flops=10_000_000,
    )
    surface_tile = x[4 * L]
    state, sring, part = call(
        first_spectra,
        [(4 * L, R, W), (3, 2 * L, W), (4 * L * z.slots + 8 * L, 2 * KMAX)],
        [y, yring, surface_tile, ring_surface, got, geom, wave_high, wave_low, phase, code],
    )
    part, got = over_lon(part)
    ht, htring, uvmodes, msg = call(
        filter_mass,
        [(2 * L, R, W), (2, 2 * L, W), (2 * L * R + 4 * L, 2 * KMAX), sent],
        [state, sring, part, got, wave_high, wave_low, phase, code],
    )
    got = from_below(msg)
    (y,) = call(
        second_step,
        [(4 * L, R, W)],
        [state, sring, uvmodes, ht, htring, geom, wave_high, wave_low, code],
        [(2 * L, R, W), (2 * L, W), (2 * L, W)],
        flops=10_000_000,
    )
    state, part = call(
        second_spectra,
        [(4 * L, R, W), (4 * L * z.slots, 2 * KMAX)],
        [y, surface_tile, ring_surface, got, geom, wave_high, wave_low, phase, code],
    )
    part, got = over_lon(part)
    return pl.pallas_call(
        functools.partial(filter_all, z),
        out_shape=jax.ShapeDtypeStruct((4, L, R, z.C), f32),
        in_specs=[vmem] * 7,
        out_specs=pl.BlockSpec(memory_space=pl.ANY),
        scratch_shapes=[
            pltpu.VMEM((4, L, R, z.C), f32),
            pltpu.SemaphoreType.DMA((len(z.chunks),)),
        ],
        compiler_params=pltpu.CompilerParams(vmem_limit_bytes=VMEM_LIMIT),
        name="filter_all",
    )(state, part, got, wave_high, wave_low, phase, code)


def row_code(z, lat, filter_rows, keep_counts):
    row = lax.broadcasted_iota(jnp.int32, (z.R + 2 * z.L, LANES), 0)
    own = lax.dynamic_slice_in_dim(filter_rows, lat * z.slots, z.slots) - lat * z.R
    kept = lax.dynamic_slice_in_dim(keep_counts, lat * z.slots, z.slots)
    code = jnp.zeros(row.shape, jnp.int32)
    for s in range(z.slots):
        at = own[s]
        code = code + jnp.where(row == at, kept[s] << (2 * z.bits), 0)
        for b in range(z.bits):
            bit = ((own[s] - s) >> b) & 1
            to = at - (bit << b)
            code = code + jnp.where((row == to) & (bit == 1), 1 << b, 0)
            code = code + jnp.where((row == at) & (bit == 1), 1 << (z.bits + b), 0)
            at = to
    before = jnp.maximum(lat * z.slots - 1, 0)
    after = jnp.minimum((lat + 1) * z.slots, z.filters - 1)
    south = jnp.where((lat > 0) & (filter_rows[before] == lat * z.R - 1), keep_counts[before], 0)
    north = jnp.where(
        (lat < z.n_lat - 1) & (filter_rows[after] == (lat + 1) * z.R), keep_counts[after], 0
    )
    ring = jnp.where(row < z.R + z.L, south, north) << (2 * z.bits)
    return jnp.where(row < z.R, code, ring)


def wave_tables(z):
    lane = np.arange(z.W)
    j = np.where(lane >= z.W - 2, lane - z.W, lane)
    angle = 2.0 * np.pi * ((j[:, None] * np.arange(KMAX)[None, :]) % z.N) / z.N
    table = np.concatenate([np.cos(angle), np.sin(angle)], 1).astype(np.float32)
    high = table.astype(ml_dtypes.bfloat16)
    low = (table - high.astype(np.float32)).astype(ml_dtypes.bfloat16)
    return high, low


def solution(mesh):
    def run(fields, surface, filter_rows, keep_counts):
        z = Sizes(mesh, fields.shape, filter_rows.shape[0])
        high, low = wave_tables(z)

        def body(fields, surface, filter_rows, keep_counts):
            return local(
                z, jnp.asarray(high), jnp.asarray(low), fields, surface, filter_rows, keep_counts
            )

        spec = P(None, "lev", "lat", "lon")
        return jax.shard_map(
            body,
            mesh=mesh,
            in_specs=(spec, P("lat", "lon"), P(), P()),
            out_specs=spec,
            check_vma=False,
        )(fields, surface, filter_rows, keep_counts)

    return run
```

```python
import functools

import jax
import jax.numpy as jnp
import ml_dtypes
import numpy as np
from jax import lax
from jax.experimental import pallas as pl
from jax.experimental.pallas import tpu as pltpu
from jax.sharding import PartitionSpec as P

KMAX = 128
GRAVITY_SCALE = 0.05
BUOYANCY = 0.5
CORIOLIS = 0.3
ZONAL_COEF = 0.08
NORTH_COEF = 0.2
DAMPING = 0.25
FIRST_LAT = -70.0
ROW_STEP = 0.05
LANES = 128
VMEM_LIMIT = 24 * 1024 * 1024


def layer_weight(h, t):
    return GRAVITY_SCALE * (1.0 + h) * (1.0 + BUOYANCY * t)


def east(x):
    return pltpu.roll(x, x.shape[1] - 1, 1)


def west(x):
    return pltpu.roll(x, 1, 1)


def rows_up(x):
    return pltpu.roll(x, x.shape[0] - 1, 0)


def rows_down(x):
    return pltpu.roll(x, 1, 0)


def row_iota(x):
    return lax.broadcasted_iota(jnp.int32, x.shape, 0)


def with_last(x, row):
    return jnp.where(row_iota(x) == x.shape[0] - 1, jnp.broadcast_to(row, x.shape), rows_up(x))


def with_first(x, row):
    return jnp.where(row_iota(x) == 0, jnp.broadcast_to(row, x.shape), rows_down(x))


def wide(geom, k, lo, hi, width):
    return jnp.concatenate([geom[k, lo:hi, :]] * (width // LANES), 1)


class Sizes:
    def __init__(self, mesh, fields_shape, filter_count):
        _, levels, rows, columns = fields_shape
        self.n_lon, self.n_lat, self.n_lev = (mesh.shape[a] for a in ("lon", "lat", "lev"))
        self.L = levels // self.n_lev
        self.R = rows // self.n_lat
        self.C = columns // self.n_lon
        self.N = columns
        self.W = -(-(self.C + 4) // LANES) * LANES
        self.slots = filter_count // self.n_lat
        self.filters = filter_count
        self.planes = 4 * self.L + 1
        self.base = (self.C - 1) // LANES * LANES
        self.tiles = self.W // LANES
        self.extra = -(-self.tiles // self.R)
        self.lat_rows = -(-(7 * self.L + 1) // 8) * 8
        width = -(-self.base // LANES // 3) * LANES if self.base else self.W
        cuts = [c for c in range(0, self.base + 1, width)] if self.base else [0]
        if self.C - cuts[-1] <= LANES and len(cuts) > 1:
            cuts.pop()
        self.chunks = list(zip(cuts, cuts[1:] + [self.C]))
        self.bits = (self.R - self.slots).bit_length()
        assert self.R == 2 * self.slots and self.n_lon <= KMAX
        assert self.R == 2 * self.L and self.n_lon % 2 == 0
        assert 2 <= self.C - self.base <= LANES - 2 and 2 * self.planes <= LANES


def edge_tiles(z, count, head, tail, width):
    lane = lax.broadcasted_iota(jnp.int32, (z.R, LANES), 1)
    left = jnp.zeros((z.R, LANES), jnp.float32)
    right = left
    first = z.C - width - z.base
    for p in range(count):
        here = (lane >= width * p) & (lane < width * (p + 1))
        left = jnp.where(here, moved(head(p), width * p), left)
        right = jnp.where(here, moved(tail(p), width * p - first), right)
    return left, right


def moved(x, shift):
    shift = shift % x.shape[1]
    return pltpu.roll(x, shift, 1) if shift else x


def by_parity(axis, first, second, even, odd):
    is_even = lax.axis_index(axis) % 2 == 0

    @pl.when(is_even)
    def _():
        first[...] = even
        second[...] = odd

    @pl.when(jnp.logical_not(is_even))
    def _():
        first[...] = odd
        second[...] = even


def patch(z, ref, p, count, width, from_right, from_left):
    lane = lax.broadcasted_iota(jnp.int32, (z.R, LANES), 1)
    last = z.C - z.base
    right = moved(from_right, last - width * p)
    left = moved(from_left, LANES - width - width * p)
    for start in sorted({z.base, z.W - LANES}):
        tile = ref[:, start : start + LANES]
        if start == z.base:
            tile = jnp.where((lane >= last) & (lane < last + width), right, tile)
        if start == z.W - LANES:
            tile = jnp.where(lane >= LANES - width, left, tile)
        ref[:, start : start + LANES] = tile


def place_tiles(z, fields, surface, x, m1, m2, e1, e2, held, held_surface, sem):
    lane = lax.broadcasted_iota(jnp.int32, (z.R, LANES), 1)
    copies = [pltpu.make_async_copy(fields.at[f], held.at[f], sem.at[f]) for f in range(4)]
    copies.append(pltpu.make_async_copy(surface, held_surface, sem.at[4]))
    for copy in copies:
        copy.start()
    for p in range(z.planes):
        if p % z.L == 0:
            copies[p // z.L].wait()
        x[p, :, 0 : z.C] = held[p // z.L, p % z.L] if p < 4 * z.L else held_surface[...]
        x[p, :, z.base : z.base + LANES] = jnp.where(
            lane < z.C - z.base, x[p, :, z.base : z.base + LANES], 0.0
        )
        if z.base + LANES < z.W:
            x[p, :, z.base + LANES :] = jnp.zeros((z.R, z.W - z.base - LANES), jnp.float32)
    lat_even = lax.axis_index("lat") % 2 == 0
    near1 = jnp.where(lat_even, z.R - 1, 0)
    far1 = jnp.where(lat_even, z.R - 2, 1)
    for msg, near, far in ((m1, near1, far1), (m2, z.R - 1 - near1, z.R - 1 - far1)):
        for p in range(4 * z.L):
            msg[p : p + 1, :] = x[p, pl.ds(near, 1), :]
        for p in range(z.L, 4 * z.L):
            to = 3 * z.L + p
            msg[to : to + 1, :] = x[p, pl.ds(far, 1), :]
        to = 7 * z.L
        msg[to : to + 1, :] = x[4 * z.L, pl.ds(near, 1), :]
        if z.lat_rows > to + 1:
            msg[to + 1 :, :] = jnp.zeros((z.lat_rows - to - 1, z.W), jnp.float32)
    left, right = edge_tiles(
        z,
        z.planes,
        lambda p: x[p, :, 0:LANES],
        lambda p: x[p, :, z.base : z.base + LANES],
        2,
    )
    by_parity("lon", e1, e2, right, left)


def widen(z, x_in, r1, r2, x, sums, from_right, from_left):
    del x_in
    by_parity("lon", from_right, from_left, r1[...], r2[...])
    right, left = from_right[...], from_left[...]
    for p in range(z.planes):
        patch(z, x.at[p], p, z.planes, 2, right, left)
    total = layer_weight(x[2 * z.L], x[3 * z.L])
    for l in range(1, z.L):
        total = total + layer_weight(x[2 * z.L + l], x[3 * z.L + l])
    sums[...] = total


def put_column_sums(z, msg, total, south, north):
    if total is not None:
        msg[:, 0 : z.W] = total
    for d, row in enumerate((south, north)):
        for t in range(z.tiles):
            at = z.W + (d * z.extra + t // z.R) * LANES
            msg[t % z.R : t % z.R + 1, at : at + LANES] = row[:, t * LANES : (t + 1) * LANES]


def ring_sum(z, w):
    south = w[0:1]
    north = w[z.L : z.L + 1]
    for l in range(1, z.L):
        south = south + w[l : l + 1]
        north = north + w[z.L + l : z.L + l + 1]
    return south, north


def halo_rows(z, sums, r1, r2, ring, ring_surface, msg, c1, c2):
    lat_even = lax.axis_index("lat") % 2 == 0

    def place(d, source):
        for k in range(7):
            ring[k, d * z.L : (d + 1) * z.L, :] = source[k * z.L : (k + 1) * z.L, :]
        ring_surface[d * z.L : (d + 1) * z.L, :] = jnp.broadcast_to(
            source[7 * z.L : 7 * z.L + 1, :], (z.L, z.W)
        )

    @pl.when(lat_even)
    def _():
        place(0, r2)
        place(1, r1)

    @pl.when(jnp.logical_not(lat_even))
    def _():
        place(0, r1)
        place(1, r2)

    def row(k, lo):
        return ring[k, :, lo : lo + LANES] if k < 4 else ring_surface[:, lo : lo + LANES]

    left, right = edge_tiles(z, 5, lambda k: row(k, 0), lambda k: row(k, z.base), 1)
    by_parity("lon", c1, c2, right, left)
    south, north = ring_sum(z, layer_weight(ring[2], ring[3]))
    put_column_sums(z, msg, sums[...], south, north)


def in_band(z, shape):
    lat = lax.axis_index("lat")
    row = lax.broadcasted_iota(jnp.int32, shape, 0)
    south = jnp.where(lat > 0, 1.0, 0.0)
    north = jnp.where(lat < z.n_lat - 1, 1.0, 0.0)
    return jnp.where(row < z.L, south, north)


def ring_geopot(z, h, t):
    w = layer_weight(h, t)
    row = row_iota(w)
    level = jnp.where(row < z.L, row, row - z.L)
    q = 0.5 * w
    for s in range(1, z.L):
        q = q + jnp.where(level < z.L - s, pltpu.roll(w, 2 * z.L - s, 0), 0.0)
    return q * in_band(z, w.shape)


def tendencies(coef, u, v, h, t, un, vs, hn, hs, tn, ts, q, qn, which="uvht"):
    zonal, cor, corn, north, south = coef
    out = {}
    if "u" in which:
        a = v + vs
        out["u"] = u + cor * (a + east(a)) - zonal * (east(q) - q)
    if "v" in which:
        b = u + un
        out["v"] = v - corn * (b + west(b)) - NORTH_COEF * (qn - q)
    if "h" in which:
        flux = u * (2.0 + h + east(h)) * 0.5
        out["h"] = (
            h
            - zonal * (flux - west(flux))
            - (north * (v * (2.0 + h + hn) * 0.5) - south * (vs * (2.0 + hs + h) * 0.5))
        )
    if "t" in which:
        out["t"] = (
            t
            - 0.25 * (u + west(u)) * zonal * (east(t) - west(t))
            - (0.25 * NORTH_COEF) * (v + vs) * (tn - ts)
        )
    return out


def advance_tile(z, geom, get, un_row, vs_row, h_ring, t_ring, q_ring, put, qput=None):
    coef = [wide(geom, k, 0, z.R, z.W) for k in range(5)]
    below = None
    for l in reversed(range(z.L)):
        u, v, h, t = (get(f, l) for f in range(4))
        w = layer_weight(h, t)
        q = 0.5 * w if below is None else below + 0.5 * w
        below = w if below is None else below + w
        s, n = l, z.L + l
        new = tendencies(
            coef, u, v, h, t,
            with_last(u, un_row(l)), with_first(v, vs_row(l)),
            with_last(h, h_ring[n : n + 1, :]), with_first(h, h_ring[s : s + 1, :]),
            with_last(t, t_ring[n : n + 1, :]), with_first(t, t_ring[s : s + 1, :]),
            q, with_last(q, q_ring[n : n + 1, :]),
        )
        for f, name in enumerate("uvht"):
            put(f, l, new[name])
        if qput is not None:
            qput(l, q)


def first_step(
    z, x, ring_in, surface_in, r1, r2, geom, y, yring, ring_surface, ring, inner, q_ring, from_right, from_left
):
    L = z.L
    by_parity("lon", from_right, from_left, r1[...], r2[...])
    right, left = from_right[...], from_left[...]
    ring[...] = ring_in[...]
    ring_surface[...] = surface_in[...]
    for k in range(5):
        patch(z, ring.at[k] if k < 4 else ring_surface, k, 5, 1, right, left)
    q_ring[...] = ring_geopot(z, ring[2], ring[3])

    def get(f, l):
        return x[f * L + l]

    def put(f, l, value):
        y[f * L + l] = value

    def qput(l, q):
        inner[3, l : l + 1, :] = q[0:1]

    inner[3, L:, :] = jnp.zeros((L, z.W), jnp.float32)
    advance_tile(
        z, geom, get,
        lambda l: ring[0, L + l : L + l + 1, :], lambda l: ring[1, l : l + 1, :],
        ring.at[2], ring.at[3], q_ring, put, qput,
    )
    for l in range(L):
        inner[0, l : l + 1, :] = x[l, 0:1, :]
        inner[0, L + l : L + l + 1, :] = x[L + l, z.R - 1 : z.R, :]
        for k, f in ((1, 2), (2, 3)):
            inner[k, l : l + 1, :] = x[f * L + l, 0:1, :]
            inner[k, L + l : L + l + 1, :] = x[f * L + l, z.R - 1 : z.R, :]
    south = lax.broadcasted_iota(jnp.int32, (2 * L, z.W), 0) < L
    coef = [wide(geom, k, z.R, z.R + 2 * L, z.W) for k in range(5)]
    u, v, h, t = (ring[k] for k in range(4))
    new = tendencies(
        coef, u, v, h, t,
        inner[0], jnp.where(south, ring[4], inner[0]),
        jnp.where(south, inner[1], ring[5]), jnp.where(south, ring[5], inner[1]),
        jnp.where(south, inner[2], ring[6]), jnp.where(south, ring[6], inner[2]),
        q_ring[...], inner[3],
    )
    mask = in_band(z, (2 * L, z.W))
    yring[0] = jnp.where(south, new["v"], new["u"]) * mask
    yring[1] = new["h"] * mask
    yring[2] = new["t"] * mask


def level_part(z, surface, ring_surface, got):
    live = jnp.where(lax.axis_index("lev") < z.n_lev - 1, 1.0, 0.0)
    lat = lax.axis_index("lat")
    tile = surface + live * got[:, 0 : z.W]
    rows, beneath = [], []
    for d in range(2):
        there = jnp.where(lat > 0, 1.0, 0.0) if d == 0 else jnp.where(lat < z.n_lat - 1, 1.0, 0.0)
        parts = []
        for t in range(z.tiles):
            at = z.W + (d * z.extra + t // z.R) * LANES
            parts.append(got[t % z.R : t % z.R + 1, at : at + LANES])
        sums = jnp.concatenate(parts, 1)
        sums = jnp.where(lax.broadcasted_iota(jnp.int32, sums.shape, 1) < z.C, sums, 0.0)
        beneath.append(there * live * sums)
        rows.append(there * ring_surface[d * z.L : d * z.L + 1, :] + beneath[d])
    return tile, rows[0], rows[1], beneath[1]


def split(x):
    high = x.astype(jnp.bfloat16)
    return high, (x - high.astype(jnp.float32)).astype(jnp.bfloat16)


def dot(a, b, dims):
    return lax.dot_general(a, b, (dims, ((), ())), preferred_element_type=jnp.float32)


def product(x, wh, wl, dims):
    high, low = split(x)
    return dot(high, wh[...], dims) + dot(low, wh[...], dims) + dot(high, wl[...], dims)


def masked(z, x):
    tail = x[:, z.base :]
    lane = lax.broadcasted_iota(jnp.int32, tail.shape, 1)
    tail = jnp.where(lane < z.C - z.base, tail, 0.0)
    return jnp.concatenate([x[:, : z.base], tail], 1) if z.base else tail


def spectra(z, x, wh, wl, phase):
    s = product(x, wh, wl, ((1,), (0,)))
    a, b = s[:, :KMAX], s[:, KMAX:]
    c, d = phase[0:1, :], phase[1:2, :]
    return jnp.concatenate([a * c - b * d, a * d + b * c], 1)


def twice(x):
    return jnp.concatenate([x, x], 1)


def code_bit(code, k):
    return twice((code >> k) & 1) == 1


def compress(z, tile, code):
    for b in range(z.bits):
        tile = jnp.where(code_bit(code, b), pltpu.roll(tile, z.R - (1 << b), 0), tile)
    return tile


def expand(z, tile, code):
    for b in reversed(range(z.bits)):
        tile = jnp.where(code_bit(code, z.bits + b), pltpu.roll(tile, 1 << b, 0), tile)
    return tile


def pick_spectra(z, full, code, out):
    code = code[0 : z.R, :]
    row = lax.broadcasted_iota(jnp.int32, (z.R, 2 * KMAX), 0)
    for i in range(2 * z.L):
        a = compress(z, full[2 * i * z.R : (2 * i + 1) * z.R], code)
        b = compress(z, full[(2 * i + 1) * z.R : (2 * i + 2) * z.R], code)
        out[i * z.R : (i + 1) * z.R, :] = jnp.where(row < z.slots, a, pltpu.roll(b, z.slots, 0))


def first_spectra(z, y, yring, surface, ring_surface, got, geom, wh, wl, phase, code, state, sring, out):
    L = z.L
    g, gs, gn, beneath = level_part(z, surface[...], ring_surface, got)
    du = wide(geom, 0, 0, z.R, z.W) * (east(g) - g)
    dv = NORTH_COEF * (with_last(g, gn) - g)
    for l in range(L):
        state[l] = y[l] - du
        state[L + l] = y[L + l] - dv
    for p in range(2 * L, 4 * L):
        state[p] = y[p]
    shape = (2 * L, z.W)
    south = lax.broadcasted_iota(jnp.int32, shape, 0) < L
    zonal = wide(geom, 0, z.R, z.R + 2 * L, z.W)
    gn = jnp.broadcast_to(gn, shape)
    du_north = zonal * (east(gn) - gn)
    dv_south = NORTH_COEF * jnp.broadcast_to(g[0:1] - gs, shape)
    uv = yring[0] - jnp.where(south, dv_south, du_north) * in_band(z, shape)
    sring[0] = uv
    sring[1] = yring[1]
    sring[2] = yring[2]
    lane = lax.broadcasted_iota(jnp.int32, shape, 1)
    corner = jnp.broadcast_to(beneath[:, 0:1], shape)
    given = jnp.where((lane == z.W - 1) & jnp.logical_not(south), -zonal * corner, masked(z, uv))
    m = 4 * L * z.R
    everything = jnp.concatenate(
        [
            masked(z, state[...].reshape(m, z.W)),
            given,
            masked(z, sring[1]),
            masked(z, sring[2]),
        ],
        0,
    )
    full = spectra(z, everything, wh, wl, phase)
    pick_spectra(z, full, code, out)
    at = 4 * L * z.slots
    out[at : at + 6 * L, :] = full[m:, :]
    wide_shape = (2 * L, 2 * KMAX)
    lane = lax.broadcasted_iota(jnp.int32, wide_shape, 1)
    lon = lax.axis_index("lon")
    ends = jnp.where(south[:, 0:1], uv[:, 0:1], uv[:, z.C - 1 : z.C])
    out[at + 6 * L :, :] = jnp.where(
        lane == lon,
        jnp.broadcast_to(ends, wide_shape),
        jnp.where(lane == KMAX + lon, jnp.broadcast_to(beneath[:, 0:1], wide_shape), 0.0),
    )


def second_spectra(z, y, surface, ring_surface, got, geom, wh, wl, phase, code, state, out):
    L = z.L
    g, _, gn, _ = level_part(z, surface[...], ring_surface, got)
    du = wide(geom, 0, 0, z.R, z.W) * (east(g) - g)
    dv = NORTH_COEF * (with_last(g, gn) - g)
    for l in range(L):
        state[l] = y[l] - du
        state[L + l] = y[L + l] - dv
    for p in range(2 * L, 4 * L):
        state[p] = y[p]
    full = spectra(z, masked(z, state[...].reshape(4 * L * z.R, z.W)), wh, wl, phase)
    pick_spectra(z, full, code, out)


def mode_weight(z, keep):
    keep = twice(keep)
    k = lax.broadcasted_iota(jnp.int32, keep.shape, 1)
    k = jnp.where(k < KMAX, k, k - KMAX)
    scale = jnp.where(k == 0, 1.0 / z.N, 2.0 / z.N)
    return jnp.where(k < keep, scale, 0.0)


def keeps(z, code):
    keep = code[...] >> (2 * z.bits)
    return keep[0 : z.R], keep[z.R :]


def damping(z, keep, width):
    value = jnp.where(keep > 0, 1.0 - DAMPING, 0.0)
    return jnp.concatenate([value] * (width // LANES), 1)


def local_modes(total, phase):
    a, b = total[:, :KMAX], total[:, KMAX:]
    c, d = phase[0:1, :], phase[1:2, :]
    return jnp.concatenate([a * c + b * d, b * c - a * d], 1)


def tile_modes(z, modes, code, weight):
    code = code[0 : z.R, :]
    out = []
    for i in range(2 * z.L):
        pair = modes[i * z.R : (i + 1) * z.R]
        out.append(expand(z, pair, code) * weight)
        out.append(expand(z, pltpu.roll(pair, z.R - z.slots, 0), code) * weight)
    return out


def smooth(modes, wh, wl):
    return product(modes, wh, wl, ((1,), (1,)))


def filter_mass(z, state, sring, part, got, wh, wl, phase, code, ht, htring, uvmodes, msg):
    L, m = z.L, 4 * z.L * z.slots
    total = part[...] + got[...]
    modes = local_modes(total, phase)
    keep, rkeep = keeps(z, code)
    weight, rweight = mode_weight(z, keep), mode_weight(z, rkeep)
    ring = [modes[m + k * 2 * L : m + (k + 1) * 2 * L] * rweight for k in range(3)]
    tiles = tile_modes(z, modes, code, weight)
    uvmodes[...] = jnp.concatenate(tiles[: 2 * L] + [ring[0], total[m + 6 * L :]], 0)
    s = smooth(jnp.concatenate(tiles[2 * L :] + ring[1:], 0), wh, wl)
    damp, rdamp = damping(z, keep, z.W), damping(z, rkeep, z.W)
    for p in range(2 * L):
        x = state[2 * L + p]
        ht[p] = x + damp * (s[p * z.R : (p + 1) * z.R] - x)
    for k in range(2):
        x = sring[1 + k]
        at = 2 * L * z.R + k * 2 * L
        htring[k] = x + rdamp * (s[at : at + 2 * L] - x)
    total = layer_weight(ht[0], ht[L])
    for l in range(1, L):
        total = total + layer_weight(ht[l], ht[L + l])
    south, north = ring_sum(z, layer_weight(htring[0], htring[1]))
    put_column_sums(z, msg, total, south, north)


def ring_corners(z, uv, gathered, geom):
    shape = uv.shape
    lon = lax.axis_index("lon")
    right = jnp.where(lon == z.n_lon - 1, 0, lon + 1)
    left = jnp.where(lon == 0, z.n_lon - 1, lon - 1)
    place = lax.broadcasted_iota(jnp.int32, gathered.shape, 1)

    def of(lane):
        value = jnp.sum(jnp.where(place == lane, gathered, 0.0), 1, keepdims=True)
        return jnp.broadcast_to(value, shape)

    south = lax.broadcasted_iota(jnp.int32, shape, 0) < z.L
    north = jnp.logical_not(south)
    lane = lax.broadcasted_iota(jnp.int32, shape, 1)
    zonal = wide(geom, 0, z.R, z.R + 2 * z.L, z.W)
    uv = jnp.where((lane == z.C) & south, of(right), uv)
    uv = jnp.where((lane == z.W - 1) & north, of(left) - zonal * of(KMAX + lon), uv)
    corner = of(KMAX + right)
    uv = jnp.where((lane == z.C - 1) & north, uv - zonal * corner, uv)
    row = lax.broadcasted_iota(jnp.int32, shape, 0)
    above = jnp.where((lane == z.C) & (row == z.R - 1), NORTH_COEF * corner, 0.0)
    return uv, above


def second_step(z, state, sring, uvmodes, ht, htring, geom, wh, wl, code, y, uv, uvring, q_ring):
    L = z.L
    m = 2 * L * z.R
    s = smooth(uvmodes[0 : m + 2 * L, :], wh, wl)
    keep, rkeep = keeps(z, code)
    damp, rdamp = damping(z, keep, z.W), damping(z, rkeep, z.W)
    x, above = ring_corners(z, sring[0], uvmodes[m + 2 * L :, :], geom)
    for p in range(2 * L):
        old = state[p] if p < L else state[p] - above
        uv[p] = old + damp * (s[p * z.R : (p + 1) * z.R] - old)
    uvring[...] = x + rdamp * (s[m:] - x)
    q_ring[...] = ring_geopot(z, htring[0], htring[1])

    def get(f, l):
        return uv[f * L + l] if f < 2 else ht[(f - 2) * L + l]

    def put(f, l, value):
        y[f * L + l] = value

    advance_tile(
        z, geom, get,
        lambda l: uvring[L + l : L + l + 1, :], lambda l: uvring[l : l + 1, :],
        htring.at[0], htring.at[1], q_ring, put,
    )


def filter_all(z, state, part, got, wh, wl, phase, code, out, held, sem):
    L = z.L
    modes = local_modes(part[...] + got[...], phase)
    keep, _ = keeps(z, code)
    high, low = split(jnp.concatenate(tile_modes(z, modes, code, mode_weight(z, keep)), 0))
    across = ((1,), (1,))
    copies = []
    for i, (lo, hi) in enumerate(z.chunks):
        top = min(-(-hi // LANES) * LANES, z.W)
        w, v = wh[lo:top, :], wl[lo:top, :]
        s = dot(high, w, across) + dot(low, w, across) + dot(high, v, across)
        d = damping(z, keep, top - lo)
        for p in range(4 * L):
            x = state[p, :, lo:top]
            new = x + d * (s[p * z.R : (p + 1) * z.R] - x)
            held[p // L, p % L, :, lo:hi] = new[:, : hi - lo]
        copies.append(
            pltpu.make_async_copy(held.at[:, :, :, lo:hi], out.at[:, :, :, lo:hi], sem.at[i])
        )
        copies[-1].start()
    for copy in copies:
        copy.wait()


def row_code(z, rows, counts, out):
    row = lax.broadcasted_iota(jnp.int32, (z.R + 2 * z.L, LANES), 0)
    lat = lax.axis_index("lat")
    code = jnp.zeros(row.shape, jnp.int32)
    for s in range(z.slots):
        at = rows[lat * z.slots + s] - lat * z.R
        far = at - s
        code = code + jnp.where(row == at, counts[lat * z.slots + s] << (2 * z.bits), 0)
        for b in range(z.bits):
            bit = (far >> b) & 1
            to = at - (bit << b)
            code = code + jnp.where((row == to) & (bit == 1), 1 << b, 0)
            code = code + jnp.where((row == at) & (bit == 1), 1 << (z.bits + b), 0)
            at = to
    before = jnp.maximum(lat * z.slots - 1, 0)
    after = jnp.minimum((lat + 1) * z.slots, z.filters - 1)
    south = jnp.where((lat > 0) & (rows[before] == lat * z.R - 1), counts[before], 0)
    north = jnp.where(
        (lat < z.n_lat - 1) & (rows[after] == (lat + 1) * z.R), counts[after], 0
    )
    ring = jnp.where(row < z.R + z.L, south, north) << (2 * z.bits)
    out[...] = jnp.where(row < z.R, code, ring)


def local(z, wave_high, wave_low, fields, surface, filter_rows, keep_counts):
    L, R, W = z.L, z.R, z.W
    f32 = jnp.float32
    vmem = pl.BlockSpec(memory_space=pltpu.VMEM)

    def call(kernel, outs, ins, scratch=(), flops=1_000_000, aliases={}):
        size = sum(int(np.prod(s)) for s in outs) * 4 + sum(i.size * i.dtype.itemsize for i in ins)
        return pl.pallas_call(
            functools.partial(kernel, z),
            out_shape=[jax.ShapeDtypeStruct(s, f32) for s in outs],
            in_specs=[vmem] * len(ins),
            out_specs=[vmem] * len(outs),
            scratch_shapes=[pltpu.VMEM(s, f32) for s in scratch],
            input_output_aliases=aliases,
            compiler_params=pltpu.CompilerParams(vmem_limit_bytes=VMEM_LIMIT),
            cost_estimate=pl.CostEstimate(flops=flops, bytes_accessed=size, transcendentals=0),
            name=kernel.__name__,
        )(*ins)

    lat, lon = lax.axis_index("lat"), lax.axis_index("lon")
    index = lax.broadcasted_iota(jnp.int32, (R + 2 * L, LANES), 0)
    index = jnp.where(index < R, index, jnp.where(index < R + L, -1, R))
    based = (lat * R + index).astype(f32)
    to_radian = jnp.pi / 180.0
    middle = (FIRST_LAT + (based + 0.5) * ROW_STEP) * to_radian
    northern = (FIRST_LAT + (based + 1.0) * ROW_STEP) * to_radian
    southern = (FIRST_LAT + based * ROW_STEP) * to_radian
    cos_mid = jnp.cos(middle)
    geom = jnp.stack(
        [
            ZONAL_COEF / cos_mid,
            (0.25 * CORIOLIS) * jnp.sin(middle),
            (0.25 * CORIOLIS) * jnp.sin(northern),
            NORTH_COEF * jnp.cos(northern) / cos_mid,
            NORTH_COEF * jnp.cos(southern) / cos_mid,
        ]
    )
    turn = (lon * z.C * jnp.arange(KMAX, dtype=jnp.int32)) % z.N
    angle = turn.astype(f32) * (2.0 * jnp.pi / z.N)
    phase = jnp.stack([jnp.cos(angle), jnp.sin(angle)])

    smem = pl.BlockSpec(memory_space=pltpu.SMEM)
    code = pl.pallas_call(
        functools.partial(row_code, z),
        out_shape=jax.ShapeDtypeStruct((R + 2 * L, LANES), jnp.int32),
        in_specs=[smem] * 2,
        out_specs=vmem,
        name="row_code",
    )(filter_rows, keep_counts)

    lon_one = [(i, i ^ 1) for i in range(z.n_lon)]
    lon_two = [(i, (((i + 1) % z.n_lon ^ 1) - 1) % z.n_lon) for i in range(z.n_lon)]
    lat_one = [(i, i ^ 1) for i in range(z.n_lat) if i ^ 1 < z.n_lat]
    lat_two = [(i, ((i + 1) ^ 1) - 1) for i in range(1, z.n_lat) if ((i + 1) ^ 1) - 1 < z.n_lat]

    def from_below(column):
        if z.n_lev == 2:
            return lax.ppermute(column, "lev", [(0, 1), (1, 0)])
        place = lax.axis_index("lev")
        total = jnp.zeros_like(column)
        for s in range(1, z.n_lev):
            got = lax.ppermute(column, "lev", [(i, i - s) for i in range(s, z.n_lev)])
            total = total + jnp.where(place + s < z.n_lev, got, 0.0)
        return total

    def over_lon(part):
        got, step = None, 1
        while step < z.n_lon:
            if got is not None:
                part = part + got
            got = lax.ppermute(part, "lon", [(i, i ^ step) for i in range(z.n_lon)])
            step *= 2
        return part, got

    tile = (R, LANES)
    outs = [(z.planes, R, W), (z.lat_rows, W), (z.lat_rows, W), tile, tile]
    x, m1, m2, e1, e2 = pl.pallas_call(
        functools.partial(place_tiles, z),
        out_shape=[jax.ShapeDtypeStruct(s, f32) for s in outs],
        in_specs=[pl.BlockSpec(memory_space=pltpu.HBM)] * 2,
        out_specs=[vmem] * 5,
        scratch_shapes=[
            pltpu.VMEM((4, L, R, z.C), f32),
            pltpu.VMEM((R, z.C), f32),
            pltpu.SemaphoreType.DMA((5,)),
        ],
        compiler_params=pltpu.CompilerParams(vmem_limit_bytes=VMEM_LIMIT),
        name="place_tiles",
    )(fields, surface)
    m1 = lax.ppermute(m1, "lat", lat_one)
    m2 = lax.ppermute(m2, "lat", lat_two)
    e1 = lax.ppermute(e1, "lon", lon_one)
    e2 = lax.ppermute(e2, "lon", lon_two)
    x, sums = call(
        widen, [(z.planes, R, W), (R, W)], [x, e1, e2], [tile] * 2, aliases={0: 0}
    )

    sent = (R, W + 2 * z.extra * LANES)
    ring, ring_surface, msg, c1, c2 = call(
        halo_rows, [(7, 2 * L, W), (2 * L, W), sent, tile, tile], [sums, m1, m2]
    )
    c1 = lax.ppermute(c1, "lon", lon_one)
    c2 = lax.ppermute(c2, "lon", lon_two)
    got = from_below(msg)
    y, yring, ring_surface = call(
        first_step,
        [(4 * L, R, W), (3, 2 * L, W), (2 * L, W)],
        [x, ring, ring_surface, c1, c2, geom],
        [(7, 2 * L, W), (4, 2 * L, W), (2 * L, W), tile, tile],
        flops=10_000_000,
    )
    surface_tile = x[4 * L]
    state, sring, part = call(
        first_spectra,
        [(4 * L, R, W), (3, 2 * L, W), (4 * L * z.slots + 8 * L, 2 * KMAX)],
        [y, yring, surface_tile, ring_surface, got, geom, wave_high, wave_low, phase, code],
    )
    part, got = over_lon(part)
    ht, htring, uvmodes, msg = call(
        filter_mass,
        [(2 * L, R, W), (2, 2 * L, W), (2 * L * R + 4 * L, 2 * KMAX), sent],
        [state, sring, part, got, wave_high, wave_low, phase, code],
    )
    got = from_below(msg)
    (y,) = call(
        second_step,
        [(4 * L, R, W)],
        [state, sring, uvmodes, ht, htring, geom, wave_high, wave_low, code],
        [(2 * L, R, W), (2 * L, W), (2 * L, W)],
        flops=10_000_000,
    )
    state, part = call(
        second_spectra,
        [(4 * L, R, W), (4 * L * z.slots, 2 * KMAX)],
        [y, surface_tile, ring_surface, got, geom, wave_high, wave_low, phase, code],
    )
    part, got = over_lon(part)
    return pl.pallas_call(
        functools.partial(filter_all, z),
        out_shape=jax.ShapeDtypeStruct((4, L, R, z.C), f32),
        in_specs=[vmem] * 7,
        out_specs=pl.BlockSpec(memory_space=pl.ANY),
        scratch_shapes=[
            pltpu.VMEM((4, L, R, z.C), f32),
            pltpu.SemaphoreType.DMA((len(z.chunks),)),
        ],
        compiler_params=pltpu.CompilerParams(vmem_limit_bytes=VMEM_LIMIT),
        name="filter_all",
    )(state, part, got, wave_high, wave_low, phase, code)


def wave_tables(z):
    lane = np.arange(z.W)
    j = np.where(lane >= z.W - 2, lane - z.W, lane)
    angle = 2.0 * np.pi * ((j[:, None] * np.arange(KMAX)[None, :]) % z.N) / z.N
    table = np.concatenate([np.cos(angle), np.sin(angle)], 1).astype(np.float32)
    high = table.astype(ml_dtypes.bfloat16)
    low = (table - high.astype(np.float32)).astype(ml_dtypes.bfloat16)
    return high, low


def solution(mesh):
    def run(fields, surface, filter_rows, keep_counts):
        z = Sizes(mesh, fields.shape, filter_rows.shape[0])
        high, low = wave_tables(z)

        def body(fields, surface, filter_rows, keep_counts):
            return local(
                z, jnp.asarray(high), jnp.asarray(low), fields, surface, filter_rows, keep_counts
            )

        spec = P(None, "lev", "lat", "lon")
        return jax.shard_map(
            body,
            mesh=mesh,
            in_specs=(spec, P("lat", "lon"), P(), P()),
            out_specs=spec,
            check_vma=False,
        )(fields, surface, filter_rows, keep_counts)

    return run
```

```python
import functools

import jax
import jax.numpy as jnp
import ml_dtypes
import numpy as np
from jax import lax
from jax.experimental import pallas as pl
from jax.experimental.pallas import tpu as pltpu
from jax.sharding import PartitionSpec as P

KMAX = 128
GRAVITY_SCALE = 0.05
BUOYANCY = 0.5
CORIOLIS = 0.3
ZONAL_COEF = 0.08
NORTH_COEF = 0.2
DAMPING = 0.25
FIRST_LAT = -70.0
ROW_STEP = 0.05
LANES = 128
VMEM_LIMIT = 24 * 1024 * 1024


def layer_weight(h, t):
    return GRAVITY_SCALE * (1.0 + h) * (1.0 + BUOYANCY * t)


def east(x):
    return pltpu.roll(x, x.shape[1] - 1, 1)


def west(x):
    return pltpu.roll(x, 1, 1)


def rows_up(x):
    return pltpu.roll(x, x.shape[0] - 1, 0)


def rows_down(x):
    return pltpu.roll(x, 1, 0)


def row_iota(x):
    return lax.broadcasted_iota(jnp.int32, x.shape, 0)


def with_last(x, row):
    return jnp.where(row_iota(x) == x.shape[0] - 1, jnp.broadcast_to(row, x.shape), rows_up(x))


def with_first(x, row):
    return jnp.where(row_iota(x) == 0, jnp.broadcast_to(row, x.shape), rows_down(x))


def wide(geom, k, lo, hi, width):
    return jnp.concatenate([geom[k, lo:hi, :]] * (width // LANES), 1)


class Sizes:
    def __init__(self, mesh, fields_shape, filter_count):
        _, levels, rows, columns = fields_shape
        self.n_lon, self.n_lat, self.n_lev = (mesh.shape[a] for a in ("lon", "lat", "lev"))
        self.L = levels // self.n_lev
        self.R = rows // self.n_lat
        self.C = columns // self.n_lon
        self.N = columns
        self.W = -(-(self.C + 4) // LANES) * LANES
        self.slots = filter_count // self.n_lat
        self.filters = filter_count
        self.planes = 4 * self.L + 1
        self.base = (self.C - 1) // LANES * LANES
        self.tiles = self.W // LANES
        self.extra = -(-self.tiles // self.R)
        self.fold = -(-self.tiles // 2)
        self.lat_lanes = 3 * self.W + (self.fold + self.extra) * LANES
        width = -(-self.base // LANES // 3) * LANES if self.base else self.W
        cuts = [c for c in range(0, self.base + 1, width)] if self.base else [0]
        if self.C - cuts[-1] <= LANES and len(cuts) > 1:
            cuts.pop()
        self.chunks = list(zip(cuts, cuts[1:] + [self.C]))
        self.bits = (self.R - self.slots).bit_length()
        assert self.R == 2 * self.slots and self.n_lon <= KMAX
        assert self.R == 2 * self.L and self.n_lon % 2 == 0
        assert 2 <= self.C - self.base <= LANES - 2 and 2 * self.planes <= LANES


def edge_tiles(z, count, head, tail, width):
    lane = lax.broadcasted_iota(jnp.int32, (z.R, LANES), 1)
    left = jnp.zeros((z.R, LANES), jnp.float32)
    right = left
    first = z.C - width - z.base
    for p in range(count):
        here = (lane >= width * p) & (lane < width * (p + 1))
        left = jnp.where(here, moved(head(p), width * p), left)
        right = jnp.where(here, moved(tail(p), width * p - first), right)
    return left, right


def moved(x, shift):
    shift = shift % x.shape[1]
    return pltpu.roll(x, shift, 1) if shift else x


def by_parity(axis, first, second, even, odd):
    is_even = lax.axis_index(axis) % 2 == 0

    @pl.when(is_even)
    def _():
        first[...] = even
        second[...] = odd

    @pl.when(jnp.logical_not(is_even))
    def _():
        first[...] = odd
        second[...] = even


def patch(z, ref, p, count, width, from_right, from_left):
    lane = lax.broadcasted_iota(jnp.int32, (z.R, LANES), 1)
    last = z.C - z.base
    right = moved(from_right, last - width * p)
    left = moved(from_left, LANES - width - width * p)
    for start in sorted({z.base, z.W - LANES}):
        tile = ref[:, start : start + LANES]
        if start == z.base:
            tile = jnp.where((lane >= last) & (lane < last + width), right, tile)
        if start == z.W - LANES:
            tile = jnp.where(lane >= LANES - width, left, tile)
        ref[:, start : start + LANES] = tile


def edge_rows(z, x, m1, m2, after):
    L, W = z.L, z.W
    fold = z.fold * LANES
    after[...] = jnp.zeros(after.shape, jnp.float32)
    lat_even = lax.axis_index("lat") % 2 == 0
    near1 = jnp.where(lat_even, z.R - 1, 0)
    far1 = jnp.where(lat_even, z.R - 2, 1)
    for msg, near, far in ((m1, near1, far1), (m2, z.R - 1 - near1, z.R - 1 - far1)):
        msg[:, 3 * W :] = jnp.zeros((z.R, z.lat_lanes - 3 * W), jnp.float32)
        for k in range(7):
            f, at = (k, near) if k < 4 else (k - 3, far)
            for l in range(L):
                row = x[f * L + l, pl.ds(at, 1), :]
                to = (k % 2) * L + l
                if k < 6:
                    msg[to : to + 1, k // 2 * W : (k // 2 + 1) * W] = row
                else:
                    msg[l : l + 1, 3 * W : 3 * W + fold] = row[:, 0:fold]
                    msg[L + l : L + l + 1, 3 * W : 4 * W - fold] = row[:, fold:]
        row = x[4 * L, pl.ds(near, 1), :]
        for t in range(z.tiles):
            at = 3 * W + fold + t // z.R * LANES
            msg[t % z.R : t % z.R + 1, at : at + LANES] = row[:, t * LANES : (t + 1) * LANES]


def edge_columns(z, x, after, e1, e2):
    del after
    left, right = edge_tiles(
        z,
        z.planes,
        lambda p: x[p, :, 0:LANES],
        lambda p: x[p, :, z.base : z.base + LANES],
        2,
    )
    by_parity("lon", e1, e2, right, left)


def widen(z, x_in, r1, r2, x, sums, from_right, from_left):
    del x_in
    by_parity("lon", from_right, from_left, r1[...], r2[...])
    right, left = from_right[...], from_left[...]
    for p in range(z.planes):
        patch(z, x.at[p], p, z.planes, 2, right, left)
    total = layer_weight(x[2 * z.L], x[3 * z.L])
    for l in range(1, z.L):
        total = total + layer_weight(x[2 * z.L + l], x[3 * z.L + l])
    sums[...] = total


def put_column_sums(z, msg, total, south, north):
    if total is not None:
        msg[:, 0 : z.W] = total
    for d, row in enumerate((south, north)):
        for t in range(z.tiles):
            at = z.W + (d * z.extra + t // z.R) * LANES
            msg[t % z.R : t % z.R + 1, at : at + LANES] = row[:, t * LANES : (t + 1) * LANES]


def ring_sum(z, w):
    south = w[0:1]
    north = w[z.L : z.L + 1]
    for l in range(1, z.L):
        south = south + w[l : l + 1]
        north = north + w[z.L + l : z.L + l + 1]
    return south, north


def halo_rows(z, sums, r1, r2, ring, ring_surface, msg, c1, c2):
    lat_even = lax.axis_index("lat") % 2 == 0

    def place(d, source):
        L, W = z.L, z.W
        fold = z.fold * LANES
        here = slice(d * L, (d + 1) * L)
        for k in range(6):
            at = (k % 2) * L
            ring[k, here, :] = source[at : at + L, k // 2 * W : (k // 2 + 1) * W]
        ring[6, here, 0:fold] = source[0:L, 3 * W : 3 * W + fold]
        ring[6, here, fold:] = source[L : 2 * L, 3 * W : 3 * W + W - fold]
        for t in range(z.tiles):
            at = 3 * W + fold + t // z.R * LANES
            part = source[t % z.R : t % z.R + 1, at : at + LANES]
            ring_surface[here, t * LANES : (t + 1) * LANES] = jnp.broadcast_to(part, (L, LANES))

    @pl.when(lat_even)
    def _():
        place(0, r2)
        place(1, r1)

    @pl.when(jnp.logical_not(lat_even))
    def _():
        place(0, r1)
        place(1, r2)

    def row(k, lo):
        return ring[k, :, lo : lo + LANES] if k < 4 else ring_surface[:, lo : lo + LANES]

    left, right = edge_tiles(z, 5, lambda k: row(k, 0), lambda k: row(k, z.base), 1)
    by_parity("lon", c1, c2, right, left)
    south, north = ring_sum(z, layer_weight(ring[2], ring[3]))
    put_column_sums(z, msg, sums[...], south, north)


def in_band(z, shape):
    lat = lax.axis_index("lat")
    row = lax.broadcasted_iota(jnp.int32, shape, 0)
    south = jnp.where(lat > 0, 1.0, 0.0)
    north = jnp.where(lat < z.n_lat - 1, 1.0, 0.0)
    return jnp.where(row < z.L, south, north)


def ring_geopot(z, h, t):
    w = layer_weight(h, t)
    row = row_iota(w)
    level = jnp.where(row < z.L, row, row - z.L)
    q = 0.5 * w
    for s in range(1, z.L):
        q = q + jnp.where(level < z.L - s, pltpu.roll(w, 2 * z.L - s, 0), 0.0)
    return q * in_band(z, w.shape)


def tendencies(coef, u, v, h, t, un, vs, hn, hs, tn, ts, q, qn, which="uvht"):
    zonal, cor, corn, north, south = coef
    out = {}
    if "u" in which:
        a = v + vs
        out["u"] = u + cor * (a + east(a)) - zonal * (east(q) - q)
    if "v" in which:
        b = u + un
        out["v"] = v - corn * (b + west(b)) - NORTH_COEF * (qn - q)
    if "h" in which:
        flux = u * (2.0 + h + east(h)) * 0.5
        out["h"] = (
            h
            - zonal * (flux - west(flux))
            - (north * (v * (2.0 + h + hn) * 0.5) - south * (vs * (2.0 + hs + h) * 0.5))
        )
    if "t" in which:
        out["t"] = (
            t
            - 0.25 * (u + west(u)) * zonal * (east(t) - west(t))
            - (0.25 * NORTH_COEF) * (v + vs) * (tn - ts)
        )
    return out


def advance_tile(z, geom, get, un_row, vs_row, h_ring, t_ring, q_ring, put, qput=None):
    coef = [wide(geom, k, 0, z.R, z.W) for k in range(5)]
    below = None
    for l in reversed(range(z.L)):
        u, v, h, t = (get(f, l) for f in range(4))
        w = layer_weight(h, t)
        q = 0.5 * w if below is None else below + 0.5 * w
        below = w if below is None else below + w
        s, n = l, z.L + l
        new = tendencies(
            coef, u, v, h, t,
            with_last(u, un_row(l)), with_first(v, vs_row(l)),
            with_last(h, h_ring[n : n + 1, :]), with_first(h, h_ring[s : s + 1, :]),
            with_last(t, t_ring[n : n + 1, :]), with_first(t, t_ring[s : s + 1, :]),
            q, with_last(q, q_ring[n : n + 1, :]),
        )
        for f, name in enumerate("uvht"):
            put(f, l, new[name])
        if qput is not None:
            qput(l, q)


def first_step(
    z, x, ring_in, surface_in, r1, r2, geom, y, yring, ring_surface, ring, inner, q_ring, from_right, from_left
):
    L = z.L
    by_parity("lon", from_right, from_left, r1[...], r2[...])
    right, left = from_right[...], from_left[...]
    ring[...] = ring_in[...]
    ring_surface[...] = surface_in[...]
    for k in range(5):
        patch(z, ring.at[k] if k < 4 else ring_surface, k, 5, 1, right, left)
    q_ring[...] = ring_geopot(z, ring[2], ring[3])

    def get(f, l):
        return x[f * L + l]

    def put(f, l, value):
        y[f * L + l] = value

    def qput(l, q):
        inner[3, l : l + 1, :] = q[0:1]

    inner[3, L:, :] = jnp.zeros((L, z.W), jnp.float32)
    advance_tile(
        z, geom, get,
        lambda l: ring[0, L + l : L + l + 1, :], lambda l: ring[1, l : l + 1, :],
        ring.at[2], ring.at[3], q_ring, put, qput,
    )
    for l in range(L):
        inner[0, l : l + 1, :] = x[l, 0:1, :]
        inner[0, L + l : L + l + 1, :] = x[L + l, z.R - 1 : z.R, :]
        for k, f in ((1, 2), (2, 3)):
            inner[k, l : l + 1, :] = x[f * L + l, 0:1, :]
            inner[k, L + l : L + l + 1, :] = x[f * L + l, z.R - 1 : z.R, :]
    south = lax.broadcasted_iota(jnp.int32, (2 * L, z.W), 0) < L
    coef = [wide(geom, k, z.R, z.R + 2 * L, z.W) for k in range(5)]
    u, v, h, t = (ring[k] for k in range(4))
    new = tendencies(
        coef, u, v, h, t,
        inner[0], jnp.where(south, ring[4], inner[0]),
        jnp.where(south, inner[1], ring[5]), jnp.where(south, ring[5], inner[1]),
        jnp.where(south, inner[2], ring[6]), jnp.where(south, ring[6], inner[2]),
        q_ring[...], inner[3],
    )
    mask = in_band(z, (2 * L, z.W))
    yring[0] = jnp.where(south, new["v"], new["u"]) * mask
    yring[1] = new["h"] * mask
    yring[2] = new["t"] * mask


def level_part(z, surface, ring_surface, got):
    live = jnp.where(lax.axis_index("lev") < z.n_lev - 1, 1.0, 0.0)
    lat = lax.axis_index("lat")
    tile = surface + live * got[:, 0 : z.W]
    rows, beneath = [], []
    for d in range(2):
        there = jnp.where(lat > 0, 1.0, 0.0) if d == 0 else jnp.where(lat < z.n_lat - 1, 1.0, 0.0)
        parts = []
        for t in range(z.tiles):
            at = z.W + (d * z.extra + t // z.R) * LANES
            parts.append(got[t % z.R : t % z.R + 1, at : at + LANES])
        sums = jnp.concatenate(parts, 1)
        sums = jnp.where(lax.broadcasted_iota(jnp.int32, sums.shape, 1) < z.C, sums, 0.0)
        beneath.append(there * live * sums)
        rows.append(there * ring_surface[d * z.L : d * z.L + 1, :] + beneath[d])
    return tile, rows[0], rows[1], beneath[1]


def split(x):
    high = x.astype(jnp.bfloat16)
    return high, (x - high.astype(jnp.float32)).astype(jnp.bfloat16)


def dot(a, b, dims):
    return lax.dot_general(a, b, (dims, ((), ())), preferred_element_type=jnp.float32)


def product(x, wh, wl, dims):
    high, low = split(x)
    return dot(high, wh[...], dims) + dot(low, wh[...], dims) + dot(high, wl[...], dims)


def masked(z, x):
    tail = x[:, z.base :]
    lane = lax.broadcasted_iota(jnp.int32, tail.shape, 1)
    tail = jnp.where(lane < z.C - z.base, tail, 0.0)
    return jnp.concatenate([x[:, : z.base], tail], 1) if z.base else tail


def spectra(z, x, wh, wl, phase):
    s = product(x, wh, wl, ((1,), (0,)))
    a, b = s[:, :KMAX], s[:, KMAX:]
    c, d = phase[0:1, :], phase[1:2, :]
    return jnp.concatenate([a * c - b * d, a * d + b * c], 1)


def twice(x):
    return jnp.concatenate([x, x], 1)


def code_bit(code, k):
    return twice((code >> k) & 1) == 1


def compress(z, tile, code):
    for b in range(z.bits):
        tile = jnp.where(code_bit(code, b), pltpu.roll(tile, z.R - (1 << b), 0), tile)
    return tile


def expand(z, tile, code):
    for b in reversed(range(z.bits)):
        tile = jnp.where(code_bit(code, z.bits + b), pltpu.roll(tile, 1 << b, 0), tile)
    return tile


def pick_spectra(z, full, code, out):
    code = code[0 : z.R, :]
    row = lax.broadcasted_iota(jnp.int32, (z.R, 2 * KMAX), 0)
    for i in range(2 * z.L):
        a = compress(z, full[2 * i * z.R : (2 * i + 1) * z.R], code)
        b = compress(z, full[(2 * i + 1) * z.R : (2 * i + 2) * z.R], code)
        out[i * z.R : (i + 1) * z.R, :] = jnp.where(row < z.slots, a, pltpu.roll(b, z.slots, 0))


def first_spectra(z, y, yring, surface, ring_surface, got, geom, wh, wl, phase, code, state, sring, out):
    L = z.L
    g, gs, gn, beneath = level_part(z, surface[...], ring_surface, got)
    du = wide(geom, 0, 0, z.R, z.W) * (east(g) - g)
    dv = NORTH_COEF * (with_last(g, gn) - g)
    for l in range(L):
        state[l] = y[l] - du
        state[L + l] = y[L + l] - dv
    for p in range(2 * L, 4 * L):
        state[p] = y[p]
    shape = (2 * L, z.W)
    south = lax.broadcasted_iota(jnp.int32, shape, 0) < L
    zonal = wide(geom, 0, z.R, z.R + 2 * L, z.W)
    gn = jnp.broadcast_to(gn, shape)
    du_north = zonal * (east(gn) - gn)
    dv_south = NORTH_COEF * jnp.broadcast_to(g[0:1] - gs, shape)
    uv = yring[0] - jnp.where(south, dv_south, du_north) * in_band(z, shape)
    sring[0] = uv
    sring[1] = yring[1]
    sring[2] = yring[2]
    lane = lax.broadcasted_iota(jnp.int32, shape, 1)
    corner = jnp.broadcast_to(beneath[:, 0:1], shape)
    given = jnp.where((lane == z.W - 1) & jnp.logical_not(south), -zonal * corner, masked(z, uv))
    m = 4 * L * z.R
    everything = jnp.concatenate(
        [
            masked(z, state[...].reshape(m, z.W)),
            given,
            masked(z, sring[1]),
            masked(z, sring[2]),
        ],
        0,
    )
    full = spectra(z, everything, wh, wl, phase)
    pick_spectra(z, full, code, out)
    at = 4 * L * z.slots
    out[at : at + 6 * L, :] = full[m:, :]
    wide_shape = (2 * L, 2 * KMAX)
    lane = lax.broadcasted_iota(jnp.int32, wide_shape, 1)
    lon = lax.axis_index("lon")
    ends = jnp.where(south[:, 0:1], uv[:, 0:1], uv[:, z.C - 1 : z.C])
    out[at + 6 * L :, :] = jnp.where(
        lane == lon,
        jnp.broadcast_to(ends, wide_shape),
        jnp.where(lane == KMAX + lon, jnp.broadcast_to(beneath[:, 0:1], wide_shape), 0.0),
    )


def second_spectra(z, y, surface, ring_surface, got, geom, wh, wl, phase, code, state, out):
    L = z.L
    g, _, gn, _ = level_part(z, surface[...], ring_surface, got)
    du = wide(geom, 0, 0, z.R, z.W) * (east(g) - g)
    dv = NORTH_COEF * (with_last(g, gn) - g)
    for l in range(L):
        state[l] = y[l] - du
        state[L + l] = y[L + l] - dv
    for p in range(2 * L, 4 * L):
        state[p] = y[p]
    full = spectra(z, masked(z, state[...].reshape(4 * L * z.R, z.W)), wh, wl, phase)
    pick_spectra(z, full, code, out)


def mode_weight(z, keep):
    keep = twice(keep)
    k = lax.broadcasted_iota(jnp.int32, keep.shape, 1)
    k = jnp.where(k < KMAX, k, k - KMAX)
    scale = jnp.where(k == 0, 1.0 / z.N, 2.0 / z.N)
    return jnp.where(k < keep, scale, 0.0)


def keeps(z, code):
    keep = code[...] >> (2 * z.bits)
    return keep[0 : z.R], keep[z.R :]


def damping(z, keep, width):
    value = jnp.where(keep > 0, 1.0 - DAMPING, 0.0)
    return jnp.concatenate([value] * (width // LANES), 1)


def local_modes(total, phase):
    a, b = total[:, :KMAX], total[:, KMAX:]
    c, d = phase[0:1, :], phase[1:2, :]
    return jnp.concatenate([a * c + b * d, b * c - a * d], 1)


def tile_modes(z, modes, code, weight):
    code = code[0 : z.R, :]
    out = []
    for i in range(2 * z.L):
        pair = modes[i * z.R : (i + 1) * z.R]
        out.append(expand(z, pair, code) * weight)
        out.append(expand(z, pltpu.roll(pair, z.R - z.slots, 0), code) * weight)
    return out


def smooth(modes, wh, wl):
    return product(modes, wh, wl, ((1,), (1,)))


def filter_mass(z, state, sring, part, got, wh, wl, phase, code, ht, htring, uvmodes, msg):
    L, m = z.L, 4 * z.L * z.slots
    total = part[...] + got[...]
    modes = local_modes(total, phase)
    keep, rkeep = keeps(z, code)
    weight, rweight = mode_weight(z, keep), mode_weight(z, rkeep)
    ring = [modes[m + k * 2 * L : m + (k + 1) * 2 * L] * rweight for k in range(3)]
    tiles = tile_modes(z, modes, code, weight)
    uvmodes[...] = jnp.concatenate(tiles[: 2 * L] + [ring[0], total[m + 6 * L :]], 0)
    s = smooth(jnp.concatenate(tiles[2 * L :] + ring[1:], 0), wh, wl)
    damp, rdamp = damping(z, keep, z.W), damping(z, rkeep, z.W)
    for p in range(2 * L):
        x = state[2 * L + p]
        ht[p] = x + damp * (s[p * z.R : (p + 1) * z.R] - x)
    for k in range(2):
        x = sring[1 + k]
        at = 2 * L * z.R + k * 2 * L
        htring[k] = x + rdamp * (s[at : at + 2 * L] - x)
    total = layer_weight(ht[0], ht[L])
    for l in range(1, L):
        total = total + layer_weight(ht[l], ht[L + l])
    south, north = ring_sum(z, layer_weight(htring[0], htring[1]))
    put_column_sums(z, msg, total, south, north)


def ring_corners(z, uv, gathered, geom):
    shape = uv.shape
    lon = lax.axis_index("lon")
    right = jnp.where(lon == z.n_lon - 1, 0, lon + 1)
    left = jnp.where(lon == 0, z.n_lon - 1, lon - 1)
    place = lax.broadcasted_iota(jnp.int32, gathered.shape, 1)

    def of(lane):
        value = jnp.sum(jnp.where(place == lane, gathered, 0.0), 1, keepdims=True)
        return jnp.broadcast_to(value, shape)

    south = lax.broadcasted_iota(jnp.int32, shape, 0) < z.L
    north = jnp.logical_not(south)
    lane = lax.broadcasted_iota(jnp.int32, shape, 1)
    zonal = wide(geom, 0, z.R, z.R + 2 * z.L, z.W)
    uv = jnp.where((lane == z.C) & south, of(right), uv)
    uv = jnp.where((lane == z.W - 1) & north, of(left) - zonal * of(KMAX + lon), uv)
    corner = of(KMAX + right)
    uv = jnp.where((lane == z.C - 1) & north, uv - zonal * corner, uv)
    row = lax.broadcasted_iota(jnp.int32, shape, 0)
    above = jnp.where((lane == z.C) & (row == z.R - 1), NORTH_COEF * corner, 0.0)
    return uv, above


def second_step(z, state, sring, uvmodes, ht, htring, geom, wh, wl, code, y, uv, uvring, q_ring):
    L = z.L
    m = 2 * L * z.R
    s = smooth(uvmodes[0 : m + 2 * L, :], wh, wl)
    keep, rkeep = keeps(z, code)
    damp, rdamp = damping(z, keep, z.W), damping(z, rkeep, z.W)
    x, above = ring_corners(z, sring[0], uvmodes[m + 2 * L :, :], geom)
    for p in range(2 * L):
        old = state[p] if p < L else state[p] - above
        uv[p] = old + damp * (s[p * z.R : (p + 1) * z.R] - old)
    uvring[...] = x + rdamp * (s[m:] - x)
    q_ring[...] = ring_geopot(z, htring[0], htring[1])

    def get(f, l):
        return uv[f * L + l] if f < 2 else ht[(f - 2) * L + l]

    def put(f, l, value):
        y[f * L + l] = value

    advance_tile(
        z, geom, get,
        lambda l: uvring[L + l : L + l + 1, :], lambda l: uvring[l : l + 1, :],
        htring.at[0], htring.at[1], q_ring, put,
    )


def filter_all(z, state, part, got, wh, wl, phase, code, out, held, sem):
    L = z.L
    modes = local_modes(part[...] + got[...], phase)
    keep, _ = keeps(z, code)
    high, low = split(jnp.concatenate(tile_modes(z, modes, code, mode_weight(z, keep)), 0))
    across = ((1,), (1,))
    copies = []
    for i, (lo, hi) in enumerate(z.chunks):
        top = min(-(-hi // LANES) * LANES, z.W)
        w, v = wh[lo:top, :], wl[lo:top, :]
        s = dot(high, w, across) + dot(low, w, across) + dot(high, v, across)
        d = damping(z, keep, top - lo)
        for p in range(4 * L):
            x = state[p, :, lo:top]
            new = x + d * (s[p * z.R : (p + 1) * z.R] - x)
            held[p // L, p % L, :, lo:hi] = new[:, : hi - lo]
        copies.append(
            pltpu.make_async_copy(held.at[:, :, :, lo:hi], out.at[:, :, :, lo:hi], sem.at[i])
        )
        copies[-1].start()
    for copy in copies:
        copy.wait()


def row_code(z, rows, counts, out):
    row = lax.broadcasted_iota(jnp.int32, (z.R + 2 * z.L, LANES), 0)
    lat = lax.axis_index("lat")
    code = jnp.zeros(row.shape, jnp.int32)
    for s in range(z.slots):
        at = rows[lat * z.slots + s] - lat * z.R
        far = at - s
        code = code + jnp.where(row == at, counts[lat * z.slots + s] << (2 * z.bits), 0)
        for b in range(z.bits):
            bit = (far >> b) & 1
            to = at - (bit << b)
            code = code + jnp.where((row == to) & (bit == 1), 1 << b, 0)
            code = code + jnp.where((row == at) & (bit == 1), 1 << (z.bits + b), 0)
            at = to
    before = jnp.maximum(lat * z.slots - 1, 0)
    after = jnp.minimum((lat + 1) * z.slots, z.filters - 1)
    south = jnp.where((lat > 0) & (rows[before] == lat * z.R - 1), counts[before], 0)
    north = jnp.where(
        (lat < z.n_lat - 1) & (rows[after] == (lat + 1) * z.R), counts[after], 0
    )
    ring = jnp.where(row < z.R + z.L, south, north) << (2 * z.bits)
    out[...] = jnp.where(row < z.R, code, ring)


def local(z, wave_high, wave_low, fields, surface, filter_rows, keep_counts):
    L, R, W = z.L, z.R, z.W
    f32 = jnp.float32
    vmem = pl.BlockSpec(memory_space=pltpu.VMEM)

    def call(kernel, outs, ins, scratch=(), flops=1_000_000, aliases={}):
        size = sum(int(np.prod(s)) for s in outs) * 4 + sum(i.size * i.dtype.itemsize for i in ins)
        return pl.pallas_call(
            functools.partial(kernel, z),
            out_shape=[jax.ShapeDtypeStruct(s, f32) for s in outs],
            in_specs=[vmem] * len(ins),
            out_specs=[vmem] * len(outs),
            scratch_shapes=[pltpu.VMEM(s, f32) for s in scratch],
            input_output_aliases=aliases,
            compiler_params=pltpu.CompilerParams(vmem_limit_bytes=VMEM_LIMIT),
            cost_estimate=pl.CostEstimate(flops=flops, bytes_accessed=size, transcendentals=0),
            name=kernel.__name__,
        )(*ins)

    lat, lon = lax.axis_index("lat"), lax.axis_index("lon")
    index = lax.broadcasted_iota(jnp.int32, (R + 2 * L, LANES), 0)
    index = jnp.where(index < R, index, jnp.where(index < R + L, -1, R))
    based = (lat * R + index).astype(f32)
    to_radian = jnp.pi / 180.0
    middle = (FIRST_LAT + (based + 0.5) * ROW_STEP) * to_radian
    northern = (FIRST_LAT + (based + 1.0) * ROW_STEP) * to_radian
    southern = (FIRST_LAT + based * ROW_STEP) * to_radian
    cos_mid = jnp.cos(middle)
    geom = jnp.stack(
        [
            ZONAL_COEF / cos_mid,
            (0.25 * CORIOLIS) * jnp.sin(middle),
            (0.25 * CORIOLIS) * jnp.sin(northern),
            NORTH_COEF * jnp.cos(northern) / cos_mid,
            NORTH_COEF * jnp.cos(southern) / cos_mid,
        ]
    )
    turn = (lon * z.C * jnp.arange(KMAX, dtype=jnp.int32)) % z.N
    angle = turn.astype(f32) * (2.0 * jnp.pi / z.N)
    phase = jnp.stack([jnp.cos(angle), jnp.sin(angle)])

    smem = pl.BlockSpec(memory_space=pltpu.SMEM)
    code = pl.pallas_call(
        functools.partial(row_code, z),
        out_shape=jax.ShapeDtypeStruct((R + 2 * L, LANES), jnp.int32),
        in_specs=[smem] * 2,
        out_specs=vmem,
        name="row_code",
    )(filter_rows, keep_counts)

    lon_one = [(i, i ^ 1) for i in range(z.n_lon)]
    lon_two = [(i, (((i + 1) % z.n_lon ^ 1) - 1) % z.n_lon) for i in range(z.n_lon)]
    lat_one = [(i, i ^ 1) for i in range(z.n_lat) if i ^ 1 < z.n_lat]
    lat_two = [(i, ((i + 1) ^ 1) - 1) for i in range(1, z.n_lat) if ((i + 1) ^ 1) - 1 < z.n_lat]

    def from_below(column):
        if z.n_lev == 2:
            return lax.ppermute(column, "lev", [(0, 1), (1, 0)])
        place = lax.axis_index("lev")
        total = jnp.zeros_like(column)
        for s in range(1, z.n_lev):
            got = lax.ppermute(column, "lev", [(i, i - s) for i in range(s, z.n_lev)])
            total = total + jnp.where(place + s < z.n_lev, got, 0.0)
        return total

    def over_lon(part):
        got, step = None, 1
        while step < z.n_lon:
            if got is not None:
                part = part + got
            got = lax.ppermute(part, "lon", [(i, i ^ step) for i in range(z.n_lon)])
            step *= 2
        return part, got

    tile = (R, LANES)
    x = jnp.concatenate([fields.reshape(4 * L, R, z.C), surface[None]], 0)
    x = jnp.pad(x, ((0, 0), (0, 0), (0, W - z.C)))
    m1, m2, after = call(edge_rows, [(R, z.lat_lanes)] * 2 + [tile], [x])
    m1 = lax.ppermute(m1, "lat", lat_one)
    m2 = lax.ppermute(m2, "lat", lat_two)
    e1, e2 = call(edge_columns, [tile, tile], [x, after])
    e1 = lax.ppermute(e1, "lon", lon_one)
    e2 = lax.ppermute(e2, "lon", lon_two)
    x, sums = call(
        widen, [(z.planes, R, W), (R, W)], [x, e1, e2], [tile] * 2, aliases={0: 0}
    )

    sent = (R, W + 2 * z.extra * LANES)
    ring, ring_surface, msg, c1, c2 = call(
        halo_rows, [(7, 2 * L, W), (2 * L, W), sent, tile, tile], [sums, m1, m2]
    )
    c1 = lax.ppermute(c1, "lon", lon_one)
    c2 = lax.ppermute(c2, "lon", lon_two)
    got = from_below(msg)
    y, yring, ring_surface = call(
        first_step,
        [(4 * L, R, W), (3, 2 * L, W), (2 * L, W)],
        [x, ring, ring_surface, c1, c2, geom],
        [(7, 2 * L, W), (4, 2 * L, W), (2 * L, W), tile, tile],
        flops=10_000_000,
    )
    surface_tile = x[4 * L]
    state, sring, part = call(
        first_spectra,
        [(4 * L, R, W), (3, 2 * L, W), (4 * L * z.slots + 8 * L, 2 * KMAX)],
        [y, yring, surface_tile, ring_surface, got, geom, wave_high, wave_low, phase, code],
    )
    part, got = over_lon(part)
    ht, htring, uvmodes, msg = call(
        filter_mass,
        [(2 * L, R, W), (2, 2 * L, W), (2 * L * R + 4 * L, 2 * KMAX), sent],
        [state, sring, part, got, wave_high, wave_low, phase, code],
    )
    got = from_below(msg)
    (y,) = call(
        second_step,
        [(4 * L, R, W)],
        [state, sring, uvmodes, ht, htring, geom, wave_high, wave_low, code],
        [(2 * L, R, W), (2 * L, W), (2 * L, W)],
        flops=10_000_000,
    )
    state, part = call(
        second_spectra,
        [(4 * L, R, W), (4 * L * z.slots, 2 * KMAX)],
        [y, surface_tile, ring_surface, got, geom, wave_high, wave_low, phase, code],
    )
    part, got = over_lon(part)
    return pl.pallas_call(
        functools.partial(filter_all, z),
        out_shape=jax.ShapeDtypeStruct((4, L, R, z.C), f32),
        in_specs=[vmem] * 7,
        out_specs=pl.BlockSpec(memory_space=pl.ANY),
        scratch_shapes=[
            pltpu.VMEM((4, L, R, z.C), f32),
            pltpu.SemaphoreType.DMA((len(z.chunks),)),
        ],
        compiler_params=pltpu.CompilerParams(vmem_limit_bytes=VMEM_LIMIT),
        name="filter_all",
    )(state, part, got, wave_high, wave_low, phase, code)


def wave_tables(z):
    lane = np.arange(z.W)
    j = np.where(lane >= z.W - 2, lane - z.W, lane)
    angle = 2.0 * np.pi * ((j[:, None] * np.arange(KMAX)[None, :]) % z.N) / z.N
    table = np.concatenate([np.cos(angle), np.sin(angle)], 1).astype(np.float32)
    high = table.astype(ml_dtypes.bfloat16)
    low = (table - high.astype(np.float32)).astype(ml_dtypes.bfloat16)
    return high, low


def solution(mesh):
    def run(fields, surface, filter_rows, keep_counts):
        z = Sizes(mesh, fields.shape, filter_rows.shape[0])
        high, low = wave_tables(z)

        def body(fields, surface, filter_rows, keep_counts):
            return local(
                z, jnp.asarray(high), jnp.asarray(low), fields, surface, filter_rows, keep_counts
            )

        spec = P(None, "lev", "lat", "lon")
        return jax.shard_map(
            body,
            mesh=mesh,
            in_specs=(spec, P("lat", "lon"), P(), P()),
            out_specs=spec,
            check_vma=False,
        )(fields, surface, filter_rows, keep_counts)

    return run
```

```python
import functools

import jax
import jax.numpy as jnp
import ml_dtypes
import numpy as np
from jax import lax
from jax.experimental import pallas as pl
from jax.experimental.pallas import tpu as pltpu
from jax.sharding import PartitionSpec as P

KMAX = 128
GRAVITY_SCALE = 0.05
BUOYANCY = 0.5
CORIOLIS = 0.3
ZONAL_COEF = 0.08
NORTH_COEF = 0.2
DAMPING = 0.25
FIRST_LAT = -70.0
ROW_STEP = 0.05
LANES = 128
VMEM_LIMIT = 24 * 1024 * 1024


def layer_weight(h, t):
    return GRAVITY_SCALE * (1.0 + h) * (1.0 + BUOYANCY * t)


def east(x):
    return pltpu.roll(x, x.shape[1] - 1, 1)


def west(x):
    return pltpu.roll(x, 1, 1)


def rows_up(x):
    return pltpu.roll(x, x.shape[0] - 1, 0)


def rows_down(x):
    return pltpu.roll(x, 1, 0)


def row_iota(x):
    return lax.broadcasted_iota(jnp.int32, x.shape, 0)


def with_last(x, row):
    return jnp.where(row_iota(x) == x.shape[0] - 1, jnp.broadcast_to(row, x.shape), rows_up(x))


def with_first(x, row):
    return jnp.where(row_iota(x) == 0, jnp.broadcast_to(row, x.shape), rows_down(x))


def wide(geom, k, lo, hi, width):
    return jnp.concatenate([geom[k, lo:hi, :]] * (width // LANES), 1)


class Sizes:
    def __init__(self, mesh, fields_shape, filter_count):
        _, levels, rows, columns = fields_shape
        self.n_lon, self.n_lat, self.n_lev = (mesh.shape[a] for a in ("lon", "lat", "lev"))
        self.L = levels // self.n_lev
        self.R = rows // self.n_lat
        self.C = columns // self.n_lon
        self.N = columns
        self.W = -(-(self.C + 4) // LANES) * LANES
        self.slots = filter_count // self.n_lat
        self.filters = filter_count
        self.planes = 4 * self.L + 1
        self.base = (self.C - 1) // LANES * LANES
        self.tiles = self.W // LANES
        self.extra = -(-self.tiles // self.R)
        whole = self.base // LANES
        self.fold = -(-whole // 2)
        self.lat_lanes = 3 * self.base + (self.fold + -(-whole // self.R)) * LANES
        width = -(-self.base // LANES // 3) * LANES if self.base else self.W
        cuts = [c for c in range(0, self.base + 1, width)] if self.base else [0]
        if self.C - cuts[-1] <= LANES and len(cuts) > 1:
            cuts.pop()
        self.chunks = list(zip(cuts, cuts[1:] + [self.C]))
        self.bits = (self.R - self.slots).bit_length()
        assert self.R == 2 * self.slots and self.base > 0
        assert self.R == 2 * self.L and self.n_lon % 4 == 0 and self.L % 2 == 0
        assert 2 <= self.C - self.base <= LANES - 2 and 2 * self.planes <= LANES


def edge_tiles(z, count, head, tail, width):
    lane = lax.broadcasted_iota(jnp.int32, (z.R, LANES), 1)
    left = jnp.zeros((z.R, LANES), jnp.float32)
    right = left
    first = z.C - width - z.base
    for p in range(count):
        here = (lane >= width * p) & (lane < width * (p + 1))
        left = jnp.where(here, moved(head(p), width * p), left)
        right = jnp.where(here, moved(tail(p), width * p - first), right)
    return left, right


def moved(x, shift):
    shift = shift % x.shape[1]
    return pltpu.roll(x, shift, 1) if shift else x


def by_parity(axis, first, second, even, odd):
    is_even = lax.axis_index(axis) % 2 == 0

    @pl.when(is_even)
    def _():
        first[...] = even
        second[...] = odd

    @pl.when(jnp.logical_not(is_even))
    def _():
        first[...] = odd
        second[...] = even


def patch(z, ref, p, count, width, from_right, from_left):
    lane = lax.broadcasted_iota(jnp.int32, (z.R, LANES), 1)
    last = z.C - z.base
    right = moved(from_right, last - width * p)
    left = moved(from_left, LANES - width - width * p)
    for start in sorted({z.base, z.W - LANES}):
        tile = ref[:, start : start + LANES]
        if start == z.base:
            tile = jnp.where((lane >= last) & (lane < last + width), right, tile)
        if start == z.W - LANES:
            tile = jnp.where(lane >= LANES - width, left, tile)
        ref[:, start : start + LANES] = tile


def near_and_far(z):
    lat_even = lax.axis_index("lat") % 2 == 0
    near = jnp.where(lat_even, z.R - 1, 0)
    far = jnp.where(lat_even, z.R - 2, 1)
    return (near, far), (z.R - 1 - near, z.R - 1 - far)


def edge_rows(z, x, m1, m2, after):
    L, B = z.L, z.base
    fold = z.fold * LANES
    after[...] = jnp.zeros(after.shape, jnp.float32)
    for msg, (near, far) in zip((m1, m2), near_and_far(z)):
        msg[:, 3 * B :] = jnp.zeros((z.R, z.lat_lanes - 3 * B), jnp.float32)
        for k in range(7):
            f, at = (k, near) if k < 4 else (k - 3, far)
            for l in range(L):
                row = x[f * L + l, pl.ds(at, 1), 0:B]
                to = (k % 2) * L + l
                if k < 6:
                    msg[to : to + 1, k // 2 * B : (k // 2 + 1) * B] = row
                else:
                    msg[l : l + 1, 3 * B : 3 * B + fold] = row[:, 0:fold]
                    msg[L + l : L + l + 1, 3 * B : 4 * B - fold] = row[:, fold:]
        row = x[4 * L, pl.ds(near, 1), 0:B]
        for t in range(B // LANES):
            at = 3 * B + fold + t // z.R * LANES
            msg[t % z.R : t % z.R + 1, at : at + LANES] = row[:, t * LANES : (t + 1) * LANES]


def edge_columns(z, x, after, e1, e2):
    del after
    left, right = edge_tiles(
        z,
        z.planes,
        lambda p: x[p, :, 0:LANES],
        lambda p: x[p, :, z.base : z.base + LANES],
        2,
    )
    by_parity("lon", e1, e2, right, left)


def widen(z, x_in, r1, r2, x, sums, k1, k2, from_right, from_left):
    del x_in
    L, T = z.L, z.W - z.base
    by_parity("lon", from_right, from_left, r1[...], r2[...])
    right, left = from_right[...], from_left[...]
    for p in range(z.planes):
        patch(z, x.at[p], p, z.planes, 2, right, left)
    total = layer_weight(x[2 * L], x[3 * L])
    for l in range(1, L):
        total = total + layer_weight(x[2 * L + l], x[3 * L + l])
    sums[...] = total
    for msg, (near, far) in zip((k1, k2), near_and_far(z)):
        for k in range(8):
            f, at = (k, near) if k < 4 else (k - 3, far) if k < 7 else (4, near)
            for l in range(L):
                p = f * L + l if k < 7 else 4 * L
                to = (k % 2) * L + l
                msg[to : to + 1, k // 2 * T : (k // 2 + 1) * T] = x[p, pl.ds(at, 1), :][:, z.base :]


def put_ring_sums(z, msg, south, north):
    for d, row in enumerate((south, north)):
        for t in range(z.tiles):
            at = (d * z.extra + t // z.R) * LANES
            msg[t % z.R : t % z.R + 1, at : at + LANES] = row[:, t * LANES : (t + 1) * LANES]


def ring_sum(z, w):
    south = w[0:1]
    north = w[z.L : z.L + 1]
    for l in range(1, z.L):
        south = south + w[l : l + 1]
        north = north + w[z.L + l : z.L + l + 1]
    return south, north


def halo_rows(z, sums, r1, r2, t1, t2, ring, ring_surface, msg):
    lat_even = lax.axis_index("lat") % 2 == 0
    L, B, T = z.L, z.base, z.W - z.base
    fold = z.fold * LANES
    msg[:, 0 : z.W] = sums[...]
    msg[:, z.W :] = jnp.zeros((z.R, 2 * z.extra * LANES), jnp.float32)

    def place(d, source, tail):
        here = slice(d * L, (d + 1) * L)
        for k in range(7):
            at = (k % 2) * L
            if k < 6:
                ring[k, here, 0:B] = source[at : at + L, k // 2 * B : (k // 2 + 1) * B]
            ring[k, here, B:] = tail[at : at + L, k // 2 * T : (k // 2 + 1) * T]
        ring[6, here, 0:fold] = source[0:L, 3 * B : 3 * B + fold]
        ring[6, here, fold:B] = source[L : 2 * L, 3 * B : 4 * B - fold]
        for t in range(B // LANES):
            at = 3 * B + fold + t // z.R * LANES
            part = source[t % z.R : t % z.R + 1, at : at + LANES]
            ring_surface[here, t * LANES : (t + 1) * LANES] = jnp.broadcast_to(part, (L, LANES))
        ring_surface[here, B:] = tail[L : 2 * L, 3 * T :]

    @pl.when(lat_even)
    def _():
        place(0, r2, t2)
        place(1, r1, t1)

    @pl.when(jnp.logical_not(lat_even))
    def _():
        place(0, r1, t1)
        place(1, r2, t2)

    south, north = ring_sum(z, layer_weight(ring[2], ring[3]))
    put_ring_sums(z, msg.at[:, z.W :], south, north)


def in_band(z, shape):
    lat = lax.axis_index("lat")
    row = lax.broadcasted_iota(jnp.int32, shape, 0)
    south = jnp.where(lat > 0, 1.0, 0.0)
    north = jnp.where(lat < z.n_lat - 1, 1.0, 0.0)
    return jnp.where(row < z.L, south, north)


def ring_geopot(z, h, t):
    w = layer_weight(h, t)
    row = row_iota(w)
    level = jnp.where(row < z.L, row, row - z.L)
    q = 0.5 * w
    for s in range(1, z.L):
        q = q + jnp.where(level < z.L - s, pltpu.roll(w, 2 * z.L - s, 0), 0.0)
    return q * in_band(z, w.shape)


def tendencies(coef, u, v, h, t, un, vs, hn, hs, tn, ts, q, qn, which="uvht"):
    zonal, cor, corn, north, south = coef
    out = {}
    if "u" in which:
        a = v + vs
        out["u"] = u + cor * (a + east(a)) - zonal * (east(q) - q)
    if "v" in which:
        b = u + un
        out["v"] = v - corn * (b + west(b)) - NORTH_COEF * (qn - q)
    if "h" in which:
        flux = u * (2.0 + h + east(h)) * 0.5
        out["h"] = (
            h
            - zonal * (flux - west(flux))
            - (north * (v * (2.0 + h + hn) * 0.5) - south * (vs * (2.0 + hs + h) * 0.5))
        )
    if "t" in which:
        out["t"] = (
            t
            - 0.25 * (u + west(u)) * zonal * (east(t) - west(t))
            - (0.25 * NORTH_COEF) * (v + vs) * (tn - ts)
        )
    return out


def advance_tile(z, geom, get, un_row, vs_row, h_ring, t_ring, q_ring, put, qput=None):
    coef = [wide(geom, k, 0, z.R, z.W) for k in range(5)]
    below = None
    for l in reversed(range(z.L)):
        u, v, h, t = (get(f, l) for f in range(4))
        w = layer_weight(h, t)
        q = 0.5 * w if below is None else below + 0.5 * w
        below = w if below is None else below + w
        s, n = l, z.L + l
        new = tendencies(
            coef, u, v, h, t,
            with_last(u, un_row(l)), with_first(v, vs_row(l)),
            with_last(h, h_ring[n : n + 1, :]), with_first(h, h_ring[s : s + 1, :]),
            with_last(t, t_ring[n : n + 1, :]), with_first(t, t_ring[s : s + 1, :]),
            q, with_last(q, q_ring[n : n + 1, :]),
        )
        for f, name in enumerate("uvht"):
            put(f, l, new[name])
        if qput is not None:
            qput(l, q)


def first_step(z, x, ring, geom, y, yring, inner, q_ring):
    L = z.L
    q_ring[...] = ring_geopot(z, ring[2], ring[3])

    def get(f, l):
        return x[f * L + l]

    def put(f, l, value):
        y[f * L + l] = value

    def qput(l, q):
        inner[3, l : l + 1, :] = q[0:1]

    inner[3, L:, :] = jnp.zeros((L, z.W), jnp.float32)
    advance_tile(
        z, geom, get,
        lambda l: ring[0, L + l : L + l + 1, :], lambda l: ring[1, l : l + 1, :],
        ring.at[2], ring.at[3], q_ring, put, qput,
    )
    for l in range(L):
        inner[0, l : l + 1, :] = x[l, 0:1, :]
        inner[0, L + l : L + l + 1, :] = x[L + l, z.R - 1 : z.R, :]
        for k, f in ((1, 2), (2, 3)):
            inner[k, l : l + 1, :] = x[f * L + l, 0:1, :]
            inner[k, L + l : L + l + 1, :] = x[f * L + l, z.R - 1 : z.R, :]
    south = lax.broadcasted_iota(jnp.int32, (2 * L, z.W), 0) < L
    coef = [wide(geom, k, z.R, z.R + 2 * L, z.W) for k in range(5)]
    u, v, h, t = (ring[k] for k in range(4))
    new = tendencies(
        coef, u, v, h, t,
        inner[0], jnp.where(south, ring[4], inner[0]),
        jnp.where(south, inner[1], ring[5]), jnp.where(south, ring[5], inner[1]),
        jnp.where(south, inner[2], ring[6]), jnp.where(south, ring[6], inner[2]),
        q_ring[...], inner[3],
    )
    mask = in_band(z, (2 * L, z.W))
    yring[0] = jnp.where(south, new["v"], new["u"]) * mask
    yring[1] = new["h"] * mask
    yring[2] = new["t"] * mask


def level_part(z, surface, ring_surface, below, ring_below):
    live = jnp.where(lax.axis_index("lev") < z.n_lev - 1, 1.0, 0.0)
    lat = lax.axis_index("lat")
    rows = []
    for d in range(2):
        there = jnp.where(lat > 0, 1.0, 0.0) if d == 0 else jnp.where(lat < z.n_lat - 1, 1.0, 0.0)
        parts = []
        for t in range(z.tiles):
            at = (d * z.extra + t // z.R) * LANES
            parts.append(ring_below[t % z.R : t % z.R + 1, at : at + LANES])
        sums = jnp.concatenate(parts, 1)
        rows.append(there * (ring_surface[d * z.L : d * z.L + 1, :] + live * sums))
    return surface + live * below, rows[0], rows[1]


def split(x):
    high = x.astype(jnp.bfloat16)
    return high, (x - high.astype(jnp.float32)).astype(jnp.bfloat16)


def dot(a, b, dims):
    return lax.dot_general(a, b, (dims, ((), ())), preferred_element_type=jnp.float32)


def product(x, wh, wl, dims):
    high, low = split(x)
    return dot(high, wh[...], dims) + dot(low, wh[...], dims) + dot(high, wl[...], dims)


def masked(z, x):
    tail = x[:, z.base :]
    lane = lax.broadcasted_iota(jnp.int32, tail.shape, 1)
    tail = jnp.where(lane < z.C - z.base, tail, 0.0)
    return jnp.concatenate([x[:, : z.base], tail], 1) if z.base else tail


def spectra(z, x, wh, wl, phase):
    s = product(x, wh, wl, ((1,), (0,)))
    a, b = s[:, :KMAX], s[:, KMAX:]
    c, d = phase[0:1, :], phase[1:2, :]
    return jnp.concatenate([a * c - b * d, a * d + b * c], 1)


def twice(x):
    return jnp.concatenate([x, x], 1)


def code_bit(code, k):
    return twice((code >> k) & 1) == 1


def compress(z, tile, code):
    for b in range(z.bits):
        tile = jnp.where(code_bit(code, b), pltpu.roll(tile, z.R - (1 << b), 0), tile)
    return tile


def expand(z, tile, code):
    for b in reversed(range(z.bits)):
        tile = jnp.where(code_bit(code, z.bits + b), pltpu.roll(tile, 1 << b, 0), tile)
    return tile


def pick_spectra(z, full, code, out):
    code = code[0 : z.R, :]
    row = lax.broadcasted_iota(jnp.int32, (z.R, 2 * KMAX), 0)
    for i in range(2 * z.L):
        a = compress(z, full[2 * i * z.R : (2 * i + 1) * z.R], code)
        b = compress(z, full[(2 * i + 1) * z.R : (2 * i + 2) * z.R], code)
        out[i * z.R : (i + 1) * z.R, :] = jnp.where(row < z.slots, a, pltpu.roll(b, z.slots, 0))


def tile_spectra(z, y, wh, wl, phase, code, out):
    x = masked(z, y[...].reshape(4 * z.L * z.R, z.W))
    pick_spectra(z, spectra(z, x, wh, wl, phase), code, out)


def tile_and_ring_spectra(z, y, yring, wh, wl, phase, code, out):
    m = 4 * z.L * z.R
    x = jnp.concatenate([y[...].reshape(m, z.W), yring[...].reshape(6 * z.L, z.W)], 0)
    full = spectra(z, masked(z, x), wh, wl, phase)
    pick_spectra(z, full, code, out)
    out[4 * z.L * z.slots :, :] = full[m:, :]


def pick_level_part(z, full, code):
    code = code[0 : z.R, :]
    row = lax.broadcasted_iota(jnp.int32, (z.R, 2 * KMAX), 0)
    a = compress(z, full[0 : z.R], code)
    b = compress(z, full[z.R : 2 * z.R], code)
    return jnp.where(row < z.slots, a, pltpu.roll(b, z.slots, 0))


def first_level_spectra(
    z, surface, ring_surface, got, part, part_got, geom, wh, wl, phase, code, sent, own, change, ring_change
):
    L = z.L
    g, gs, gn = level_part(z, surface[...], ring_surface, got[:, 0 : z.W], got[:, z.W :])
    du = wide(geom, 0, 0, z.R, z.W) * (east(g) - g)
    dv = NORTH_COEF * (with_last(g, gn) - g)
    shape = (2 * L, z.W)
    south = lax.broadcasted_iota(jnp.int32, shape, 0) < L
    gn = jnp.broadcast_to(gn, shape)
    du_north = wide(geom, 0, z.R, z.R + 2 * L, z.W) * (east(gn) - gn)
    dv_south = NORTH_COEF * jnp.broadcast_to(g[0:1] - gs, shape)
    ring = jnp.where(south, dv_south, du_north) * in_band(z, shape)
    change[0] = du
    change[1] = dv
    ring_change[...] = ring
    full = spectra(z, masked(z, jnp.concatenate([du, dv, ring], 0)), wh, wl, phase)
    own[0 : z.R, :] = pick_level_part(z, full, code)
    own[z.R :, :] = full[2 * z.R :]
    n = part.shape[0]
    sent[0:n, :] = part[...] + part_got[...]
    sent[n:, :] = own[...]


def second_level_spectra(
    z, surface, ring_surface, got, part, part_got, geom, wh, wl, phase, code, sent, own, change
):
    g, _, gn = level_part(z, surface[...], ring_surface, got[:, 0 : z.W], got[:, z.W :])
    du = wide(geom, 0, 0, z.R, z.W) * (east(g) - g)
    dv = NORTH_COEF * (with_last(g, gn) - g)
    change[0] = du
    change[1] = dv
    full = spectra(z, masked(z, jnp.concatenate([du, dv], 0)), wh, wl, phase)
    own[...] = pick_level_part(z, full, code)
    n = part.shape[0]
    sent[0:n, :] = part[...] + part_got[...]
    sent[n:, :] = own[...]


def total_modes(z, parts):
    if len(parts) == 2:
        return parts[0][...] + parts[1][...]
    mine, got, core, across = parts
    n = mine.shape[0] - core.shape[0]
    total = mine[0:n, :] + got[0:n, :]
    level = (mine[n:, :] + core[...]) + (got[n:, :] + across[...])
    both = level[0 : z.R]
    row = lax.broadcasted_iota(jnp.int32, both.shape, 0)
    other = pltpu.roll(both, z.slots, 0)
    du = jnp.where(row < z.slots, both, other)
    dv = jnp.where(row < z.slots, other, both)
    pairs = z.L // 2
    m = 4 * z.L * z.slots
    tiles = [total[i * z.R : (i + 1) * z.R] - (du if i < pairs else dv) for i in range(z.L)]
    tiles.append(total[z.L * z.R : m])
    if n > m:
        tiles += [total[m : m + 2 * z.L] - level[z.R :], total[m + 2 * z.L :]]
    return jnp.concatenate(tiles, 0)


def join(z, mine, got, core, across, out):
    out[...] = total_modes(z, (mine, got, core, across))


def mode_weight(z, keep):
    keep = twice(keep)
    k = lax.broadcasted_iota(jnp.int32, keep.shape, 1)
    k = jnp.where(k < KMAX, k, k - KMAX)
    scale = jnp.where(k == 0, 1.0 / z.N, 2.0 / z.N)
    return jnp.where(k < keep, scale, 0.0)


def keeps(z, code):
    keep = code[...] >> (2 * z.bits)
    return keep[0 : z.R], keep[z.R :]


def damping(z, keep, width):
    value = jnp.where(keep > 0, 1.0 - DAMPING, 0.0)
    return jnp.concatenate([value] * (width // LANES), 1)


def local_modes(total, phase):
    a, b = total[:, :KMAX], total[:, KMAX:]
    c, d = phase[0:1, :], phase[1:2, :]
    return jnp.concatenate([a * c + b * d, b * c - a * d], 1)


def tile_modes(z, modes, code, weight):
    code = code[0 : z.R, :]
    out = []
    for i in range(2 * z.L):
        pair = modes[i * z.R : (i + 1) * z.R]
        out.append(expand(z, pair, code) * weight)
        out.append(expand(z, pltpu.roll(pair, z.R - z.slots, 0), code) * weight)
    return out


def smooth(modes, wh, wl):
    return product(modes, wh, wl, ((1,), (1,)))


def filter_mass(z, *refs):
    parts, refs = refs[:-10], refs[-10:]
    state, sring, wh, wl, phase, code, ht, htring, uvmodes, msg = refs
    L, m = z.L, 4 * z.L * z.slots
    modes = local_modes(total_modes(z, parts), phase)
    keep, rkeep = keeps(z, code)
    weight, rweight = mode_weight(z, keep), mode_weight(z, rkeep)
    ring = [modes[m + k * 2 * L : m + (k + 1) * 2 * L] * rweight for k in range(3)]
    tiles = tile_modes(z, modes, code, weight)
    uvmodes[...] = jnp.concatenate(tiles[: 2 * L] + [ring[0]], 0)
    s = smooth(jnp.concatenate(tiles[2 * L :] + ring[1:], 0), wh, wl)
    damp, rdamp = damping(z, keep, z.W), damping(z, rkeep, z.W)
    for p in range(2 * L):
        x = state[2 * L + p]
        ht[p] = x + damp * (s[p * z.R : (p + 1) * z.R] - x)
    for k in range(2):
        x = sring[1 + k]
        at = 2 * L * z.R + k * 2 * L
        htring[k] = x + rdamp * (s[at : at + 2 * L] - x)
    total = layer_weight(ht[0], ht[L])
    for l in range(1, L):
        total = total + layer_weight(ht[l], ht[L + l])
    south, north = ring_sum(z, layer_weight(htring[0], htring[1]))
    msg[:, 0 : z.W] = total
    msg[:, z.W :] = jnp.zeros((z.R, 2 * z.extra * LANES), jnp.float32)
    put_ring_sums(z, msg.at[:, z.W :], south, north)


def second_step(z, state, sring, change, ring_change, uvmodes, ht, htring, geom, wh, wl, code, y, uv, uvring, q_ring):
    L = z.L
    m = 2 * L * z.R
    s = smooth(uvmodes[...], wh, wl)
    keep, rkeep = keeps(z, code)
    damp, rdamp = damping(z, keep, z.W), damping(z, rkeep, z.W)
    for p in range(2 * L):
        x = state[p] - change[p // L]
        uv[p] = x + damp * (s[p * z.R : (p + 1) * z.R] - x)
    x = sring[0] - ring_change[...]
    uvring[...] = x + rdamp * (s[m:] - x)
    q_ring[...] = ring_geopot(z, htring[0], htring[1])

    def get(f, l):
        return uv[f * L + l] if f < 2 else ht[(f - 2) * L + l]

    def put(f, l, value):
        y[f * L + l] = value

    advance_tile(
        z, geom, get,
        lambda l: uvring[L + l : L + l + 1, :], lambda l: uvring[l : l + 1, :],
        htring.at[0], htring.at[1], q_ring, put,
    )


def filter_all(z, *refs):
    parts, refs = refs[:-9], refs[-9:]
    state, change, wh, wl, phase, code, out, held, sem = refs
    L = z.L
    modes = local_modes(total_modes(z, parts), phase)
    keep, _ = keeps(z, code)
    high, low = split(jnp.concatenate(tile_modes(z, modes, code, mode_weight(z, keep)), 0))
    across = ((1,), (1,))
    copies = []
    for i, (lo, hi) in enumerate(z.chunks):
        top = min(-(-hi // LANES) * LANES, z.W)
        w, v = wh[lo:top, :], wl[lo:top, :]
        s = dot(high, w, across) + dot(low, w, across) + dot(high, v, across)
        d = damping(z, keep, top - lo)
        for p in range(4 * L):
            x = state[p, :, lo:top]
            if p < 2 * L:
                x = x - change[p // L, :, lo:top]
            new = x + d * (s[p * z.R : (p + 1) * z.R] - x)
            held[p // L, p % L, :, lo:hi] = new[:, : hi - lo]
        copies.append(
            pltpu.make_async_copy(held.at[:, :, :, lo:hi], out.at[:, :, :, lo:hi], sem.at[i])
        )
        copies[-1].start()
    for copy in copies:
        copy.wait()


def row_code(z, rows, counts, out):
    row = lax.broadcasted_iota(jnp.int32, (z.R + 2 * z.L, LANES), 0)
    lat = lax.axis_index("lat")
    code = jnp.zeros(row.shape, jnp.int32)
    for s in range(z.slots):
        at = rows[lat * z.slots + s] - lat * z.R
        far = at - s
        code = code + jnp.where(row == at, counts[lat * z.slots + s] << (2 * z.bits), 0)
        for b in range(z.bits):
            bit = (far >> b) & 1
            to = at - (bit << b)
            code = code + jnp.where((row == to) & (bit == 1), 1 << b, 0)
            code = code + jnp.where((row == at) & (bit == 1), 1 << (z.bits + b), 0)
            at = to
    before = jnp.maximum(lat * z.slots - 1, 0)
    after = jnp.minimum((lat + 1) * z.slots, z.filters - 1)
    south = jnp.where((lat > 0) & (rows[before] == lat * z.R - 1), counts[before], 0)
    north = jnp.where(
        (lat < z.n_lat - 1) & (rows[after] == (lat + 1) * z.R), counts[after], 0
    )
    ring = jnp.where(row < z.R + z.L, south, north) << (2 * z.bits)
    out[...] = jnp.where(row < z.R, code, ring)


def local(z, wave_high, wave_low, fields, surface, filter_rows, keep_counts):
    L, R, W = z.L, z.R, z.W
    f32 = jnp.float32
    vmem = pl.BlockSpec(memory_space=pltpu.VMEM)

    def call(kernel, outs, ins, scratch=(), flops=1_000_000, aliases={}):
        size = sum(int(np.prod(s)) for s in outs) * 4 + sum(i.size * i.dtype.itemsize for i in ins)
        return pl.pallas_call(
            functools.partial(kernel, z),
            out_shape=[jax.ShapeDtypeStruct(s, f32) for s in outs],
            in_specs=[vmem] * len(ins),
            out_specs=[vmem] * len(outs),
            scratch_shapes=[pltpu.VMEM(s, f32) for s in scratch],
            input_output_aliases=aliases,
            compiler_params=pltpu.CompilerParams(vmem_limit_bytes=VMEM_LIMIT),
            cost_estimate=pl.CostEstimate(flops=flops, bytes_accessed=size, transcendentals=0),
            name=kernel.__name__,
        )(*ins)

    lat, lon = lax.axis_index("lat"), lax.axis_index("lon")
    index = lax.broadcasted_iota(jnp.int32, (R + 2 * L, LANES), 0)
    index = jnp.where(index < R, index, jnp.where(index < R + L, -1, R))
    based = (lat * R + index).astype(f32)
    to_radian = jnp.pi / 180.0
    middle = (FIRST_LAT + (based + 0.5) * ROW_STEP) * to_radian
    northern = (FIRST_LAT + (based + 1.0) * ROW_STEP) * to_radian
    southern = (FIRST_LAT + based * ROW_STEP) * to_radian
    cos_mid = jnp.cos(middle)
    geom = jnp.stack(
        [
            ZONAL_COEF / cos_mid,
            (0.25 * CORIOLIS) * jnp.sin(middle),
            (0.25 * CORIOLIS) * jnp.sin(northern),
            NORTH_COEF * jnp.cos(northern) / cos_mid,
            NORTH_COEF * jnp.cos(southern) / cos_mid,
        ]
    )
    turn = (lon * z.C * jnp.arange(KMAX, dtype=jnp.int32)) % z.N
    angle = turn.astype(f32) * (2.0 * jnp.pi / z.N)
    phase = jnp.stack([jnp.cos(angle), jnp.sin(angle)])

    smem = pl.BlockSpec(memory_space=pltpu.SMEM)
    code = pl.pallas_call(
        functools.partial(row_code, z),
        out_shape=jax.ShapeDtypeStruct((R + 2 * L, LANES), jnp.int32),
        in_specs=[smem] * 2,
        out_specs=vmem,
        name="row_code",
    )(filter_rows, keep_counts)

    lon_one = [(i, i ^ 1) for i in range(z.n_lon)]
    lon_two = [(i, (((i + 1) % z.n_lon ^ 1) - 1) % z.n_lon) for i in range(z.n_lon)]
    lat_one = [(i, i ^ 1) for i in range(z.n_lat) if i ^ 1 < z.n_lat]
    lat_two = [(i, ((i + 1) ^ 1) - 1) for i in range(1, z.n_lat) if ((i + 1) ^ 1) - 1 < z.n_lat]

    def from_below(column):
        if z.n_lev == 2:
            return lax.ppermute(column, "lev", [(0, 1), (1, 0)])
        place = lax.axis_index("lev")
        total = jnp.zeros_like(column)
        for s in range(1, z.n_lev):
            got = lax.ppermute(column, "lev", [(i, i - s) for i in range(s, z.n_lev)])
            total = total + jnp.where(place + s < z.n_lev, got, 0.0)
        return total

    def lon_swap(value, step):
        return lax.ppermute(value, "lon", [(i, i ^ step) for i in range(z.n_lon)])

    def over_lon(sent, own, rows):
        parts = [sent, lon_swap(sent, 2), lon_swap(own, 1), lon_swap(own, 3)]
        if z.n_lon == 4:
            return parts
        (part,) = call(join, [(rows, 2 * KMAX)], parts)
        got, step = lon_swap(part, 4), 8
        while step < z.n_lon:
            part = part + got
            got, step = lon_swap(part, step), step * 2
        return [part, got]

    tile = (R, LANES)
    x = jnp.concatenate([fields.reshape(4 * L, R, z.C), surface[None]], 0)
    x = jnp.pad(x, ((0, 0), (0, 0), (0, W - z.C)))
    m1, m2, after = call(edge_rows, [(R, z.lat_lanes)] * 2 + [tile], [x])
    m1 = lax.ppermute(m1, "lat", lat_one)
    m2 = lax.ppermute(m2, "lat", lat_two)
    e1, e2 = call(edge_columns, [tile, tile], [x, after])
    e1 = lax.ppermute(e1, "lon", lon_one)
    e2 = lax.ppermute(e2, "lon", lon_two)
    tails = (R, 4 * (W - z.base))
    x, sums, t1, t2 = call(
        widen,
        [(z.planes, R, W), (R, W), tails, tails],
        [x, e1, e2],
        [tile] * 2,
        aliases={0: 0},
    )
    t1 = lax.ppermute(t1, "lat", lat_one)
    t2 = lax.ppermute(t2, "lat", lat_two)
    ring_lanes = 2 * z.extra * LANES
    ring, ring_surface, msg = call(
        halo_rows, [(7, 2 * L, W), (2 * L, W), (R, W + ring_lanes)], [sums, m1, m2, t1, t2]
    )
    got = from_below(msg)
    y, yring = call(
        first_step,
        [(4 * L, R, W), (3, 2 * L, W)],
        [x, ring, geom],
        [(4, 2 * L, W), (2 * L, W)],
        flops=10_000_000,
    )
    waves = [wave_high, wave_low, phase, code]
    rows = 4 * L * z.slots
    (part,) = call(tile_and_ring_spectra, [(rows + 6 * L, 2 * KMAX)], [y, yring, *waves])
    surface_tile = x[4 * L]
    sent, own, change, ring_change = call(
        first_level_spectra,
        [(rows + 8 * L + R, 2 * KMAX), (2 * L + R, 2 * KMAX), (2, R, W), (2 * L, W)],
        [surface_tile, ring_surface, got, part, lon_swap(part, 1), geom, *waves],
    )
    parts = over_lon(sent, own, rows + 6 * L)
    ht, htring, uvmodes, msg = call(
        filter_mass,
        [(2 * L, R, W), (2, 2 * L, W), (2 * L * R + 2 * L, 2 * KMAX), (R, W + ring_lanes)],
        [*parts, y, yring, *waves],
    )
    got = from_below(msg)
    (y,) = call(
        second_step,
        [(4 * L, R, W)],
        [y, yring, change, ring_change, uvmodes, ht, htring, geom, wave_high, wave_low, code],
        [(2 * L, R, W), (2 * L, W), (2 * L, W)],
        flops=10_000_000,
    )
    (part,) = call(tile_spectra, [(rows, 2 * KMAX)], [y, *waves])
    sent, own, change = call(
        second_level_spectra,
        [(rows + R, 2 * KMAX), (R, 2 * KMAX), (2, R, W)],
        [surface_tile, ring_surface, got, part, lon_swap(part, 1), geom, *waves],
    )
    parts = over_lon(sent, own, rows)
    return pl.pallas_call(
        functools.partial(filter_all, z),
        out_shape=jax.ShapeDtypeStruct((4, L, R, z.C), f32),
        in_specs=[vmem] * (len(parts) + 6),
        out_specs=pl.BlockSpec(memory_space=pl.ANY),
        scratch_shapes=[
            pltpu.VMEM((4, L, R, z.C), f32),
            pltpu.SemaphoreType.DMA((len(z.chunks),)),
        ],
        compiler_params=pltpu.CompilerParams(vmem_limit_bytes=VMEM_LIMIT),
        name="filter_all",
    )(*parts, y, change, *waves)


def wave_tables(z):
    lane = np.arange(z.W)
    j = np.where(lane >= z.W - 2, lane - z.W, lane)
    angle = 2.0 * np.pi * ((j[:, None] * np.arange(KMAX)[None, :]) % z.N) / z.N
    table = np.concatenate([np.cos(angle), np.sin(angle)], 1).astype(np.float32)
    high = table.astype(ml_dtypes.bfloat16)
    low = (table - high.astype(np.float32)).astype(ml_dtypes.bfloat16)
    return high, low


def solution(mesh):
    def run(fields, surface, filter_rows, keep_counts):
        z = Sizes(mesh, fields.shape, filter_rows.shape[0])
        high, low = wave_tables(z)

        def body(fields, surface, filter_rows, keep_counts):
            return local(
                z, jnp.asarray(high), jnp.asarray(low), fields, surface, filter_rows, keep_counts
            )

        spec = P(None, "lev", "lat", "lon")
        return jax.shard_map(
            body,
            mesh=mesh,
            in_specs=(spec, P("lat", "lon"), P(), P()),
            out_specs=spec,
            check_vma=False,
        )(fields, surface, filter_rows, keep_counts)

    return run
```

```python
import functools

import jax
import jax.numpy as jnp
import ml_dtypes
import numpy as np
from jax import lax
from jax.experimental import pallas as pl
from jax.experimental.pallas import tpu as pltpu
from jax.sharding import PartitionSpec as P

KMAX = 128
GRAVITY_SCALE = 0.05
BUOYANCY = 0.5
CORIOLIS = 0.3
ZONAL_COEF = 0.08
NORTH_COEF = 0.2
DAMPING = 0.25
FIRST_LAT = -70.0
ROW_STEP = 0.05
LANES = 128
VMEM_LIMIT = 24 * 1024 * 1024


def layer_weight(h, t):
    return GRAVITY_SCALE * (1.0 + h) * (1.0 + BUOYANCY * t)


def east(x):
    return pltpu.roll(x, x.shape[1] - 1, 1)


def west(x):
    return pltpu.roll(x, 1, 1)


def rows_up(x):
    return pltpu.roll(x, x.shape[0] - 1, 0)


def rows_down(x):
    return pltpu.roll(x, 1, 0)


def row_iota(x):
    return lax.broadcasted_iota(jnp.int32, x.shape, 0)


def with_last(x, row):
    return jnp.where(row_iota(x) == x.shape[0] - 1, jnp.broadcast_to(row, x.shape), rows_up(x))


def with_first(x, row):
    return jnp.where(row_iota(x) == 0, jnp.broadcast_to(row, x.shape), rows_down(x))


def wide(geom, k, lo, hi, width):
    return jnp.concatenate([geom[k, lo:hi, :]] * (width // LANES), 1)


class Sizes:
    def __init__(self, mesh, fields_shape, filter_count):
        _, levels, rows, columns = fields_shape
        self.n_lon, self.n_lat, self.n_lev = (mesh.shape[a] for a in ("lon", "lat", "lev"))
        self.L = levels // self.n_lev
        self.R = rows // self.n_lat
        self.C = columns // self.n_lon
        self.N = columns
        self.W = -(-(self.C + 4) // LANES) * LANES
        self.slots = filter_count // self.n_lat
        self.filters = filter_count
        self.planes = 4 * self.L + 1
        self.base = (self.C - 1) // LANES * LANES
        self.tiles = self.W // LANES
        self.extra = -(-self.tiles // self.R)
        whole = self.base // LANES
        self.fold = -(-whole // 2)
        self.lat_lanes = 3 * self.base + (self.fold + -(-whole // self.R)) * LANES
        width = -(-self.base // LANES // 3) * LANES if self.base else self.W
        cuts = [c for c in range(0, self.base + 1, width)] if self.base else [0]
        if self.C - cuts[-1] <= LANES and len(cuts) > 1:
            cuts.pop()
        self.chunks = list(zip(cuts, cuts[1:] + [self.C]))
        self.bits = (self.R - self.slots).bit_length()
        assert self.R == 2 * self.slots and self.base > 0
        assert self.R == 2 * self.L and self.n_lon % 4 == 0 and self.L % 2 == 0
        assert 2 <= self.C - self.base <= LANES - 2 and 2 * self.planes <= LANES


def edge_tiles(z, count, head, tail, width):
    lane = lax.broadcasted_iota(jnp.int32, (z.R, LANES), 1)
    left = jnp.zeros((z.R, LANES), jnp.float32)
    right = left
    first = z.C - width - z.base
    for p in range(count):
        here = (lane >= width * p) & (lane < width * (p + 1))
        left = jnp.where(here, moved(head(p), width * p), left)
        right = jnp.where(here, moved(tail(p), width * p - first), right)
    return left, right


def moved(x, shift):
    shift = shift % x.shape[1]
    return pltpu.roll(x, shift, 1) if shift else x


def by_parity(axis, first, second, even, odd):
    is_even = lax.axis_index(axis) % 2 == 0

    @pl.when(is_even)
    def _():
        first[...] = even
        second[...] = odd

    @pl.when(jnp.logical_not(is_even))
    def _():
        first[...] = odd
        second[...] = even


def patch(z, ref, p, count, width, from_right, from_left):
    lane = lax.broadcasted_iota(jnp.int32, (z.R, LANES), 1)
    last = z.C - z.base
    right = moved(from_right, last - width * p)
    left = moved(from_left, LANES - width - width * p)
    for start in sorted({z.base, z.W - LANES}):
        tile = ref[:, start : start + LANES]
        if start == z.base:
            tile = jnp.where((lane >= last) & (lane < last + width), right, tile)
        if start == z.W - LANES:
            tile = jnp.where(lane >= LANES - width, left, tile)
        ref[:, start : start + LANES] = tile


def near_and_far(z):
    lat_even = lax.axis_index("lat") % 2 == 0
    near = jnp.where(lat_even, z.R - 1, 0)
    far = jnp.where(lat_even, z.R - 2, 1)
    return (near, far), (z.R - 1 - near, z.R - 1 - far)


def edge_rows(z, x, m1, m2, after):
    L, B = z.L, z.base
    fold = z.fold * LANES
    after[...] = jnp.zeros(after.shape, jnp.float32)
    for msg, (near, far) in zip((m1, m2), near_and_far(z)):
        msg[:, 3 * B :] = jnp.zeros((z.R, z.lat_lanes - 3 * B), jnp.float32)
        for k in range(7):
            f, at = (k, near) if k < 4 else (k - 3, far)
            for l in range(L):
                row = x[f * L + l, pl.ds(at, 1), 0:B]
                to = (k % 2) * L + l
                if k < 6:
                    msg[to : to + 1, k // 2 * B : (k // 2 + 1) * B] = row
                else:
                    msg[l : l + 1, 3 * B : 3 * B + fold] = row[:, 0:fold]
                    msg[L + l : L + l + 1, 3 * B : 4 * B - fold] = row[:, fold:]
        row = x[4 * L, pl.ds(near, 1), 0:B]
        for t in range(B // LANES):
            at = 3 * B + fold + t // z.R * LANES
            msg[t % z.R : t % z.R + 1, at : at + LANES] = row[:, t * LANES : (t + 1) * LANES]


def edge_columns(z, x, after, e1, e2):
    del after
    left, right = edge_tiles(
        z,
        z.planes,
        lambda p: x[p, :, 0:LANES],
        lambda p: x[p, :, z.base : z.base + LANES],
        2,
    )
    by_parity("lon", e1, e2, right, left)


def widen(z, x_in, r1, r2, x, sums, k1, k2, from_right, from_left):
    del x_in
    L, T = z.L, z.W - z.base
    by_parity("lon", from_right, from_left, r1[...], r2[...])
    right, left = from_right[...], from_left[...]
    for p in range(z.planes):
        patch(z, x.at[p], p, z.planes, 2, right, left)
    total = layer_weight(x[2 * L], x[3 * L])
    for l in range(1, L):
        total = total + layer_weight(x[2 * L + l], x[3 * L + l])
    sums[...] = total
    for msg, (near, far) in zip((k1, k2), near_and_far(z)):
        for k in range(8):
            f, at = (k, near) if k < 4 else (k - 3, far) if k < 7 else (4, near)
            for l in range(L):
                p = f * L + l if k < 7 else 4 * L
                to = (k % 2) * L + l
                msg[to : to + 1, k // 2 * T : (k // 2 + 1) * T] = x[p, pl.ds(at, 1), :][:, z.base :]


def put_ring_sums(z, msg, south, north):
    for d, row in enumerate((south, north)):
        for t in range(z.tiles):
            at = (d * z.extra + t // z.R) * LANES
            msg[t % z.R : t % z.R + 1, at : at + LANES] = row[:, t * LANES : (t + 1) * LANES]


def ring_sum(z, w):
    south = w[0:1]
    north = w[z.L : z.L + 1]
    for l in range(1, z.L):
        south = south + w[l : l + 1]
        north = north + w[z.L + l : z.L + l + 1]
    return south, north


def halo_rows(z, sums, r1, r2, t1, t2, ring, ring_surface, msg):
    lat_even = lax.axis_index("lat") % 2 == 0
    L, B, T = z.L, z.base, z.W - z.base
    fold = z.fold * LANES
    msg[:, 0 : z.W] = sums[...]
    msg[:, z.W :] = jnp.zeros((z.R, 2 * z.extra * LANES), jnp.float32)

    def place(d, source, tail):
        here = slice(d * L, (d + 1) * L)
        for k in range(7):
            at = (k % 2) * L
            if k < 6:
                ring[k, here, 0:B] = source[at : at + L, k // 2 * B : (k // 2 + 1) * B]
            ring[k, here, B:] = tail[at : at + L, k // 2 * T : (k // 2 + 1) * T]
        ring[6, here, 0:fold] = source[0:L, 3 * B : 3 * B + fold]
        ring[6, here, fold:B] = source[L : 2 * L, 3 * B : 4 * B - fold]
        for t in range(B // LANES):
            at = 3 * B + fold + t // z.R * LANES
            part = source[t % z.R : t % z.R + 1, at : at + LANES]
            ring_surface[here, t * LANES : (t + 1) * LANES] = jnp.broadcast_to(part, (L, LANES))
        ring_surface[here, B:] = tail[L : 2 * L, 3 * T :]

    @pl.when(lat_even)
    def _():
        place(0, r2, t2)
        place(1, r1, t1)

    @pl.when(jnp.logical_not(lat_even))
    def _():
        place(0, r1, t1)
        place(1, r2, t2)

    south, north = ring_sum(z, layer_weight(ring[2], ring[3]))
    put_ring_sums(z, msg.at[:, z.W :], south, north)


def in_band(z, shape):
    lat = lax.axis_index("lat")
    row = lax.broadcasted_iota(jnp.int32, shape, 0)
    south = jnp.where(lat > 0, 1.0, 0.0)
    north = jnp.where(lat < z.n_lat - 1, 1.0, 0.0)
    return jnp.where(row < z.L, south, north)


def ring_geopot(z, h, t):
    w = layer_weight(h, t)
    row = row_iota(w)
    level = jnp.where(row < z.L, row, row - z.L)
    q = 0.5 * w
    for s in range(1, z.L):
        q = q + jnp.where(level < z.L - s, pltpu.roll(w, 2 * z.L - s, 0), 0.0)
    return q * in_band(z, w.shape)


def tendencies(coef, u, v, h, t, un, vs, hn, hs, tn, ts, q, qn, which="uvht"):
    zonal, cor, corn, north, south = coef
    out = {}
    if "u" in which:
        a = v + vs
        out["u"] = u + cor * (a + east(a)) - zonal * (east(q) - q)
    if "v" in which:
        b = u + un
        out["v"] = v - corn * (b + west(b)) - NORTH_COEF * (qn - q)
    if "h" in which:
        flux = u * (2.0 + h + east(h)) * 0.5
        out["h"] = (
            h
            - zonal * (flux - west(flux))
            - (north * (v * (2.0 + h + hn) * 0.5) - south * (vs * (2.0 + hs + h) * 0.5))
        )
    if "t" in which:
        out["t"] = (
            t
            - 0.25 * (u + west(u)) * zonal * (east(t) - west(t))
            - (0.25 * NORTH_COEF) * (v + vs) * (tn - ts)
        )
    return out


def advance_tile(z, geom, get, un_row, vs_row, h_ring, t_ring, q_ring, put, qput=None):
    coef = [wide(geom, k, 0, z.R, z.W) for k in range(5)]
    below = None
    for l in reversed(range(z.L)):
        u, v, h, t = (get(f, l) for f in range(4))
        w = layer_weight(h, t)
        q = 0.5 * w if below is None else below + 0.5 * w
        below = w if below is None else below + w
        s, n = l, z.L + l
        new = tendencies(
            coef, u, v, h, t,
            with_last(u, un_row(l)), with_first(v, vs_row(l)),
            with_last(h, h_ring[n : n + 1, :]), with_first(h, h_ring[s : s + 1, :]),
            with_last(t, t_ring[n : n + 1, :]), with_first(t, t_ring[s : s + 1, :]),
            q, with_last(q, q_ring[n : n + 1, :]),
        )
        for f, name in enumerate("uvht"):
            put(f, l, new[name])
        if qput is not None:
            qput(l, q)


def first_step(z, x, ring, geom, y, yring, inner, q_ring):
    L = z.L
    q_ring[...] = ring_geopot(z, ring[2], ring[3])

    def get(f, l):
        return x[f * L + l]

    def put(f, l, value):
        y[f * L + l] = value

    def qput(l, q):
        inner[3, l : l + 1, :] = q[0:1]

    inner[3, L:, :] = jnp.zeros((L, z.W), jnp.float32)
    advance_tile(
        z, geom, get,
        lambda l: ring[0, L + l : L + l + 1, :], lambda l: ring[1, l : l + 1, :],
        ring.at[2], ring.at[3], q_ring, put, qput,
    )
    for l in range(L):
        inner[0, l : l + 1, :] = x[l, 0:1, :]
        inner[0, L + l : L + l + 1, :] = x[L + l, z.R - 1 : z.R, :]
        for k, f in ((1, 2), (2, 3)):
            inner[k, l : l + 1, :] = x[f * L + l, 0:1, :]
            inner[k, L + l : L + l + 1, :] = x[f * L + l, z.R - 1 : z.R, :]
    south = lax.broadcasted_iota(jnp.int32, (2 * L, z.W), 0) < L
    coef = [wide(geom, k, z.R, z.R + 2 * L, z.W) for k in range(5)]
    u, v, h, t = (ring[k] for k in range(4))
    new = tendencies(
        coef, u, v, h, t,
        inner[0], jnp.where(south, ring[4], inner[0]),
        jnp.where(south, inner[1], ring[5]), jnp.where(south, ring[5], inner[1]),
        jnp.where(south, inner[2], ring[6]), jnp.where(south, ring[6], inner[2]),
        q_ring[...], inner[3],
    )
    mask = in_band(z, (2 * L, z.W))
    yring[0] = jnp.where(south, new["v"], new["u"]) * mask
    yring[1] = new["h"] * mask
    yring[2] = new["t"] * mask


def level_part(z, surface, ring_surface, below, ring_below):
    live = jnp.where(lax.axis_index("lev") < z.n_lev - 1, 1.0, 0.0)
    lat = lax.axis_index("lat")
    rows = []
    for d in range(2):
        there = jnp.where(lat > 0, 1.0, 0.0) if d == 0 else jnp.where(lat < z.n_lat - 1, 1.0, 0.0)
        parts = []
        for t in range(z.tiles):
            at = (d * z.extra + t // z.R) * LANES
            parts.append(ring_below[t % z.R : t % z.R + 1, at : at + LANES])
        sums = jnp.concatenate(parts, 1)
        rows.append(there * (ring_surface[d * z.L : d * z.L + 1, :] + live * sums))
    return surface + live * below, rows[0], rows[1]


def split(x):
    high = x.astype(jnp.bfloat16)
    return high, (x - high.astype(jnp.float32)).astype(jnp.bfloat16)


def dot(a, b, dims):
    return lax.dot_general(a, b, (dims, ((), ())), preferred_element_type=jnp.float32)


def product(x, wh, wl, dims):
    high, low = split(x)
    return dot(high, wh[...], dims) + dot(low, wh[...], dims) + dot(high, wl[...], dims)


def masked(z, x):
    tail = x[:, z.base :]
    lane = lax.broadcasted_iota(jnp.int32, tail.shape, 1)
    tail = jnp.where(lane < z.C - z.base, tail, 0.0)
    return jnp.concatenate([x[:, : z.base], tail], 1) if z.base else tail


def spectra(z, x, wh, wl, phase):
    s = product(x, wh, wl, ((1,), (0,)))
    a, b = s[:, :KMAX], s[:, KMAX:]
    c, d = phase[0:1, :], phase[1:2, :]
    return jnp.concatenate([a * c - b * d, a * d + b * c], 1)


def twice(x):
    return jnp.concatenate([x, x], 1)


def code_bit(code, k):
    return twice((code >> k) & 1) == 1


def compress(z, tile, code):
    for b in range(z.bits):
        tile = jnp.where(code_bit(code, b), pltpu.roll(tile, z.R - (1 << b), 0), tile)
    return tile


def expand(z, tile, code):
    for b in reversed(range(z.bits)):
        tile = jnp.where(code_bit(code, z.bits + b), pltpu.roll(tile, 1 << b, 0), tile)
    return tile


def pick_spectra(z, full, code, out):
    code = code[0 : z.R, :]
    row = lax.broadcasted_iota(jnp.int32, (z.R, 2 * KMAX), 0)
    for i in range(2 * z.L):
        a = compress(z, full[2 * i * z.R : (2 * i + 1) * z.R], code)
        b = compress(z, full[(2 * i + 1) * z.R : (2 * i + 2) * z.R], code)
        out[i * z.R : (i + 1) * z.R, :] = jnp.where(row < z.slots, a, pltpu.roll(b, z.slots, 0))


def tile_spectra(z, y, wh, wl, phase, code, out):
    x = masked(z, y[...].reshape(4 * z.L * z.R, z.W))
    pick_spectra(z, spectra(z, x, wh, wl, phase), code, out)


def tile_and_ring_spectra(z, y, yring, wh, wl, phase, code, out):
    m = 4 * z.L * z.R
    x = jnp.concatenate([y[...].reshape(m, z.W), yring[...].reshape(6 * z.L, z.W)], 0)
    full = spectra(z, masked(z, x), wh, wl, phase)
    pick_spectra(z, full, code, out)
    out[4 * z.L * z.slots :, :] = full[m:, :]


def pick_level_part(z, full, code):
    code = code[0 : z.R, :]
    row = lax.broadcasted_iota(jnp.int32, (z.R, 2 * KMAX), 0)
    a = compress(z, full[0 : z.R], code)
    b = compress(z, full[z.R : 2 * z.R], code)
    return jnp.where(row < z.slots, a, pltpu.roll(b, z.slots, 0))


def first_level_spectra(
    z, surface, ring_surface, got, part, part_got, geom, wh, wl, phase, code, sent, own, change, ring_change
):
    L = z.L
    g, gs, gn = level_part(z, surface[...], ring_surface, got[:, 0 : z.W], got[:, z.W :])
    du = wide(geom, 0, 0, z.R, z.W) * (east(g) - g)
    dv = NORTH_COEF * (with_last(g, gn) - g)
    shape = (2 * L, z.W)
    south = lax.broadcasted_iota(jnp.int32, shape, 0) < L
    gn = jnp.broadcast_to(gn, shape)
    du_north = wide(geom, 0, z.R, z.R + 2 * L, z.W) * (east(gn) - gn)
    dv_south = NORTH_COEF * jnp.broadcast_to(g[0:1] - gs, shape)
    ring = jnp.where(south, dv_south, du_north) * in_band(z, shape)
    change[0] = du
    change[1] = dv
    ring_change[...] = ring
    full = spectra(z, masked(z, jnp.concatenate([du, dv, ring], 0)), wh, wl, phase)
    own[0 : z.R, :] = pick_level_part(z, full, code)
    own[z.R :, :] = full[2 * z.R :]
    n = part.shape[0]
    sent[0:n, :] = part[...] + part_got[...]
    sent[n:, :] = own[...]


def second_level_spectra(
    z, surface, ring_surface, got, part, part_got, geom, wh, wl, phase, code, sent, own, change
):
    g, _, gn = level_part(z, surface[...], ring_surface, got[:, 0 : z.W], got[:, z.W :])
    du = wide(geom, 0, 0, z.R, z.W) * (east(g) - g)
    dv = NORTH_COEF * (with_last(g, gn) - g)
    change[0] = du
    change[1] = dv
    full = spectra(z, masked(z, jnp.concatenate([du, dv], 0)), wh, wl, phase)
    own[...] = pick_level_part(z, full, code)
    n = part.shape[0]
    sent[0:n, :] = part[...] + part_got[...]
    sent[n:, :] = own[...]


def total_modes(z, parts):
    if len(parts) == 2:
        return parts[0][...] + parts[1][...]
    mine, got, core, across = parts
    n = mine.shape[0] - core.shape[0]
    total = mine[0:n, :] + got[0:n, :]
    level = (mine[n:, :] + core[...]) + (got[n:, :] + across[...])
    both = level[0 : z.R]
    row = lax.broadcasted_iota(jnp.int32, both.shape, 0)
    other = pltpu.roll(both, z.slots, 0)
    du = jnp.where(row < z.slots, both, other)
    dv = jnp.where(row < z.slots, other, both)
    pairs = z.L // 2
    m = 4 * z.L * z.slots
    tiles = [total[i * z.R : (i + 1) * z.R] - (du if i < pairs else dv) for i in range(z.L)]
    tiles.append(total[z.L * z.R : m])
    if n > m:
        tiles += [total[m : m + 2 * z.L] - level[z.R :], total[m + 2 * z.L :]]
    return jnp.concatenate(tiles, 0)


def join(z, mine, got, core, across, out):
    out[...] = total_modes(z, (mine, got, core, across))


def mode_weight(z, keep):
    keep = twice(keep)
    k = lax.broadcasted_iota(jnp.int32, keep.shape, 1)
    k = jnp.where(k < KMAX, k, k - KMAX)
    scale = jnp.where(k == 0, 1.0 / z.N, 2.0 / z.N)
    return jnp.where(k < keep, scale, 0.0)


def keeps(z, code):
    keep = code[...] >> (2 * z.bits)
    return keep[0 : z.R], keep[z.R :]


def damping(z, keep, width):
    value = jnp.where(keep > 0, 1.0 - DAMPING, 0.0)
    return jnp.concatenate([value] * (width // LANES), 1)


def local_modes(total, phase):
    a, b = total[:, :KMAX], total[:, KMAX:]
    c, d = phase[0:1, :], phase[1:2, :]
    return jnp.concatenate([a * c + b * d, b * c - a * d], 1)


def tile_modes(z, modes, code, weight):
    code = code[0 : z.R, :]
    out = []
    for i in range(2 * z.L):
        pair = modes[i * z.R : (i + 1) * z.R]
        out.append(expand(z, pair, code) * weight)
        out.append(expand(z, pltpu.roll(pair, z.R - z.slots, 0), code) * weight)
    return out


def smooth(modes, wh, wl):
    return product(modes, wh, wl, ((1,), (0,)))


def filter_mass(z, *refs):
    parts, refs = refs[:-10], refs[-10:]
    state, sring, wh, wl, phase, code, ht, htring, uvmodes, msg = refs
    L, m = z.L, 4 * z.L * z.slots
    modes = local_modes(total_modes(z, parts), phase)
    keep, rkeep = keeps(z, code)
    weight, rweight = mode_weight(z, keep), mode_weight(z, rkeep)
    ring = [modes[m + k * 2 * L : m + (k + 1) * 2 * L] * rweight for k in range(3)]
    tiles = tile_modes(z, modes, code, weight)
    uvmodes[...] = jnp.concatenate(tiles[: 2 * L] + [ring[0]], 0)
    s = smooth(jnp.concatenate(tiles[2 * L :] + ring[1:], 0), wh, wl)
    damp, rdamp = damping(z, keep, z.W), damping(z, rkeep, z.W)
    for p in range(2 * L):
        x = state[2 * L + p]
        ht[p] = x + damp * (s[p * z.R : (p + 1) * z.R] - x)
    for k in range(2):
        x = sring[1 + k]
        at = 2 * L * z.R + k * 2 * L
        htring[k] = x + rdamp * (s[at : at + 2 * L] - x)
    total = layer_weight(ht[0], ht[L])
    for l in range(1, L):
        total = total + layer_weight(ht[l], ht[L + l])
    south, north = ring_sum(z, layer_weight(htring[0], htring[1]))
    msg[:, 0 : z.W] = total
    msg[:, z.W :] = jnp.zeros((z.R, 2 * z.extra * LANES), jnp.float32)
    put_ring_sums(z, msg.at[:, z.W :], south, north)


def second_step(z, state, sring, change, ring_change, uvmodes, ht, htring, geom, wh, wl, code, y, uv, uvring, q_ring):
    L = z.L
    m = 2 * L * z.R
    s = smooth(uvmodes[...], wh, wl)
    keep, rkeep = keeps(z, code)
    damp, rdamp = damping(z, keep, z.W), damping(z, rkeep, z.W)
    for p in range(2 * L):
        x = state[p] - change[p // L]
        uv[p] = x + damp * (s[p * z.R : (p + 1) * z.R] - x)
    x = sring[0] - ring_change[...]
    uvring[...] = x + rdamp * (s[m:] - x)
    q_ring[...] = ring_geopot(z, htring[0], htring[1])

    def get(f, l):
        return uv[f * L + l] if f < 2 else ht[(f - 2) * L + l]

    def put(f, l, value):
        y[f * L + l] = value

    advance_tile(
        z, geom, get,
        lambda l: uvring[L + l : L + l + 1, :], lambda l: uvring[l : l + 1, :],
        htring.at[0], htring.at[1], q_ring, put,
    )


def filter_all(z, *refs):
    parts, refs = refs[:-9], refs[-9:]
    state, change, wh, wl, phase, code, out, held, sem = refs
    L = z.L
    modes = local_modes(total_modes(z, parts), phase)
    keep, _ = keeps(z, code)
    high, low = split(jnp.concatenate(tile_modes(z, modes, code, mode_weight(z, keep)), 0))
    across = ((1,), (0,))
    copies = []
    for i, (lo, hi) in enumerate(z.chunks):
        top = min(-(-hi // LANES) * LANES, z.W)
        w, v = wh[:, lo:top], wl[:, lo:top]
        s = dot(high, w, across) + dot(low, w, across) + dot(high, v, across)
        d = damping(z, keep, top - lo)
        for p in range(4 * L):
            x = state[p, :, lo:top]
            if p < 2 * L:
                x = x - change[p // L, :, lo:top]
            new = x + d * (s[p * z.R : (p + 1) * z.R] - x)
            held[p // L, p % L, :, lo:hi] = new[:, : hi - lo]
        copies.append(
            pltpu.make_async_copy(held.at[:, :, :, lo:hi], out.at[:, :, :, lo:hi], sem.at[i])
        )
        copies[-1].start()
    for copy in copies:
        copy.wait()


def row_code(z, rows, counts, out):
    row = lax.broadcasted_iota(jnp.int32, (z.R + 2 * z.L, LANES), 0)
    lat = lax.axis_index("lat")
    code = jnp.zeros(row.shape, jnp.int32)
    for s in range(z.slots):
        at = rows[lat * z.slots + s] - lat * z.R
        far = at - s
        code = code + jnp.where(row == at, counts[lat * z.slots + s] << (2 * z.bits), 0)
        for b in range(z.bits):
            bit = (far >> b) & 1
            to = at - (bit << b)
            code = code + jnp.where((row == to) & (bit == 1), 1 << b, 0)
            code = code + jnp.where((row == at) & (bit == 1), 1 << (z.bits + b), 0)
            at = to
    before = jnp.maximum(lat * z.slots - 1, 0)
    after = jnp.minimum((lat + 1) * z.slots, z.filters - 1)
    south = jnp.where((lat > 0) & (rows[before] == lat * z.R - 1), counts[before], 0)
    north = jnp.where(
        (lat < z.n_lat - 1) & (rows[after] == (lat + 1) * z.R), counts[after], 0
    )
    ring = jnp.where(row < z.R + z.L, south, north) << (2 * z.bits)
    out[...] = jnp.where(row < z.R, code, ring)


def local(z, tables, fields, surface, filter_rows, keep_counts):
    L, R, W = z.L, z.R, z.W
    f32 = jnp.float32
    wave_high, wave_low, back_high, back_low = tables
    vmem = pl.BlockSpec(memory_space=pltpu.VMEM)

    def call(kernel, outs, ins, scratch=(), flops=1_000_000, aliases={}):
        size = sum(int(np.prod(s)) for s in outs) * 4 + sum(i.size * i.dtype.itemsize for i in ins)
        return pl.pallas_call(
            functools.partial(kernel, z),
            out_shape=[jax.ShapeDtypeStruct(s, f32) for s in outs],
            in_specs=[vmem] * len(ins),
            out_specs=[vmem] * len(outs),
            scratch_shapes=[pltpu.VMEM(s, f32) for s in scratch],
            input_output_aliases=aliases,
            compiler_params=pltpu.CompilerParams(vmem_limit_bytes=VMEM_LIMIT),
            cost_estimate=pl.CostEstimate(flops=flops, bytes_accessed=size, transcendentals=0),
            name=kernel.__name__,
        )(*ins)

    lat, lon = lax.axis_index("lat"), lax.axis_index("lon")
    index = lax.broadcasted_iota(jnp.int32, (R + 2 * L, LANES), 0)
    index = jnp.where(index < R, index, jnp.where(index < R + L, -1, R))
    based = (lat * R + index).astype(f32)
    to_radian = jnp.pi / 180.0
    middle = (FIRST_LAT + (based + 0.5) * ROW_STEP) * to_radian
    northern = (FIRST_LAT + (based + 1.0) * ROW_STEP) * to_radian
    southern = (FIRST_LAT + based * ROW_STEP) * to_radian
    cos_mid = jnp.cos(middle)
    geom = jnp.stack(
        [
            ZONAL_COEF / cos_mid,
            (0.25 * CORIOLIS) * jnp.sin(middle),
            (0.25 * CORIOLIS) * jnp.sin(northern),
            NORTH_COEF * jnp.cos(northern) / cos_mid,
            NORTH_COEF * jnp.cos(southern) / cos_mid,
        ]
    )
    turn = (lon * z.C * jnp.arange(KMAX, dtype=jnp.int32)) % z.N
    angle = turn.astype(f32) * (2.0 * jnp.pi / z.N)
    phase = jnp.stack([jnp.cos(angle), jnp.sin(angle)])

    smem = pl.BlockSpec(memory_space=pltpu.SMEM)
    code = pl.pallas_call(
        functools.partial(row_code, z),
        out_shape=jax.ShapeDtypeStruct((R + 2 * L, LANES), jnp.int32),
        in_specs=[smem] * 2,
        out_specs=vmem,
        name="row_code",
    )(filter_rows, keep_counts)

    lon_one = [(i, i ^ 1) for i in range(z.n_lon)]
    lon_two = [(i, (((i + 1) % z.n_lon ^ 1) - 1) % z.n_lon) for i in range(z.n_lon)]
    lat_one = [(i, i ^ 1) for i in range(z.n_lat) if i ^ 1 < z.n_lat]
    lat_two = [(i, ((i + 1) ^ 1) - 1) for i in range(1, z.n_lat) if ((i + 1) ^ 1) - 1 < z.n_lat]

    def from_below(column):
        if z.n_lev == 2:
            return lax.ppermute(column, "lev", [(0, 1), (1, 0)])
        place = lax.axis_index("lev")
        total = jnp.zeros_like(column)
        for s in range(1, z.n_lev):
            got = lax.ppermute(column, "lev", [(i, i - s) for i in range(s, z.n_lev)])
            total = total + jnp.where(place + s < z.n_lev, got, 0.0)
        return total

    def lon_swap(value, step):
        return lax.ppermute(value, "lon", [(i, i ^ step) for i in range(z.n_lon)])

    def over_lon(sent, own, rows):
        parts = [sent, lon_swap(sent, 2), lon_swap(own, 1), lon_swap(own, 3)]
        if z.n_lon == 4:
            return parts
        (part,) = call(join, [(rows, 2 * KMAX)], parts)
        got, step = lon_swap(part, 4), 8
        while step < z.n_lon:
            part = part + got
            got, step = lon_swap(part, step), step * 2
        return [part, got]

    tile = (R, LANES)
    x = jnp.concatenate([fields.reshape(4 * L, R, z.C), surface[None]], 0)
    x = jnp.pad(x, ((0, 0), (0, 0), (0, W - z.C)))
    m1, m2, after = call(edge_rows, [(R, z.lat_lanes)] * 2 + [tile], [x])
    m1 = lax.ppermute(m1, "lat", lat_one)
    m2 = lax.ppermute(m2, "lat", lat_two)
    e1, e2 = call(edge_columns, [tile, tile], [x, after])
    e1 = lax.ppermute(e1, "lon", lon_one)
    e2 = lax.ppermute(e2, "lon", lon_two)
    tails = (R, 4 * (W - z.base))
    x, sums, t1, t2 = call(
        widen,
        [(z.planes, R, W), (R, W), tails, tails],
        [x, e1, e2],
        [tile] * 2,
        aliases={0: 0},
    )
    t1 = lax.ppermute(t1, "lat", lat_one)
    t2 = lax.ppermute(t2, "lat", lat_two)
    ring_lanes = 2 * z.extra * LANES
    ring, ring_surface, msg = call(
        halo_rows, [(7, 2 * L, W), (2 * L, W), (R, W + ring_lanes)], [sums, m1, m2, t1, t2]
    )
    got = from_below(msg)
    y, yring = call(
        first_step,
        [(4 * L, R, W), (3, 2 * L, W)],
        [x, ring, geom],
        [(4, 2 * L, W), (2 * L, W)],
        flops=10_000_000,
    )
    waves = [wave_high, wave_low, phase, code]
    back = [back_high, back_low, phase, code]
    rows = 4 * L * z.slots
    (part,) = call(tile_and_ring_spectra, [(rows + 6 * L, 2 * KMAX)], [y, yring, *waves])
    surface_tile = x[4 * L]
    sent, own, change, ring_change = call(
        first_level_spectra,
        [(rows + 8 * L + R, 2 * KMAX), (2 * L + R, 2 * KMAX), (2, R, W), (2 * L, W)],
        [surface_tile, ring_surface, got, part, lon_swap(part, 1), geom, *waves],
    )
    parts = over_lon(sent, own, rows + 6 * L)
    ht, htring, uvmodes, msg = call(
        filter_mass,
        [(2 * L, R, W), (2, 2 * L, W), (2 * L * R + 2 * L, 2 * KMAX), (R, W + ring_lanes)],
        [*parts, y, yring, *back],
    )
    got = from_below(msg)
    (y,) = call(
        second_step,
        [(4 * L, R, W)],
        [y, yring, change, ring_change, uvmodes, ht, htring, geom, back_high, back_low, code],
        [(2 * L, R, W), (2 * L, W), (2 * L, W)],
        flops=10_000_000,
    )
    (part,) = call(tile_spectra, [(rows, 2 * KMAX)], [y, *waves])
    sent, own, change = call(
        second_level_spectra,
        [(rows + R, 2 * KMAX), (R, 2 * KMAX), (2, R, W)],
        [surface_tile, ring_surface, got, part, lon_swap(part, 1), geom, *waves],
    )
    parts = over_lon(sent, own, rows)
    return pl.pallas_call(
        functools.partial(filter_all, z),
        out_shape=jax.ShapeDtypeStruct((4, L, R, z.C), f32),
        in_specs=[vmem] * (len(parts) + 6),
        out_specs=pl.BlockSpec(memory_space=pl.ANY),
        scratch_shapes=[
            pltpu.VMEM((4, L, R, z.C), f32),
            pltpu.SemaphoreType.DMA((len(z.chunks),)),
        ],
        compiler_params=pltpu.CompilerParams(vmem_limit_bytes=VMEM_LIMIT),
        name="filter_all",
    )(*parts, y, change, *back)


def wave_tables(z):
    lane = np.arange(z.W)
    j = np.where(lane >= z.W - 2, lane - z.W, lane)
    angle = 2.0 * np.pi * ((j[:, None] * np.arange(KMAX)[None, :]) % z.N) / z.N
    table = np.concatenate([np.cos(angle), np.sin(angle)], 1).astype(np.float32)
    high = table.astype(ml_dtypes.bfloat16)
    low = (table - high.astype(np.float32)).astype(ml_dtypes.bfloat16)
    return high, low


def solution(mesh):
    def run(fields, surface, filter_rows, keep_counts):
        z = Sizes(mesh, fields.shape, filter_rows.shape[0])
        high, low = wave_tables(z)
        tables = [high, low, np.ascontiguousarray(high.T), np.ascontiguousarray(low.T)]

        def body(fields, surface, filter_rows, keep_counts):
            return local(
                z, [jnp.asarray(t) for t in tables], fields, surface, filter_rows, keep_counts
            )

        spec = P(None, "lev", "lat", "lon")
        return jax.shard_map(
            body,
            mesh=mesh,
            in_specs=(spec, P("lat", "lon"), P(), P()),
            out_specs=spec,
            check_vma=False,
        )(fields, surface, filter_rows, keep_counts)

    return run
```

```python
import functools

import jax
import jax.numpy as jnp
import ml_dtypes
import numpy as np
from jax import lax
from jax.experimental import pallas as pl
from jax.experimental.pallas import tpu as pltpu
from jax.sharding import PartitionSpec as P

KMAX = 128
GRAVITY_SCALE = 0.05
BUOYANCY = 0.5
CORIOLIS = 0.3
ZONAL_COEF = 0.08
NORTH_COEF = 0.2
DAMPING = 0.25
FIRST_LAT = -70.0
ROW_STEP = 0.05
LANES = 128
VMEM_LIMIT = 24 * 1024 * 1024


def layer_weight(h, t):
    return GRAVITY_SCALE * (1.0 + h) * (1.0 + BUOYANCY * t)


def east(x):
    return pltpu.roll(x, x.shape[1] - 1, 1)


def west(x):
    return pltpu.roll(x, 1, 1)


def rows_up(x):
    return pltpu.roll(x, x.shape[0] - 1, 0)


def rows_down(x):
    return pltpu.roll(x, 1, 0)


def row_iota(x):
    return lax.broadcasted_iota(jnp.int32, x.shape, 0)


def with_last(x, row):
    return jnp.where(row_iota(x) == x.shape[0] - 1, jnp.broadcast_to(row, x.shape), rows_up(x))


def with_first(x, row):
    return jnp.where(row_iota(x) == 0, jnp.broadcast_to(row, x.shape), rows_down(x))


def wide(geom, k, lo, hi, width):
    return jnp.concatenate([geom[k, lo:hi, :]] * (width // LANES), 1)


class Sizes:
    def __init__(self, mesh, fields_shape, filter_count):
        _, levels, rows, columns = fields_shape
        self.n_lon, self.n_lat, self.n_lev = (mesh.shape[a] for a in ("lon", "lat", "lev"))
        self.L = levels // self.n_lev
        self.R = rows // self.n_lat
        self.C = columns // self.n_lon
        self.N = columns
        self.W = -(-(self.C + 4) // LANES) * LANES
        self.slots = filter_count // self.n_lat
        self.filters = filter_count
        self.planes = 4 * self.L + 1
        self.base = (self.C - 1) // LANES * LANES
        self.tiles = self.W // LANES
        self.extra = -(-self.tiles // self.R)
        whole = self.base // LANES
        self.fold = -(-whole // 2)
        self.lat_lanes = 3 * self.base + (self.fold + -(-whole // self.R)) * LANES
        width = -(-self.base // LANES // 4) * LANES if self.base else self.W
        cuts = [c for c in range(0, self.base + 1, width)] if self.base else [0]
        if self.C - cuts[-1] <= LANES and len(cuts) > 1:
            cuts.pop()
        self.chunks = list(zip(cuts, cuts[1:] + [self.C]))
        self.bits = (self.R - self.slots).bit_length()
        assert self.R == 2 * self.slots and self.base > 0
        assert self.R == 2 * self.L and self.n_lon % 4 == 0 and self.L % 2 == 0
        assert 2 <= self.C - self.base <= LANES - 2 and 2 * self.planes <= LANES


def edge_tiles(z, count, head, tail, width):
    lane = lax.broadcasted_iota(jnp.int32, (z.R, LANES), 1)
    left = jnp.zeros((z.R, LANES), jnp.float32)
    right = left
    first = z.C - width - z.base
    for p in range(count):
        here = (lane >= width * p) & (lane < width * (p + 1))
        left = jnp.where(here, moved(head(p), width * p), left)
        right = jnp.where(here, moved(tail(p), width * p - first), right)
    return left, right


def moved(x, shift):
    shift = shift % x.shape[1]
    return pltpu.roll(x, shift, 1) if shift else x


def by_parity(axis, first, second, even, odd):
    is_even = lax.axis_index(axis) % 2 == 0

    @pl.when(is_even)
    def _():
        first[...] = even
        second[...] = odd

    @pl.when(jnp.logical_not(is_even))
    def _():
        first[...] = odd
        second[...] = even


def patch(z, ref, p, count, width, from_right, from_left):
    lane = lax.broadcasted_iota(jnp.int32, (z.R, LANES), 1)
    last = z.C - z.base
    right = moved(from_right, last - width * p)
    left = moved(from_left, LANES - width - width * p)
    for start in sorted({z.base, z.W - LANES}):
        tile = ref[:, start : start + LANES]
        if start == z.base:
            tile = jnp.where((lane >= last) & (lane < last + width), right, tile)
        if start == z.W - LANES:
            tile = jnp.where(lane >= LANES - width, left, tile)
        ref[:, start : start + LANES] = tile


def near_and_far(z):
    lat_even = lax.axis_index("lat") % 2 == 0
    near = jnp.where(lat_even, z.R - 1, 0)
    far = jnp.where(lat_even, z.R - 2, 1)
    return (near, far), (z.R - 1 - near, z.R - 1 - far)


def edge_rows(z, x, m1, m2, after):
    L, B = z.L, z.base
    fold = z.fold * LANES
    after[...] = jnp.zeros(after.shape, jnp.float32)
    for msg, (near, far) in zip((m1, m2), near_and_far(z)):
        msg[:, 3 * B :] = jnp.zeros((z.R, z.lat_lanes - 3 * B), jnp.float32)
        for k in range(7):
            f, at = (k, near) if k < 4 else (k - 3, far)
            for l in range(L):
                row = x[f * L + l, pl.ds(at, 1), 0:B]
                to = (k % 2) * L + l
                if k < 6:
                    msg[to : to + 1, k // 2 * B : (k // 2 + 1) * B] = row
                else:
                    msg[l : l + 1, 3 * B : 3 * B + fold] = row[:, 0:fold]
                    msg[L + l : L + l + 1, 3 * B : 4 * B - fold] = row[:, fold:]
        row = x[4 * L, pl.ds(near, 1), 0:B]
        for t in range(B // LANES):
            at = 3 * B + fold + t // z.R * LANES
            msg[t % z.R : t % z.R + 1, at : at + LANES] = row[:, t * LANES : (t + 1) * LANES]


def edge_columns(z, x, after, e1, e2):
    del after
    left, right = edge_tiles(
        z,
        z.planes,
        lambda p: x[p, :, 0:LANES],
        lambda p: x[p, :, z.base : z.base + LANES],
        2,
    )
    by_parity("lon", e1, e2, right, left)


def widen(z, x_in, r1, r2, x, sums, k1, k2, from_right, from_left):
    del x_in
    L, T = z.L, z.W - z.base
    by_parity("lon", from_right, from_left, r1[...], r2[...])
    right, left = from_right[...], from_left[...]
    for p in range(z.planes):
        patch(z, x.at[p], p, z.planes, 2, right, left)
    total = layer_weight(x[2 * L], x[3 * L])
    for l in range(1, L):
        total = total + layer_weight(x[2 * L + l], x[3 * L + l])
    sums[...] = total
    for msg, (near, far) in zip((k1, k2), near_and_far(z)):
        for k in range(8):
            f, at = (k, near) if k < 4 else (k - 3, far) if k < 7 else (4, near)
            for l in range(L):
                p = f * L + l if k < 7 else 4 * L
                to = (k % 2) * L + l
                msg[to : to + 1, k // 2 * T : (k // 2 + 1) * T] = x[p, pl.ds(at, 1), :][:, z.base :]


def put_ring_sums(z, msg, south, north):
    for d, row in enumerate((south, north)):
        for t in range(z.tiles):
            at = (d * z.extra + t // z.R) * LANES
            msg[t % z.R : t % z.R + 1, at : at + LANES] = row[:, t * LANES : (t + 1) * LANES]


def ring_sum(z, w):
    south = w[0:1]
    north = w[z.L : z.L + 1]
    for l in range(1, z.L):
        south = south + w[l : l + 1]
        north = north + w[z.L + l : z.L + l + 1]
    return south, north


def unfold(z, r1, r2, ring, ring_surface):
    lat_even = lax.axis_index("lat") % 2 == 0
    L, B = z.L, z.base
    fold = z.fold * LANES

    def place(d, source):
        here = slice(d * L, (d + 1) * L)
        for k in range(6):
            at = (k % 2) * L
            ring[k, here, 0:B] = source[at : at + L, k // 2 * B : (k // 2 + 1) * B]
        ring[6, here, 0:fold] = source[0:L, 3 * B : 3 * B + fold]
        ring[6, here, fold:B] = source[L : 2 * L, 3 * B : 4 * B - fold]
        for t in range(B // LANES):
            at = 3 * B + fold + t // z.R * LANES
            part = source[t % z.R : t % z.R + 1, at : at + LANES]
            ring_surface[here, t * LANES : (t + 1) * LANES] = jnp.broadcast_to(part, (L, LANES))

    @pl.when(lat_even)
    def _():
        place(0, r2)
        place(1, r1)

    @pl.when(jnp.logical_not(lat_even))
    def _():
        place(0, r1)
        place(1, r2)


def halo_rows(z, ring_in, surface_in, sums, t1, t2, ring, ring_surface, msg):
    del ring_in, surface_in
    lat_even = lax.axis_index("lat") % 2 == 0
    L, B, T = z.L, z.base, z.W - z.base
    msg[:, 0 : z.W] = sums[...]
    msg[:, z.W :] = jnp.zeros((z.R, 2 * z.extra * LANES), jnp.float32)

    def place(d, tail):
        here = slice(d * L, (d + 1) * L)
        for k in range(7):
            at = (k % 2) * L
            ring[k, here, B:] = tail[at : at + L, k // 2 * T : (k // 2 + 1) * T]
        ring_surface[here, B:] = tail[L : 2 * L, 3 * T :]

    @pl.when(lat_even)
    def _():
        place(0, t2)
        place(1, t1)

    @pl.when(jnp.logical_not(lat_even))
    def _():
        place(0, t1)
        place(1, t2)

    south, north = ring_sum(z, layer_weight(ring[2], ring[3]))
    put_ring_sums(z, msg.at[:, z.W :], south, north)


def in_band(z, shape):
    lat = lax.axis_index("lat")
    row = lax.broadcasted_iota(jnp.int32, shape, 0)
    south = jnp.where(lat > 0, 1.0, 0.0)
    north = jnp.where(lat < z.n_lat - 1, 1.0, 0.0)
    return jnp.where(row < z.L, south, north)


def ring_geopot(z, h, t):
    w = layer_weight(h, t)
    row = row_iota(w)
    level = jnp.where(row < z.L, row, row - z.L)
    q = 0.5 * w
    for s in range(1, z.L):
        q = q + jnp.where(level < z.L - s, pltpu.roll(w, 2 * z.L - s, 0), 0.0)
    return q * in_band(z, w.shape)


def tendencies(coef, u, v, h, t, un, vs, hn, hs, tn, ts, q, qn, which="uvht"):
    zonal, cor, corn, north, south = coef
    out = {}
    if "u" in which:
        a = v + vs
        out["u"] = u + cor * (a + east(a)) - zonal * (east(q) - q)
    if "v" in which:
        b = u + un
        out["v"] = v - corn * (b + west(b)) - NORTH_COEF * (qn - q)
    if "h" in which:
        flux = u * (2.0 + h + east(h)) * 0.5
        out["h"] = (
            h
            - zonal * (flux - west(flux))
            - (north * (v * (2.0 + h + hn) * 0.5) - south * (vs * (2.0 + hs + h) * 0.5))
        )
    if "t" in which:
        out["t"] = (
            t
            - 0.25 * (u + west(u)) * zonal * (east(t) - west(t))
            - (0.25 * NORTH_COEF) * (v + vs) * (tn - ts)
        )
    return out


def advance_tile(z, geom, get, un_row, vs_row, h_ring, t_ring, q_ring, put, qput=None):
    coef = [wide(geom, k, 0, z.R, z.W) for k in range(5)]
    below = None
    for l in reversed(range(z.L)):
        u, v, h, t = (get(f, l) for f in range(4))
        w = layer_weight(h, t)
        q = 0.5 * w if below is None else below + 0.5 * w
        below = w if below is None else below + w
        s, n = l, z.L + l
        new = tendencies(
            coef, u, v, h, t,
            with_last(u, un_row(l)), with_first(v, vs_row(l)),
            with_last(h, h_ring[n : n + 1, :]), with_first(h, h_ring[s : s + 1, :]),
            with_last(t, t_ring[n : n + 1, :]), with_first(t, t_ring[s : s + 1, :]),
            q, with_last(q, q_ring[n : n + 1, :]),
        )
        for f, name in enumerate("uvht"):
            put(f, l, new[name])
        if qput is not None:
            qput(l, q)


def first_step(z, x, ring, geom, y, yring, inner, q_ring):
    L = z.L
    q_ring[...] = ring_geopot(z, ring[2], ring[3])

    def get(f, l):
        return x[f * L + l]

    def put(f, l, value):
        y[f * L + l] = value

    def qput(l, q):
        inner[3, l : l + 1, :] = q[0:1]

    inner[3, L:, :] = jnp.zeros((L, z.W), jnp.float32)
    advance_tile(
        z, geom, get,
        lambda l: ring[0, L + l : L + l + 1, :], lambda l: ring[1, l : l + 1, :],
        ring.at[2], ring.at[3], q_ring, put, qput,
    )
    for l in range(L):
        inner[0, l : l + 1, :] = x[l, 0:1, :]
        inner[0, L + l : L + l + 1, :] = x[L + l, z.R - 1 : z.R, :]
        for k, f in ((1, 2), (2, 3)):
            inner[k, l : l + 1, :] = x[f * L + l, 0:1, :]
            inner[k, L + l : L + l + 1, :] = x[f * L + l, z.R - 1 : z.R, :]
    south = lax.broadcasted_iota(jnp.int32, (2 * L, z.W), 0) < L
    coef = [wide(geom, k, z.R, z.R + 2 * L, z.W) for k in range(5)]
    u, v, h, t = (ring[k] for k in range(4))
    new = tendencies(
        coef, u, v, h, t,
        inner[0], jnp.where(south, ring[4], inner[0]),
        jnp.where(south, inner[1], ring[5]), jnp.where(south, ring[5], inner[1]),
        jnp.where(south, inner[2], ring[6]), jnp.where(south, ring[6], inner[2]),
        q_ring[...], inner[3],
    )
    mask = in_band(z, (2 * L, z.W))
    yring[0] = jnp.where(south, new["v"], new["u"]) * mask
    yring[1] = new["h"] * mask
    yring[2] = new["t"] * mask


def level_part(z, surface, ring_surface, below, ring_below):
    live = jnp.where(lax.axis_index("lev") < z.n_lev - 1, 1.0, 0.0)
    lat = lax.axis_index("lat")
    rows = []
    for d in range(2):
        there = jnp.where(lat > 0, 1.0, 0.0) if d == 0 else jnp.where(lat < z.n_lat - 1, 1.0, 0.0)
        parts = []
        for t in range(z.tiles):
            at = (d * z.extra + t // z.R) * LANES
            parts.append(ring_below[t % z.R : t % z.R + 1, at : at + LANES])
        sums = jnp.concatenate(parts, 1)
        rows.append(there * (ring_surface[d * z.L : d * z.L + 1, :] + live * sums))
    return surface + live * below, rows[0], rows[1]


def dot(a, b, dims):
    return lax.dot_general(a, b, (dims, ((), ())), preferred_element_type=jnp.float32)


def product(x, wh, wl, dims):
    high = x.astype(jnp.bfloat16)
    wide = high.astype(jnp.float32)
    both = dot(jnp.concatenate([wide, x - wide], 0).astype(jnp.bfloat16), wh[...], dims)
    m = x.shape[0]
    return both[0:m] + both[m:] + dot(high, wl[...], dims)


def masked(z, x):
    tail = x[:, z.base :]
    lane = lax.broadcasted_iota(jnp.int32, tail.shape, 1)
    tail = jnp.where(lane < z.C - z.base, tail, 0.0)
    return jnp.concatenate([x[:, : z.base], tail], 1) if z.base else tail


def spectra(z, x, wh, wl, phase):
    s = product(x, wh, wl, ((1,), (0,)))
    a, b = s[:, :KMAX], s[:, KMAX:]
    c, d = phase[0:1, :], phase[1:2, :]
    return jnp.concatenate([a * c - b * d, a * d + b * c], 1)


def twice(x):
    return jnp.concatenate([x, x], 1)


def code_bit(code, k):
    return twice((code >> k) & 1) == 1


def compress(z, tile, code):
    for b in range(z.bits):
        tile = jnp.where(code_bit(code, b), pltpu.roll(tile, z.R - (1 << b), 0), tile)
    return tile


def expand(z, tile, code):
    for b in reversed(range(z.bits)):
        tile = jnp.where(code_bit(code, z.bits + b), pltpu.roll(tile, 1 << b, 0), tile)
    return tile


def pick_spectra(z, full, code, out):
    code = code[0 : z.R, :]
    row = lax.broadcasted_iota(jnp.int32, (z.R, 2 * KMAX), 0)
    for i in range(2 * z.L):
        a = compress(z, full[2 * i * z.R : (2 * i + 1) * z.R], code)
        b = compress(z, full[(2 * i + 1) * z.R : (2 * i + 2) * z.R], code)
        out[i * z.R : (i + 1) * z.R, :] = jnp.where(row < z.slots, a, pltpu.roll(b, z.slots, 0))


def tile_spectra(z, y, wh, wl, phase, code, out):
    x = masked(z, y[...].reshape(4 * z.L * z.R, z.W))
    pick_spectra(z, spectra(z, x, wh, wl, phase), code, out)


def tile_and_ring_spectra(z, y, yring, wh, wl, phase, code, out):
    m = 4 * z.L * z.R
    x = jnp.concatenate([y[...].reshape(m, z.W), yring[...].reshape(6 * z.L, z.W)], 0)
    full = spectra(z, masked(z, x), wh, wl, phase)
    pick_spectra(z, full, code, out)
    out[4 * z.L * z.slots :, :] = full[m:, :]


def pick_level_part(z, full, code):
    code = code[0 : z.R, :]
    row = lax.broadcasted_iota(jnp.int32, (z.R, 2 * KMAX), 0)
    a = compress(z, full[0 : z.R], code)
    b = compress(z, full[z.R : 2 * z.R], code)
    return jnp.where(row < z.slots, a, pltpu.roll(b, z.slots, 0))


def first_level_spectra(
    z, surface, ring_surface, got, part, part_got, geom, wh, wl, phase, code, sent, own, change, ring_change
):
    L = z.L
    g, gs, gn = level_part(z, surface[...], ring_surface, got[:, 0 : z.W], got[:, z.W :])
    du = wide(geom, 0, 0, z.R, z.W) * (east(g) - g)
    dv = NORTH_COEF * (with_last(g, gn) - g)
    shape = (2 * L, z.W)
    south = lax.broadcasted_iota(jnp.int32, shape, 0) < L
    gn = jnp.broadcast_to(gn, shape)
    du_north = wide(geom, 0, z.R, z.R + 2 * L, z.W) * (east(gn) - gn)
    dv_south = NORTH_COEF * jnp.broadcast_to(g[0:1] - gs, shape)
    ring = jnp.where(south, dv_south, du_north) * in_band(z, shape)
    change[0] = du
    change[1] = dv
    ring_change[...] = ring
    full = spectra(z, masked(z, jnp.concatenate([du, dv, ring], 0)), wh, wl, phase)
    own[0 : z.R, :] = pick_level_part(z, full, code)
    own[z.R :, :] = full[2 * z.R :]
    n = part.shape[0]
    sent[0:n, :] = part[...] + part_got[...]
    sent[n:, :] = own[...]


def second_level_spectra(
    z, surface, ring_surface, got, part, part_got, geom, wh, wl, phase, code, sent, own, change
):
    g, _, gn = level_part(z, surface[...], ring_surface, got[:, 0 : z.W], got[:, z.W :])
    du = wide(geom, 0, 0, z.R, z.W) * (east(g) - g)
    dv = NORTH_COEF * (with_last(g, gn) - g)
    change[0] = du
    change[1] = dv
    full = spectra(z, masked(z, jnp.concatenate([du, dv], 0)), wh, wl, phase)
    own[...] = pick_level_part(z, full, code)
    n = part.shape[0]
    sent[0:n, :] = part[...] + part_got[...]
    sent[n:, :] = own[...]


def total_modes(z, parts):
    if len(parts) == 2:
        return parts[0][...] + parts[1][...]
    mine, got, core, across = parts
    n = mine.shape[0] - core.shape[0]
    total = mine[0:n, :] + got[0:n, :]
    level = (mine[n:, :] + core[...]) + (got[n:, :] + across[...])
    both = level[0 : z.R]
    row = lax.broadcasted_iota(jnp.int32, both.shape, 0)
    other = pltpu.roll(both, z.slots, 0)
    du = jnp.where(row < z.slots, both, other)
    dv = jnp.where(row < z.slots, other, both)
    pairs = z.L // 2
    m = 4 * z.L * z.slots
    tiles = [total[i * z.R : (i + 1) * z.R] - (du if i < pairs else dv) for i in range(z.L)]
    tiles.append(total[z.L * z.R : m])
    if n > m:
        tiles += [total[m : m + 2 * z.L] - level[z.R :], total[m + 2 * z.L :]]
    return jnp.concatenate(tiles, 0)


def join(z, mine, got, core, across, out):
    out[...] = total_modes(z, (mine, got, core, across))


def mode_weight(z, keep):
    keep = twice(keep)
    k = lax.broadcasted_iota(jnp.int32, keep.shape, 1)
    k = jnp.where(k < KMAX, k, k - KMAX)
    scale = jnp.where(k == 0, 1.0 / z.N, 2.0 / z.N)
    return jnp.where(k < keep, scale, 0.0)


def keeps(z, code):
    keep = code[...] >> (2 * z.bits)
    return keep[0 : z.R], keep[z.R :]


def damping(z, keep, width):
    value = jnp.where(keep > 0, 1.0 - DAMPING, 0.0)
    return jnp.concatenate([value] * (width // LANES), 1)


def local_modes(total, phase):
    a, b = total[:, :KMAX], total[:, KMAX:]
    c, d = phase[0:1, :], phase[1:2, :]
    return jnp.concatenate([a * c + b * d, b * c - a * d], 1)


def tile_modes(z, modes, code, weight):
    code = code[0 : z.R, :]
    out = []
    for i in range(2 * z.L):
        pair = modes[i * z.R : (i + 1) * z.R]
        out.append(expand(z, pair, code) * weight)
        out.append(expand(z, pltpu.roll(pair, z.R - z.slots, 0), code) * weight)
    return out


def smooth(modes, wh, wl):
    return product(modes, wh, wl, ((1,), (0,)))


def filter_mass(z, *refs):
    parts, refs = refs[:-10], refs[-10:]
    state, sring, wh, wl, phase, code, ht, htring, uvmodes, msg = refs
    L, m = z.L, 4 * z.L * z.slots
    modes = local_modes(total_modes(z, parts), phase)
    keep, rkeep = keeps(z, code)
    weight, rweight = mode_weight(z, keep), mode_weight(z, rkeep)
    ring = [modes[m + k * 2 * L : m + (k + 1) * 2 * L] * rweight for k in range(3)]
    tiles = tile_modes(z, modes, code, weight)
    uvmodes[...] = jnp.concatenate(tiles[: 2 * L] + [ring[0]], 0)
    s = smooth(jnp.concatenate(tiles[2 * L :] + ring[1:], 0), wh, wl)
    damp, rdamp = damping(z, keep, z.W), damping(z, rkeep, z.W)
    for p in range(2 * L):
        x = state[2 * L + p]
        ht[p] = x + damp * (s[p * z.R : (p + 1) * z.R] - x)
    for k in range(2):
        x = sring[1 + k]
        at = 2 * L * z.R + k * 2 * L
        htring[k] = x + rdamp * (s[at : at + 2 * L] - x)
    total = layer_weight(ht[0], ht[L])
    for l in range(1, L):
        total = total + layer_weight(ht[l], ht[L + l])
    south, north = ring_sum(z, layer_weight(htring[0], htring[1]))
    msg[:, 0 : z.W] = total
    msg[:, z.W :] = jnp.zeros((z.R, 2 * z.extra * LANES), jnp.float32)
    put_ring_sums(z, msg.at[:, z.W :], south, north)


def second_step(z, state, sring, change, ring_change, uvmodes, ht, htring, geom, wh, wl, code, y, uv, uvring, q_ring):
    L = z.L
    m = 2 * L * z.R
    s = smooth(uvmodes[...], wh, wl)
    keep, rkeep = keeps(z, code)
    damp, rdamp = damping(z, keep, z.W), damping(z, rkeep, z.W)
    for p in range(2 * L):
        x = state[p] - change[p // L]
        uv[p] = x + damp * (s[p * z.R : (p + 1) * z.R] - x)
    x = sring[0] - ring_change[...]
    uvring[...] = x + rdamp * (s[m:] - x)
    q_ring[...] = ring_geopot(z, htring[0], htring[1])

    def get(f, l):
        return uv[f * L + l] if f < 2 else ht[(f - 2) * L + l]

    def put(f, l, value):
        y[f * L + l] = value

    advance_tile(
        z, geom, get,
        lambda l: uvring[L + l : L + l + 1, :], lambda l: uvring[l : l + 1, :],
        htring.at[0], htring.at[1], q_ring, put,
    )


def filter_all(z, *refs):
    parts, refs = refs[:-9], refs[-9:]
    state, change, wh, wl, phase, code, out, held, sem = refs
    L = z.L
    modes = local_modes(total_modes(z, parts), phase)
    keep, _ = keeps(z, code)
    modes = jnp.concatenate(tile_modes(z, modes, code, mode_weight(z, keep)), 0)
    high = modes.astype(jnp.bfloat16)
    wide_high = high.astype(jnp.float32)
    both = jnp.concatenate([wide_high, modes - wide_high], 0).astype(jnp.bfloat16)
    m = modes.shape[0]
    across = ((1,), (0,))
    copies = []
    for i, (lo, hi) in enumerate(z.chunks):
        top = min(-(-hi // LANES) * LANES, z.W)
        w, v = wh[:, lo:top], wl[:, lo:top]
        s = dot(both, w, across)
        s = s[0:m] + s[m:] + dot(high, v, across)
        d = damping(z, keep, top - lo)
        for p in range(4 * L):
            x = state[p, :, lo:top]
            if p < 2 * L:
                x = x - change[p // L, :, lo:top]
            new = x + d * (s[p * z.R : (p + 1) * z.R] - x)
            held[p // L, p % L, :, lo:hi] = new[:, : hi - lo]
        copies.append(
            pltpu.make_async_copy(held.at[:, :, :, lo:hi], out.at[:, :, :, lo:hi], sem.at[i])
        )
        copies[-1].start()
    for copy in copies:
        copy.wait()


def row_code(z, rows, counts, out):
    row = lax.broadcasted_iota(jnp.int32, (z.R + 2 * z.L, LANES), 0)
    lat = lax.axis_index("lat")
    code = jnp.zeros(row.shape, jnp.int32)
    for s in range(z.slots):
        at = rows[lat * z.slots + s] - lat * z.R
        far = at - s
        code = code + jnp.where(row == at, counts[lat * z.slots + s] << (2 * z.bits), 0)
        for b in range(z.bits):
            bit = (far >> b) & 1
            to = at - (bit << b)
            code = code + jnp.where((row == to) & (bit == 1), 1 << b, 0)
            code = code + jnp.where((row == at) & (bit == 1), 1 << (z.bits + b), 0)
            at = to
    before = jnp.maximum(lat * z.slots - 1, 0)
    after = jnp.minimum((lat + 1) * z.slots, z.filters - 1)
    south = jnp.where((lat > 0) & (rows[before] == lat * z.R - 1), counts[before], 0)
    north = jnp.where(
        (lat < z.n_lat - 1) & (rows[after] == (lat + 1) * z.R), counts[after], 0
    )
    ring = jnp.where(row < z.R + z.L, south, north) << (2 * z.bits)
    out[...] = jnp.where(row < z.R, code, ring)


def local(z, tables, fields, surface, filter_rows, keep_counts):
    L, R, W = z.L, z.R, z.W
    f32 = jnp.float32
    wave_high, wave_low, back_high, back_low = tables
    vmem = pl.BlockSpec(memory_space=pltpu.VMEM)

    def call(kernel, outs, ins, scratch=(), flops=1_000_000, aliases={}):
        size = sum(int(np.prod(s)) for s in outs) * 4 + sum(i.size * i.dtype.itemsize for i in ins)
        return pl.pallas_call(
            functools.partial(kernel, z),
            out_shape=[jax.ShapeDtypeStruct(s, f32) for s in outs],
            in_specs=[vmem] * len(ins),
            out_specs=[vmem] * len(outs),
            scratch_shapes=[pltpu.VMEM(s, f32) for s in scratch],
            input_output_aliases=aliases,
            compiler_params=pltpu.CompilerParams(vmem_limit_bytes=VMEM_LIMIT),
            cost_estimate=pl.CostEstimate(flops=flops, bytes_accessed=size, transcendentals=0),
            name=kernel.__name__,
        )(*ins)

    lat, lon = lax.axis_index("lat"), lax.axis_index("lon")
    index = lax.broadcasted_iota(jnp.int32, (R + 2 * L, LANES), 0)
    index = jnp.where(index < R, index, jnp.where(index < R + L, -1, R))
    based = (lat * R + index).astype(f32)
    to_radian = jnp.pi / 180.0
    middle = (FIRST_LAT + (based + 0.5) * ROW_STEP) * to_radian
    northern = (FIRST_LAT + (based + 1.0) * ROW_STEP) * to_radian
    southern = (FIRST_LAT + based * ROW_STEP) * to_radian
    cos_mid = jnp.cos(middle)
    geom = jnp.stack(
        [
            ZONAL_COEF / cos_mid,
            (0.25 * CORIOLIS) * jnp.sin(middle),
            (0.25 * CORIOLIS) * jnp.sin(northern),
            NORTH_COEF * jnp.cos(northern) / cos_mid,
            NORTH_COEF * jnp.cos(southern) / cos_mid,
        ]
    )
    turn = (lon * z.C * jnp.arange(KMAX, dtype=jnp.int32)) % z.N
    angle = turn.astype(f32) * (2.0 * jnp.pi / z.N)
    phase = jnp.stack([jnp.cos(angle), jnp.sin(angle)])

    smem = pl.BlockSpec(memory_space=pltpu.SMEM)
    code = pl.pallas_call(
        functools.partial(row_code, z),
        out_shape=jax.ShapeDtypeStruct((R + 2 * L, LANES), jnp.int32),
        in_specs=[smem] * 2,
        out_specs=vmem,
        name="row_code",
    )(filter_rows, keep_counts)

    lon_one = [(i, i ^ 1) for i in range(z.n_lon)]
    lon_two = [(i, (((i + 1) % z.n_lon ^ 1) - 1) % z.n_lon) for i in range(z.n_lon)]
    lat_one = [(i, i ^ 1) for i in range(z.n_lat) if i ^ 1 < z.n_lat]
    lat_two = [(i, ((i + 1) ^ 1) - 1) for i in range(1, z.n_lat) if ((i + 1) ^ 1) - 1 < z.n_lat]

    def from_below(column):
        if z.n_lev == 2:
            return lax.ppermute(column, "lev", [(0, 1), (1, 0)])
        place = lax.axis_index("lev")
        total = jnp.zeros_like(column)
        for s in range(1, z.n_lev):
            got = lax.ppermute(column, "lev", [(i, i - s) for i in range(s, z.n_lev)])
            total = total + jnp.where(place + s < z.n_lev, got, 0.0)
        return total

    def lon_swap(value, step):
        return lax.ppermute(value, "lon", [(i, i ^ step) for i in range(z.n_lon)])

    def over_lon(sent, own, rows):
        parts = [sent, lon_swap(sent, 2), lon_swap(own, 1), lon_swap(own, 3)]
        if z.n_lon == 4:
            return parts
        (part,) = call(join, [(rows, 2 * KMAX)], parts)
        got, step = lon_swap(part, 4), 8
        while step < z.n_lon:
            part = part + got
            got, step = lon_swap(part, step), step * 2
        return [part, got]

    tile = (R, LANES)
    x = jnp.concatenate([fields.reshape(4 * L, R, z.C), surface[None]], 0)
    x = jnp.pad(x, ((0, 0), (0, 0), (0, W - z.C)))
    m1, m2, after = call(edge_rows, [(R, z.lat_lanes)] * 2 + [tile], [x])
    m1 = lax.ppermute(m1, "lat", lat_one)
    m2 = lax.ppermute(m2, "lat", lat_two)
    e1, e2 = call(edge_columns, [tile, tile], [x, after])
    e1 = lax.ppermute(e1, "lon", lon_one)
    e2 = lax.ppermute(e2, "lon", lon_two)
    tails = (R, 4 * (W - z.base))
    x, sums, t1, t2 = call(
        widen,
        [(z.planes, R, W), (R, W), tails, tails],
        [x, e1, e2],
        [tile] * 2,
        aliases={0: 0},
    )
    t1 = lax.ppermute(t1, "lat", lat_one)
    t2 = lax.ppermute(t2, "lat", lat_two)
    ring_lanes = 2 * z.extra * LANES
    ring, ring_surface = call(unfold, [(7, 2 * L, W), (2 * L, W)], [m1, m2], flops=2_000_000)
    ring, ring_surface, msg = call(
        halo_rows,
        [(7, 2 * L, W), (2 * L, W), (R, W + ring_lanes)],
        [ring, ring_surface, sums, t1, t2],
        aliases={0: 0, 1: 1},
    )
    got = from_below(msg)
    y, yring = call(
        first_step,
        [(4 * L, R, W), (3, 2 * L, W)],
        [x, ring, geom],
        [(4, 2 * L, W), (2 * L, W)],
        flops=10_000_000,
    )
    waves = [wave_high, wave_low, phase, code]
    back = [back_high, back_low, phase, code]
    rows = 4 * L * z.slots
    (part,) = call(tile_and_ring_spectra, [(rows + 6 * L, 2 * KMAX)], [y, yring, *waves])
    surface_tile = x[4 * L]
    sent, own, change, ring_change = call(
        first_level_spectra,
        [(rows + 8 * L + R, 2 * KMAX), (2 * L + R, 2 * KMAX), (2, R, W), (2 * L, W)],
        [surface_tile, ring_surface, got, part, lon_swap(part, 1), geom, *waves],
    )
    parts = over_lon(sent, own, rows + 6 * L)
    ht, htring, uvmodes, msg = call(
        filter_mass,
        [(2 * L, R, W), (2, 2 * L, W), (2 * L * R + 2 * L, 2 * KMAX), (R, W + ring_lanes)],
        [*parts, y, yring, *back],
    )
    got = from_below(msg)
    (y,) = call(
        second_step,
        [(4 * L, R, W)],
        [y, yring, change, ring_change, uvmodes, ht, htring, geom, back_high, back_low, code],
        [(2 * L, R, W), (2 * L, W), (2 * L, W)],
        flops=10_000_000,
    )
    (part,) = call(tile_spectra, [(rows, 2 * KMAX)], [y, *waves])
    sent, own, change = call(
        second_level_spectra,
        [(rows + R, 2 * KMAX), (R, 2 * KMAX), (2, R, W)],
        [surface_tile, ring_surface, got, part, lon_swap(part, 1), geom, *waves],
    )
    parts = over_lon(sent, own, rows)
    return pl.pallas_call(
        functools.partial(filter_all, z),
        out_shape=jax.ShapeDtypeStruct((4, L, R, z.C), f32),
        in_specs=[vmem] * (len(parts) + 6),
        out_specs=pl.BlockSpec(memory_space=pl.ANY),
        scratch_shapes=[
            pltpu.VMEM((4, L, R, z.C), f32),
            pltpu.SemaphoreType.DMA((len(z.chunks),)),
        ],
        compiler_params=pltpu.CompilerParams(vmem_limit_bytes=VMEM_LIMIT),
        name="filter_all",
    )(*parts, y, change, *back)


def wave_tables(z):
    lane = np.arange(z.W)
    j = np.where(lane >= z.W - 2, lane - z.W, lane)
    angle = 2.0 * np.pi * ((j[:, None] * np.arange(KMAX)[None, :]) % z.N) / z.N
    table = np.concatenate([np.cos(angle), np.sin(angle)], 1).astype(np.float32)
    high = table.astype(ml_dtypes.bfloat16)
    low = (table - high.astype(np.float32)).astype(ml_dtypes.bfloat16)
    return high, low


def solution(mesh):
    def run(fields, surface, filter_rows, keep_counts):
        z = Sizes(mesh, fields.shape, filter_rows.shape[0])
        high, low = wave_tables(z)
        tables = [high, low, np.ascontiguousarray(high.T), np.ascontiguousarray(low.T)]

        def body(fields, surface, filter_rows, keep_counts):
            return local(
                z, [jnp.asarray(t) for t in tables], fields, surface, filter_rows, keep_counts
            )

        spec = P(None, "lev", "lat", "lon")
        return jax.shard_map(
            body,
            mesh=mesh,
            in_specs=(spec, P("lat", "lon"), P(), P()),
            out_specs=spec,
            check_vma=False,
        )(fields, surface, filter_rows, keep_counts)

    return run
```

```python
import functools

import jax
import jax.numpy as jnp
import ml_dtypes
import numpy as np
from jax import lax
from jax.experimental import pallas as pl
from jax.experimental.pallas import tpu as pltpu
from jax.sharding import PartitionSpec as P

KMAX = 128
GRAVITY_SCALE = 0.05
BUOYANCY = 0.5
CORIOLIS = 0.3
ZONAL_COEF = 0.08
NORTH_COEF = 0.2
DAMPING = 0.25
FIRST_LAT = -70.0
ROW_STEP = 0.05
LANES = 128
VMEM_LIMIT = 24 * 1024 * 1024


def layer_weight(h, t):
    return GRAVITY_SCALE * (1.0 + h) * (1.0 + BUOYANCY * t)


def east(x):
    return pltpu.roll(x, x.shape[1] - 1, 1)


def west(x):
    return pltpu.roll(x, 1, 1)


def rows_up(x):
    return pltpu.roll(x, x.shape[0] - 1, 0)


def rows_down(x):
    return pltpu.roll(x, 1, 0)


def row_iota(x):
    return lax.broadcasted_iota(jnp.int32, x.shape, 0)


def with_last(x, row):
    return jnp.where(row_iota(x) == x.shape[0] - 1, jnp.broadcast_to(row, x.shape), rows_up(x))


def with_first(x, row):
    return jnp.where(row_iota(x) == 0, jnp.broadcast_to(row, x.shape), rows_down(x))


def wide(geom, k, lo, hi, width):
    return jnp.concatenate([geom[k, lo:hi, :]] * (width // LANES), 1)


class Sizes:
    def __init__(self, mesh, fields_shape, filter_count):
        _, levels, rows, columns = fields_shape
        self.n_lon, self.n_lat, self.n_lev = (mesh.shape[a] for a in ("lon", "lat", "lev"))
        self.L = levels // self.n_lev
        self.R = rows // self.n_lat
        self.C = columns // self.n_lon
        self.N = columns
        self.W = -(-(self.C + 4) // LANES) * LANES
        self.slots = filter_count // self.n_lat
        self.filters = filter_count
        self.planes = 4 * self.L + 1
        self.base = (self.C - 1) // LANES * LANES
        self.tiles = self.W // LANES
        self.extra = -(-self.tiles // self.R)
        whole = self.base // LANES
        self.fold = -(-whole // 2)
        self.lat_lanes = 3 * self.base + (self.fold + -(-whole // self.R)) * LANES
        width = -(-self.base // LANES // 4) * LANES if self.base else self.W
        cuts = [c for c in range(0, self.base + 1, width)] if self.base else [0]
        if self.C - cuts[-1] <= LANES and len(cuts) > 1:
            cuts.pop()
        self.chunks = list(zip(cuts, cuts[1:] + [self.C]))
        self.bits = (self.R - self.slots).bit_length()
        assert self.R == 2 * self.slots and self.base > 0
        assert self.R == 2 * self.L and self.n_lon % 4 == 0 and self.L % 2 == 0
        assert 2 <= self.C - self.base <= LANES - 2 and 2 * self.planes <= LANES


def edge_tiles(z, count, head, tail, width):
    lane = lax.broadcasted_iota(jnp.int32, (z.R, LANES), 1)
    left = jnp.zeros((z.R, LANES), jnp.float32)
    right = left
    first = z.C - width - z.base
    for p in range(count):
        here = (lane >= width * p) & (lane < width * (p + 1))
        left = jnp.where(here, moved(head(p), width * p), left)
        right = jnp.where(here, moved(tail(p), width * p - first), right)
    return left, right


def moved(x, shift):
    shift = shift % x.shape[1]
    return pltpu.roll(x, shift, 1) if shift else x


def by_parity(axis, first, second, even, odd):
    is_even = lax.axis_index(axis) % 2 == 0

    @pl.when(is_even)
    def _():
        first[...] = even
        second[...] = odd

    @pl.when(jnp.logical_not(is_even))
    def _():
        first[...] = odd
        second[...] = even


def patch(z, ref, p, count, width, from_right, from_left):
    lane = lax.broadcasted_iota(jnp.int32, (z.R, LANES), 1)
    last = z.C - z.base
    right = moved(from_right, last - width * p)
    left = moved(from_left, LANES - width - width * p)
    for start in sorted({z.base, z.W - LANES}):
        tile = ref[:, start : start + LANES]
        if start == z.base:
            tile = jnp.where((lane >= last) & (lane < last + width), right, tile)
        if start == z.W - LANES:
            tile = jnp.where(lane >= LANES - width, left, tile)
        ref[:, start : start + LANES] = tile


def near_and_far(z):
    lat_odd = lax.axis_index("lat") % 2 == 1
    near = jnp.where(lat_odd, z.R - 1, 0)
    far = jnp.where(lat_odd, z.R - 2, 1)
    return (near, far), (z.R - 1 - near, z.R - 1 - far)


def edge_rows(z, x, m1, m2, after):
    L, B = z.L, z.base
    fold = z.fold * LANES
    after[...] = jnp.zeros(after.shape, jnp.float32)
    for msg, (near, far) in zip((m1, m2), near_and_far(z)):
        msg[:, 3 * B :] = jnp.zeros((z.R, z.lat_lanes - 3 * B), jnp.float32)
        for k in range(7):
            f, at = (k, near) if k < 4 else (k - 3, far)
            for l in range(L):
                row = x[f * L + l, pl.ds(at, 1), 0:B]
                to = (k % 2) * L + l
                if k < 6:
                    msg[to : to + 1, k // 2 * B : (k // 2 + 1) * B] = row
                else:
                    msg[l : l + 1, 3 * B : 3 * B + fold] = row[:, 0:fold]
                    msg[L + l : L + l + 1, 3 * B : 4 * B - fold] = row[:, fold:]
        row = x[4 * L, pl.ds(near, 1), 0:B]
        for t in range(B // LANES):
            at = 3 * B + fold + t // z.R * LANES
            msg[t % z.R : t % z.R + 1, at : at + LANES] = row[:, t * LANES : (t + 1) * LANES]


def edge_columns(z, x, after, e1, e2):
    del after
    left, right = edge_tiles(
        z,
        z.planes,
        lambda p: x[p, :, 0:LANES],
        lambda p: x[p, :, z.base : z.base + LANES],
        2,
    )
    by_parity("lon", e1, e2, right, left)


def widen(z, x_in, r1, r2, x, sums, k1, k2, from_right, from_left):
    del x_in
    L, T = z.L, z.W - z.base
    by_parity("lon", from_right, from_left, r1[...], r2[...])
    right, left = from_right[...], from_left[...]
    for p in range(z.planes):
        patch(z, x.at[p], p, z.planes, 2, right, left)
    total = layer_weight(x[2 * L], x[3 * L])
    for l in range(1, L):
        total = total + layer_weight(x[2 * L + l], x[3 * L + l])
    sums[...] = total
    for msg, (near, far) in zip((k1, k2), near_and_far(z)):
        for k in range(8):
            f, at = (k, near) if k < 4 else (k - 3, far) if k < 7 else (4, near)
            for l in range(L):
                p = f * L + l if k < 7 else 4 * L
                to = (k % 2) * L + l
                msg[to : to + 1, k // 2 * T : (k // 2 + 1) * T] = x[p, pl.ds(at, 1), :][:, z.base :]


def put_ring_sums(z, msg, *rows):
    for d, row in enumerate(rows):
        for t in range(z.tiles):
            at = (d * z.extra + t // z.R) * LANES
            msg[t % z.R : t % z.R + 1, at : at + LANES] = row[:, t * LANES : (t + 1) * LANES]


def ring_sum(z, w):
    south = w[0:1]
    north = w[z.L : z.L + 1]
    for l in range(1, z.L):
        south = south + w[l : l + 1]
        north = north + w[z.L + l : z.L + l + 1]
    return south, north


def unfold(z, r1, r2, ring, ring_surface):
    lat_odd = lax.axis_index("lat") % 2 == 1
    L, B = z.L, z.base
    fold = z.fold * LANES

    def place(d, source):
        here = slice(d * L, (d + 1) * L)
        for k in range(6):
            at = (k % 2) * L
            ring[k, here, 0:B] = source[at : at + L, k // 2 * B : (k // 2 + 1) * B]
        ring[6, here, 0:fold] = source[0:L, 3 * B : 3 * B + fold]
        ring[6, here, fold:B] = source[L : 2 * L, 3 * B : 4 * B - fold]
        for t in range(B // LANES):
            at = 3 * B + fold + t // z.R * LANES
            part = source[t % z.R : t % z.R + 1, at : at + LANES]
            ring_surface[here, t * LANES : (t + 1) * LANES] = jnp.broadcast_to(part, (L, LANES))

    @pl.when(lat_odd)
    def _():
        place(0, r2)
        place(1, r1)

    @pl.when(jnp.logical_not(lat_odd))
    def _():
        place(0, r1)
        place(1, r2)


def halo_rows(z, ring_in, surface_in, sums, t1, t2, ring, ring_surface, msg):
    del ring_in, surface_in
    lat_odd = lax.axis_index("lat") % 2 == 1
    L, B, T = z.L, z.base, z.W - z.base
    msg[:, 0 : z.W] = sums[...]
    msg[:, z.W :] = jnp.zeros((z.R, 2 * z.extra * LANES), jnp.float32)

    def place(d, tail):
        here = slice(d * L, (d + 1) * L)
        for k in range(7):
            at = (k % 2) * L
            ring[k, here, B:] = tail[at : at + L, k // 2 * T : (k // 2 + 1) * T]
        ring_surface[here, B:] = tail[L : 2 * L, 3 * T :]

    @pl.when(lat_odd)
    def _():
        place(0, t2)
        place(1, t1)

    @pl.when(jnp.logical_not(lat_odd))
    def _():
        place(0, t1)
        place(1, t2)

    south, north = ring_sum(z, layer_weight(ring[2], ring[3]))
    put_ring_sums(z, msg.at[:, z.W :], north, south)


def in_band(z, shape):
    lat = lax.axis_index("lat")
    row = lax.broadcasted_iota(jnp.int32, shape, 0)
    south = jnp.where(lat > 0, 1.0, 0.0)
    north = jnp.where(lat < z.n_lat - 1, 1.0, 0.0)
    return jnp.where(row < z.L, south, north)


def ring_geopot(z, h, t):
    w = layer_weight(h, t)
    row = row_iota(w)
    level = jnp.where(row < z.L, row, row - z.L)
    q = 0.5 * w
    for s in range(1, z.L):
        q = q + jnp.where(level < z.L - s, pltpu.roll(w, 2 * z.L - s, 0), 0.0)
    return q * in_band(z, w.shape)


def tendencies(coef, u, v, h, t, un, vs, hn, hs, tn, ts, q, qn, which="uvht"):
    zonal, cor, corn, north, south = coef
    out = {}
    if "u" in which:
        a = v + vs
        out["u"] = u + cor * (a + east(a)) - zonal * (east(q) - q)
    if "v" in which:
        b = u + un
        out["v"] = v - corn * (b + west(b)) - NORTH_COEF * (qn - q)
    if "h" in which:
        flux = u * (2.0 + h + east(h)) * 0.5
        out["h"] = (
            h
            - zonal * (flux - west(flux))
            - (north * (v * (2.0 + h + hn) * 0.5) - south * (vs * (2.0 + hs + h) * 0.5))
        )
    if "t" in which:
        out["t"] = (
            t
            - 0.25 * (u + west(u)) * zonal * (east(t) - west(t))
            - (0.25 * NORTH_COEF) * (v + vs) * (tn - ts)
        )
    return out


def advance_tile(z, geom, get, un_row, vs_row, h_ring, t_ring, q_ring, put, qput=None):
    coef = [wide(geom, k, 0, z.R, z.W) for k in range(5)]
    below = None
    for l in reversed(range(z.L)):
        u, v, h, t = (get(f, l) for f in range(4))
        w = layer_weight(h, t)
        q = 0.5 * w if below is None else below + 0.5 * w
        below = w if below is None else below + w
        s, n = l, z.L + l
        new = tendencies(
            coef, u, v, h, t,
            with_last(u, un_row(l)), with_first(v, vs_row(l)),
            with_last(h, h_ring[n : n + 1, :]), with_first(h, h_ring[s : s + 1, :]),
            with_last(t, t_ring[n : n + 1, :]), with_first(t, t_ring[s : s + 1, :]),
            q, with_last(q, q_ring[n : n + 1, :]),
        )
        for f, name in enumerate("uvht"):
            put(f, l, new[name])
        if qput is not None:
            qput(l, q)


def first_step(z, x, ring, geom, y, yring, inner, q_ring):
    L = z.L
    q_ring[...] = ring_geopot(z, ring[2], ring[3])

    def get(f, l):
        return x[f * L + l]

    def put(f, l, value):
        y[f * L + l] = value

    def qput(l, q):
        inner[3, l : l + 1, :] = q[0:1]

    inner[3, L:, :] = jnp.zeros((L, z.W), jnp.float32)
    advance_tile(
        z, geom, get,
        lambda l: ring[0, L + l : L + l + 1, :], lambda l: ring[1, l : l + 1, :],
        ring.at[2], ring.at[3], q_ring, put, qput,
    )
    for l in range(L):
        inner[0, l : l + 1, :] = x[l, 0:1, :]
        inner[0, L + l : L + l + 1, :] = x[L + l, z.R - 1 : z.R, :]
        for k, f in ((1, 2), (2, 3)):
            inner[k, l : l + 1, :] = x[f * L + l, 0:1, :]
            inner[k, L + l : L + l + 1, :] = x[f * L + l, z.R - 1 : z.R, :]
    south = lax.broadcasted_iota(jnp.int32, (2 * L, z.W), 0) < L
    coef = [wide(geom, k, z.R, z.R + 2 * L, z.W) for k in range(5)]
    u, v, h, t = (ring[k] for k in range(4))
    new = tendencies(
        coef, u, v, h, t,
        inner[0], jnp.where(south, ring[4], inner[0]),
        jnp.where(south, inner[1], ring[5]), jnp.where(south, ring[5], inner[1]),
        jnp.where(south, inner[2], ring[6]), jnp.where(south, ring[6], inner[2]),
        q_ring[...], inner[3],
    )
    mask = in_band(z, (2 * L, z.W))
    yring[0] = jnp.where(south, new["v"], new["u"]) * mask
    yring[1] = new["h"] * mask
    yring[2] = new["t"] * mask


def level_part(z, surface, ring_surface, got):
    live = jnp.where(lax.axis_index("lev") < z.n_lev - 1, 1.0, 0.0)
    lat = lax.axis_index("lat")
    out = [surface + live * got[:, 0 : z.W]]
    for d in range((got.shape[1] - z.W) // (z.extra * LANES)):
        inside = lat < z.n_lat - 1 if d == 0 else lat > 0
        parts = []
        for t in range(z.tiles):
            at = z.W + (d * z.extra + t // z.R) * LANES
            parts.append(got[t % z.R : t % z.R + 1, at : at + LANES])
        sums = jnp.concatenate(parts, 1)
        row = (1 - d) * z.L
        out.append(jnp.where(inside, 1.0, 0.0) * (ring_surface[row : row + 1, :] + live * sums))
    return out


def dot(a, b, dims):
    return lax.dot_general(a, b, (dims, ((), ())), preferred_element_type=jnp.float32)


def product(x, wh, wl, dims):
    high = x.astype(jnp.bfloat16)
    wide = high.astype(jnp.float32)
    both = dot(jnp.concatenate([wide, x - wide], 0).astype(jnp.bfloat16), wh[...], dims)
    m = x.shape[0]
    return both[0:m] + both[m:] + dot(high, wl[...], dims)


def masked(z, x):
    tail = x[:, z.base :]
    lane = lax.broadcasted_iota(jnp.int32, tail.shape, 1)
    tail = jnp.where(lane < z.C - z.base, tail, 0.0)
    return jnp.concatenate([x[:, : z.base], tail], 1) if z.base else tail


def spectra(z, x, wh, wl, phase):
    s = product(x, wh, wl, ((1,), (0,)))
    a, b = s[:, :KMAX], s[:, KMAX:]
    c, d = phase[0:1, :], phase[1:2, :]
    return jnp.concatenate([a * c - b * d, a * d + b * c], 1)


def twice(x):
    return jnp.concatenate([x, x], 1)


def code_bit(code, k):
    return twice((code >> k) & 1) == 1


def compress(z, tile, code):
    for b in range(z.bits):
        tile = jnp.where(code_bit(code, b), pltpu.roll(tile, z.R - (1 << b), 0), tile)
    return tile


def expand(z, tile, code):
    for b in reversed(range(z.bits)):
        tile = jnp.where(code_bit(code, z.bits + b), pltpu.roll(tile, 1 << b, 0), tile)
    return tile


def pick_spectra(z, full, code, out):
    code = code[0 : z.R, :]
    row = lax.broadcasted_iota(jnp.int32, (z.R, 2 * KMAX), 0)
    for i in range(2 * z.L):
        a = compress(z, full[2 * i * z.R : (2 * i + 1) * z.R], code)
        b = compress(z, full[(2 * i + 1) * z.R : (2 * i + 2) * z.R], code)
        out[i * z.R : (i + 1) * z.R, :] = jnp.where(row < z.slots, a, pltpu.roll(b, z.slots, 0))


def tile_spectra(z, y, wh, wl, phase, code, out):
    x = masked(z, y[...].reshape(4 * z.L * z.R, z.W))
    pick_spectra(z, spectra(z, x, wh, wl, phase), code, out)


def tile_and_ring_spectra(z, y, yring, wh, wl, phase, code, out):
    m = 4 * z.L * z.R
    x = jnp.concatenate([y[...].reshape(m, z.W), yring[...].reshape(6 * z.L, z.W)], 0)
    full = spectra(z, masked(z, x), wh, wl, phase)
    pick_spectra(z, full, code, out)
    out[4 * z.L * z.slots :, :] = full[m:, :]


def pick_level_part(z, full, code):
    code = code[0 : z.R, :]
    row = lax.broadcasted_iota(jnp.int32, (z.R, 2 * KMAX), 0)
    a = compress(z, full[0 : z.R], code)
    b = compress(z, full[z.R : 2 * z.R], code)
    return jnp.where(row < z.slots, a, pltpu.roll(b, z.slots, 0))


def first_level_spectra(
    z, surface, ring_surface, got, part, part_got, geom, wh, wl, phase, code, sent, own, change, ring_change
):
    L = z.L
    g, gn, gs = level_part(z, surface[...], ring_surface, got)
    du = wide(geom, 0, 0, z.R, z.W) * (east(g) - g)
    dv = NORTH_COEF * (with_last(g, gn) - g)
    shape = (2 * L, z.W)
    south = lax.broadcasted_iota(jnp.int32, shape, 0) < L
    gn = jnp.broadcast_to(gn, shape)
    du_north = wide(geom, 0, z.R, z.R + 2 * L, z.W) * (east(gn) - gn)
    dv_south = NORTH_COEF * jnp.broadcast_to(g[0:1] - gs, shape)
    ring = jnp.where(south, dv_south, du_north) * in_band(z, shape)
    change[0] = du
    change[1] = dv
    ring_change[...] = ring
    full = spectra(z, masked(z, jnp.concatenate([du, dv, ring], 0)), wh, wl, phase)
    own[0 : z.R, :] = pick_level_part(z, full, code)
    own[z.R :, :] = full[2 * z.R :]
    n = part.shape[0]
    sent[0:n, :] = part[...] + part_got[...]
    sent[n:, :] = own[...]


def second_level_spectra(
    z, surface, ring_surface, got, part, part_got, geom, wh, wl, phase, code, sent, own, change
):
    g, gn = level_part(z, surface[...], ring_surface, got)
    du = wide(geom, 0, 0, z.R, z.W) * (east(g) - g)
    dv = NORTH_COEF * (with_last(g, gn) - g)
    change[0] = du
    change[1] = dv
    full = spectra(z, masked(z, jnp.concatenate([du, dv], 0)), wh, wl, phase)
    own[...] = pick_level_part(z, full, code)
    n = part.shape[0]
    sent[0:n, :] = part[...] + part_got[...]
    sent[n:, :] = own[...]


def total_modes(z, parts):
    if len(parts) == 2:
        return parts[0][...] + parts[1][...]
    mine, got, core, across = parts
    n = mine.shape[0] - core.shape[0]
    total = mine[0:n, :] + got[0:n, :]
    level = (mine[n:, :] + core[...]) + (got[n:, :] + across[...])
    both = level[0 : z.R]
    row = lax.broadcasted_iota(jnp.int32, both.shape, 0)
    other = pltpu.roll(both, z.slots, 0)
    du = jnp.where(row < z.slots, both, other)
    dv = jnp.where(row < z.slots, other, both)
    pairs = z.L // 2
    m = 4 * z.L * z.slots
    tiles = [total[i * z.R : (i + 1) * z.R] - (du if i < pairs else dv) for i in range(z.L)]
    tiles.append(total[z.L * z.R : m])
    if n > m:
        tiles += [total[m : m + 2 * z.L] - level[z.R :], total[m + 2 * z.L :]]
    return jnp.concatenate(tiles, 0)


def join(z, mine, got, core, across, out):
    out[...] = total_modes(z, (mine, got, core, across))


def mode_weight(z, keep):
    keep = twice(keep)
    k = lax.broadcasted_iota(jnp.int32, keep.shape, 1)
    k = jnp.where(k < KMAX, k, k - KMAX)
    scale = jnp.where(k == 0, 1.0 / z.N, 2.0 / z.N)
    return jnp.where(k < keep, scale, 0.0)


def keeps(z, code):
    keep = code[...] >> (2 * z.bits)
    return keep[0 : z.R], keep[z.R :]


def damping(z, keep, width):
    value = jnp.where(keep > 0, 1.0 - DAMPING, 0.0)
    return jnp.concatenate([value] * (width // LANES), 1)


def local_modes(total, phase):
    a, b = total[:, :KMAX], total[:, KMAX:]
    c, d = phase[0:1, :], phase[1:2, :]
    return jnp.concatenate([a * c + b * d, b * c - a * d], 1)


def tile_modes(z, modes, code, weight):
    code = code[0 : z.R, :]
    out = []
    for i in range(2 * z.L):
        pair = modes[i * z.R : (i + 1) * z.R]
        out.append(expand(z, pair, code) * weight)
        out.append(expand(z, pltpu.roll(pair, z.R - z.slots, 0), code) * weight)
    return out


def smooth(modes, wh, wl):
    return product(modes, wh, wl, ((1,), (0,)))


def filter_mass(z, *refs):
    parts, refs = refs[:-10], refs[-10:]
    state, sring, wh, wl, phase, code, ht, htring, uvmodes, msg = refs
    L, m = z.L, 4 * z.L * z.slots
    modes = local_modes(total_modes(z, parts), phase)
    keep, rkeep = keeps(z, code)
    weight, rweight = mode_weight(z, keep), mode_weight(z, rkeep)
    ring = [modes[m + k * 2 * L : m + (k + 1) * 2 * L] * rweight for k in range(3)]
    tiles = tile_modes(z, modes, code, weight)
    uvmodes[...] = jnp.concatenate(tiles[: 2 * L] + [ring[0]], 0)
    s = smooth(jnp.concatenate(tiles[2 * L :] + ring[1:], 0), wh, wl)
    damp, rdamp = damping(z, keep, z.W), damping(z, rkeep, z.W)
    for p in range(2 * L):
        x = state[2 * L + p]
        ht[p] = x + damp * (s[p * z.R : (p + 1) * z.R] - x)
    for k in range(2):
        x = sring[1 + k]
        at = 2 * L * z.R + k * 2 * L
        htring[k] = x + rdamp * (s[at : at + 2 * L] - x)
    total = layer_weight(ht[0], ht[L])
    for l in range(1, L):
        total = total + layer_weight(ht[l], ht[L + l])
    _, north = ring_sum(z, layer_weight(htring[0], htring[1]))
    msg[:, 0 : z.W] = total
    msg[:, z.W :] = jnp.zeros((z.R, z.extra * LANES), jnp.float32)
    put_ring_sums(z, msg.at[:, z.W :], north)


def second_step(z, state, sring, change, ring_change, uvmodes, ht, htring, geom, wh, wl, code, y, uv, uvring, q_ring):
    L = z.L
    m = 2 * L * z.R
    s = smooth(uvmodes[...], wh, wl)
    keep, rkeep = keeps(z, code)
    damp, rdamp = damping(z, keep, z.W), damping(z, rkeep, z.W)
    for p in range(2 * L):
        x = state[p] - change[p // L]
        uv[p] = x + damp * (s[p * z.R : (p + 1) * z.R] - x)
    x = sring[0] - ring_change[...]
    uvring[...] = x + rdamp * (s[m:] - x)
    q_ring[...] = ring_geopot(z, htring[0], htring[1])

    def get(f, l):
        return uv[f * L + l] if f < 2 else ht[(f - 2) * L + l]

    def put(f, l, value):
        y[f * L + l] = value

    advance_tile(
        z, geom, get,
        lambda l: uvring[L + l : L + l + 1, :], lambda l: uvring[l : l + 1, :],
        htring.at[0], htring.at[1], q_ring, put,
    )


def filter_all(z, *refs):
    parts, refs = refs[:-9], refs[-9:]
    state, change, wh, wl, phase, code, out, held, sem = refs
    L = z.L
    modes = local_modes(total_modes(z, parts), phase)
    keep, _ = keeps(z, code)
    modes = jnp.concatenate(tile_modes(z, modes, code, mode_weight(z, keep)), 0)
    high = modes.astype(jnp.bfloat16)
    wide_high = high.astype(jnp.float32)
    both = jnp.concatenate([wide_high, modes - wide_high], 0).astype(jnp.bfloat16)
    m = modes.shape[0]
    across = ((1,), (0,))
    copies = []
    for i, (lo, hi) in enumerate(z.chunks):
        top = min(-(-hi // LANES) * LANES, z.W)
        w, v = wh[:, lo:top], wl[:, lo:top]
        s = dot(both, w, across)
        s = s[0:m] + s[m:] + dot(high, v, across)
        d = damping(z, keep, top - lo)
        for p in range(4 * L):
            x = state[p, :, lo:top]
            if p < 2 * L:
                x = x - change[p // L, :, lo:top]
            new = x + d * (s[p * z.R : (p + 1) * z.R] - x)
            held[p // L, p % L, :, lo:hi] = new[:, : hi - lo]
        copies.append(
            pltpu.make_async_copy(held.at[:, :, :, lo:hi], out.at[:, :, :, lo:hi], sem.at[i])
        )
        copies[-1].start()
    for copy in copies:
        copy.wait()


def row_code(z, rows, counts, out):
    row = lax.broadcasted_iota(jnp.int32, (z.R + 2 * z.L, LANES), 0)
    lat = lax.axis_index("lat")
    code = jnp.zeros(row.shape, jnp.int32)
    for s in range(z.slots):
        at = rows[lat * z.slots + s] - lat * z.R
        far = at - s
        code = code + jnp.where(row == at, counts[lat * z.slots + s] << (2 * z.bits), 0)
        for b in range(z.bits):
            bit = (far >> b) & 1
            to = at - (bit << b)
            code = code + jnp.where((row == to) & (bit == 1), 1 << b, 0)
            code = code + jnp.where((row == at) & (bit == 1), 1 << (z.bits + b), 0)
            at = to
    before = jnp.maximum(lat * z.slots - 1, 0)
    after = jnp.minimum((lat + 1) * z.slots, z.filters - 1)
    south = jnp.where((lat > 0) & (rows[before] == lat * z.R - 1), counts[before], 0)
    north = jnp.where(
        (lat < z.n_lat - 1) & (rows[after] == (lat + 1) * z.R), counts[after], 0
    )
    ring = jnp.where(row < z.R + z.L, south, north) << (2 * z.bits)
    out[...] = jnp.where(row < z.R, code, ring)


def local(z, tables, fields, surface, filter_rows, keep_counts):
    L, R, W = z.L, z.R, z.W
    f32 = jnp.float32
    wave_high, wave_low, back_high, back_low = tables
    vmem = pl.BlockSpec(memory_space=pltpu.VMEM)

    def call(kernel, outs, ins, scratch=(), flops=1_000_000, aliases={}):
        size = sum(int(np.prod(s)) for s in outs) * 4 + sum(i.size * i.dtype.itemsize for i in ins)
        return pl.pallas_call(
            functools.partial(kernel, z),
            out_shape=[jax.ShapeDtypeStruct(s, f32) for s in outs],
            in_specs=[vmem] * len(ins),
            out_specs=[vmem] * len(outs),
            scratch_shapes=[pltpu.VMEM(s, f32) for s in scratch],
            input_output_aliases=aliases,
            compiler_params=pltpu.CompilerParams(vmem_limit_bytes=VMEM_LIMIT),
            cost_estimate=pl.CostEstimate(flops=flops, bytes_accessed=size, transcendentals=0),
            name=kernel.__name__,
        )(*ins)

    lat, lon = lax.axis_index("lat"), lax.axis_index("lon")
    index = lax.broadcasted_iota(jnp.int32, (R + 2 * L, LANES), 0)
    index = jnp.where(index < R, index, jnp.where(index < R + L, -1, R))
    based = (lat * R + index).astype(f32)
    to_radian = jnp.pi / 180.0
    middle = (FIRST_LAT + (based + 0.5) * ROW_STEP) * to_radian
    northern = (FIRST_LAT + (based + 1.0) * ROW_STEP) * to_radian
    southern = (FIRST_LAT + based * ROW_STEP) * to_radian
    cos_mid = jnp.cos(middle)
    geom = jnp.stack(
        [
            ZONAL_COEF / cos_mid,
            (0.25 * CORIOLIS) * jnp.sin(middle),
            (0.25 * CORIOLIS) * jnp.sin(northern),
            NORTH_COEF * jnp.cos(northern) / cos_mid,
            NORTH_COEF * jnp.cos(southern) / cos_mid,
        ]
    )
    turn = (lon * z.C * jnp.arange(KMAX, dtype=jnp.int32)) % z.N
    angle = turn.astype(f32) * (2.0 * jnp.pi / z.N)
    phase = jnp.stack([jnp.cos(angle), jnp.sin(angle)])

    smem = pl.BlockSpec(memory_space=pltpu.SMEM)
    code = pl.pallas_call(
        functools.partial(row_code, z),
        out_shape=jax.ShapeDtypeStruct((R + 2 * L, LANES), jnp.int32),
        in_specs=[smem] * 2,
        out_specs=vmem,
        name="row_code",
    )(filter_rows, keep_counts)

    lon_one = [(i, i ^ 1) for i in range(z.n_lon)]
    lon_two = [(i, (((i + 1) % z.n_lon ^ 1) - 1) % z.n_lon) for i in range(z.n_lon)]
    lat_two = [(i, i ^ 1) for i in range(z.n_lat) if i ^ 1 < z.n_lat]
    lat_one = [(i, ((i + 1) ^ 1) - 1) for i in range(1, z.n_lat) if ((i + 1) ^ 1) - 1 < z.n_lat]

    def from_below(column):
        if z.n_lev == 2:
            return lax.ppermute(column, "lev", [(0, 1), (1, 0)])
        place = lax.axis_index("lev")
        total = jnp.zeros_like(column)
        for s in range(1, z.n_lev):
            got = lax.ppermute(column, "lev", [(i, i - s) for i in range(s, z.n_lev)])
            total = total + jnp.where(place + s < z.n_lev, got, 0.0)
        return total

    def lon_swap(value, step):
        return lax.ppermute(value, "lon", [(i, i ^ step) for i in range(z.n_lon)])

    def over_lon(sent, own, rows):
        parts = [sent, lon_swap(sent, 2), lon_swap(own, 1), lon_swap(own, 3)]
        if z.n_lon == 4:
            return parts
        (part,) = call(join, [(rows, 2 * KMAX)], parts)
        got, step = lon_swap(part, 4), 8
        while step < z.n_lon:
            part = part + got
            got, step = lon_swap(part, step), step * 2
        return [part, got]

    tile = (R, LANES)
    x = jnp.concatenate([fields.reshape(4 * L, R, z.C), surface[None]], 0)
    x = jnp.pad(x, ((0, 0), (0, 0), (0, W - z.C)))
    m1, m2, after = call(edge_rows, [(R, z.lat_lanes)] * 2 + [tile], [x])
    m1 = lax.ppermute(m1, "lat", lat_one)
    m2 = lax.ppermute(m2, "lat", lat_two)
    e1, e2 = call(edge_columns, [tile, tile], [x, after])
    e1 = lax.ppermute(e1, "lon", lon_one)
    e2 = lax.ppermute(e2, "lon", lon_two)
    tails = (R, 4 * (W - z.base))
    x, sums, t1, t2 = call(
        widen,
        [(z.planes, R, W), (R, W), tails, tails],
        [x, e1, e2],
        [tile] * 2,
        aliases={0: 0},
    )
    t1 = lax.ppermute(t1, "lat", lat_one)
    t2 = lax.ppermute(t2, "lat", lat_two)
    ring_lanes = 2 * z.extra * LANES
    ring, ring_surface = call(unfold, [(7, 2 * L, W), (2 * L, W)], [m1, m2], flops=2_000_000)
    ring, ring_surface, msg = call(
        halo_rows,
        [(7, 2 * L, W), (2 * L, W), (R, W + ring_lanes)],
        [ring, ring_surface, sums, t1, t2],
        aliases={0: 0, 1: 1},
    )
    got = from_below(msg)
    y, yring = call(
        first_step,
        [(4 * L, R, W), (3, 2 * L, W)],
        [x, ring, geom],
        [(4, 2 * L, W), (2 * L, W)],
        flops=10_000_000,
    )
    waves = [wave_high, wave_low, phase, code]
    back = [back_high, back_low, phase, code]
    rows = 4 * L * z.slots
    (part,) = call(tile_and_ring_spectra, [(rows + 6 * L, 2 * KMAX)], [y, yring, *waves])
    surface_tile = x[4 * L]
    sent, own, change, ring_change = call(
        first_level_spectra,
        [(rows + 8 * L + R, 2 * KMAX), (2 * L + R, 2 * KMAX), (2, R, W), (2 * L, W)],
        [surface_tile, ring_surface, got, part, lon_swap(part, 1), geom, *waves],
    )
    parts = over_lon(sent, own, rows + 6 * L)
    ht, htring, uvmodes, msg = call(
        filter_mass,
        [(2 * L, R, W), (2, 2 * L, W), (2 * L * R + 2 * L, 2 * KMAX), (R, W + ring_lanes // 2)],
        [*parts, y, yring, *back],
    )
    got = from_below(msg)
    (y,) = call(
        second_step,
        [(4 * L, R, W)],
        [y, yring, change, ring_change, uvmodes, ht, htring, geom, back_high, back_low, code],
        [(2 * L, R, W), (2 * L, W), (2 * L, W)],
        flops=10_000_000,
    )
    (part,) = call(tile_spectra, [(rows, 2 * KMAX)], [y, *waves])
    sent, own, change = call(
        second_level_spectra,
        [(rows + R, 2 * KMAX), (R, 2 * KMAX), (2, R, W)],
        [surface_tile, ring_surface, got, part, lon_swap(part, 1), geom, *waves],
    )
    parts = over_lon(sent, own, rows)
    return pl.pallas_call(
        functools.partial(filter_all, z),
        out_shape=jax.ShapeDtypeStruct((4, L, R, z.C), f32),
        in_specs=[vmem] * (len(parts) + 6),
        out_specs=pl.BlockSpec(memory_space=pl.ANY),
        scratch_shapes=[
            pltpu.VMEM((4, L, R, z.C), f32),
            pltpu.SemaphoreType.DMA((len(z.chunks),)),
        ],
        compiler_params=pltpu.CompilerParams(vmem_limit_bytes=VMEM_LIMIT),
        name="filter_all",
    )(*parts, y, change, *back)


def wave_tables(z):
    lane = np.arange(z.W)
    j = np.where(lane >= z.W - 2, lane - z.W, lane)
    angle = 2.0 * np.pi * ((j[:, None] * np.arange(KMAX)[None, :]) % z.N) / z.N
    table = np.concatenate([np.cos(angle), np.sin(angle)], 1).astype(np.float32)
    high = table.astype(ml_dtypes.bfloat16)
    low = (table - high.astype(np.float32)).astype(ml_dtypes.bfloat16)
    return high, low


def solution(mesh):
    def run(fields, surface, filter_rows, keep_counts):
        z = Sizes(mesh, fields.shape, filter_rows.shape[0])
        high, low = wave_tables(z)
        tables = [high, low, np.ascontiguousarray(high.T), np.ascontiguousarray(low.T)]

        def body(fields, surface, filter_rows, keep_counts):
            return local(
                z, [jnp.asarray(t) for t in tables], fields, surface, filter_rows, keep_counts
            )

        spec = P(None, "lev", "lat", "lon")
        return jax.shard_map(
            body,
            mesh=mesh,
            in_specs=(spec, P("lat", "lon"), P(), P()),
            out_specs=spec,
            check_vma=False,
        )(fields, surface, filter_rows, keep_counts)

    return run
```

```python
import functools

import jax
import jax.numpy as jnp
import ml_dtypes
import numpy as np
from jax import lax
from jax.experimental import pallas as pl
from jax.experimental.pallas import tpu as pltpu
from jax.sharding import PartitionSpec as P

KMAX = 128
GRAVITY_SCALE = 0.05
BUOYANCY = 0.5
CORIOLIS = 0.3
ZONAL_COEF = 0.08
NORTH_COEF = 0.2
DAMPING = 0.25
FIRST_LAT = -70.0
ROW_STEP = 0.05
LANES = 128
VMEM_LIMIT = 24 * 1024 * 1024


def layer_weight(h, t):
    return GRAVITY_SCALE * (1.0 + h) * (1.0 + BUOYANCY * t)


def east(x):
    return pltpu.roll(x, x.shape[1] - 1, 1)


def west(x):
    return pltpu.roll(x, 1, 1)


def rows_up(x):
    return pltpu.roll(x, x.shape[0] - 1, 0)


def rows_down(x):
    return pltpu.roll(x, 1, 0)


def row_iota(x):
    return lax.broadcasted_iota(jnp.int32, x.shape, 0)


def with_last(x, row):
    return jnp.where(row_iota(x) == x.shape[0] - 1, jnp.broadcast_to(row, x.shape), rows_up(x))


def with_first(x, row):
    return jnp.where(row_iota(x) == 0, jnp.broadcast_to(row, x.shape), rows_down(x))


def wide(geom, k, lo, hi, width):
    return jnp.concatenate([geom[k, lo:hi, :]] * (width // LANES), 1)


class Sizes:
    def __init__(self, mesh, fields_shape, filter_count):
        _, levels, rows, columns = fields_shape
        self.n_lon, self.n_lat, self.n_lev = (mesh.shape[a] for a in ("lon", "lat", "lev"))
        self.L = levels // self.n_lev
        self.R = rows // self.n_lat
        self.C = columns // self.n_lon
        self.N = columns
        self.W = -(-(self.C + 4) // LANES) * LANES
        self.slots = filter_count // self.n_lat
        self.filters = filter_count
        self.planes = 4 * self.L + 1
        self.base = (self.C - 1) // LANES * LANES
        self.tiles = self.W // LANES
        self.extra = -(-self.tiles // self.R)
        whole = self.base // LANES
        self.fold = -(-whole // 2)
        self.lat_lanes = 3 * self.base + (self.fold + -(-whole // self.R)) * LANES
        width = -(-self.base // LANES // 4) * LANES if self.base else self.W
        cuts = [c for c in range(0, self.base + 1, width)] if self.base else [0]
        if self.C - cuts[-1] <= LANES and len(cuts) > 1:
            cuts.pop()
        self.chunks = list(zip(cuts, cuts[1:] + [self.C]))
        self.bits = (self.R - self.slots).bit_length()
        assert self.R == 2 * self.slots and self.base > 0
        assert self.R == 2 * self.L and self.n_lon % 4 == 0 and self.L % 2 == 0
        assert 2 <= self.C - self.base <= LANES - 2 and 2 * self.planes <= LANES


def edge_tiles(z, count, head, tail, width):
    lane = lax.broadcasted_iota(jnp.int32, (z.R, LANES), 1)
    left = jnp.zeros((z.R, LANES), jnp.float32)
    right = left
    first = z.C - width - z.base
    for p in range(count):
        here = (lane >= width * p) & (lane < width * (p + 1))
        left = jnp.where(here, moved(head(p), width * p), left)
        right = jnp.where(here, moved(tail(p), width * p - first), right)
    return left, right


def moved(x, shift):
    shift = shift % x.shape[1]
    return pltpu.roll(x, shift, 1) if shift else x


def by_parity(axis, first, second, even, odd):
    is_even = lax.axis_index(axis) % 2 == 0

    @pl.when(is_even)
    def _():
        first[...] = even
        second[...] = odd

    @pl.when(jnp.logical_not(is_even))
    def _():
        first[...] = odd
        second[...] = even


def patch(z, ref, p, count, width, from_right, from_left):
    lane = lax.broadcasted_iota(jnp.int32, (z.R, LANES), 1)
    last = z.C - z.base
    right = moved(from_right, last - width * p)
    left = moved(from_left, LANES - width - width * p)
    for start in sorted({z.base, z.W - LANES}):
        tile = ref[:, start : start + LANES]
        if start == z.base:
            tile = jnp.where((lane >= last) & (lane < last + width), right, tile)
        if start == z.W - LANES:
            tile = jnp.where(lane >= LANES - width, left, tile)
        ref[:, start : start + LANES] = tile


def near_and_far(z):
    lat_odd = lax.axis_index("lat") % 2 == 1
    near = jnp.where(lat_odd, z.R - 1, 0)
    far = jnp.where(lat_odd, z.R - 2, 1)
    return (near, far), (z.R - 1 - near, z.R - 1 - far)


def edges(z, x, m1, m2, e1, e2):
    L, B = z.L, z.base
    fold = z.fold * LANES
    for msg, (near, far) in zip((m1, m2), near_and_far(z)):
        msg[:, 3 * B :] = jnp.zeros((z.R, z.lat_lanes - 3 * B), jnp.float32)
        for k in range(7):
            f, at = (k, near) if k < 4 else (k - 3, far)
            for l in range(L):
                row = x[f * L + l, pl.ds(at, 1), 0:B]
                to = (k % 2) * L + l
                if k < 6:
                    msg[to : to + 1, k // 2 * B : (k // 2 + 1) * B] = row
                else:
                    msg[l : l + 1, 3 * B : 3 * B + fold] = row[:, 0:fold]
                    msg[L + l : L + l + 1, 3 * B : 4 * B - fold] = row[:, fold:]
        row = x[4 * L, pl.ds(near, 1), 0:B]
        for t in range(B // LANES):
            at = 3 * B + fold + t // z.R * LANES
            msg[t % z.R : t % z.R + 1, at : at + LANES] = row[:, t * LANES : (t + 1) * LANES]
    left, right = edge_tiles(
        z,
        z.planes,
        lambda p: x[p, :, 0:LANES],
        lambda p: x[p, :, z.base : z.base + LANES],
        2,
    )
    by_parity("lon", e1, e2, right, left)


def widen(z, x_in, r1, r2, x, sums, k1, k2, from_right, from_left):
    del x_in
    L, T = z.L, z.W - z.base
    by_parity("lon", from_right, from_left, r1[...], r2[...])
    right, left = from_right[...], from_left[...]
    for p in range(z.planes):
        patch(z, x.at[p], p, z.planes, 2, right, left)
    total = layer_weight(x[2 * L], x[3 * L])
    for l in range(1, L):
        total = total + layer_weight(x[2 * L + l], x[3 * L + l])
    sums[...] = total
    for msg, (near, far) in zip((k1, k2), near_and_far(z)):
        for k in range(8):
            f, at = (k, near) if k < 4 else (k - 3, far) if k < 7 else (4, near)
            for l in range(L):
                p = f * L + l if k < 7 else 4 * L
                to = (k % 2) * L + l
                msg[to : to + 1, k // 2 * T : (k // 2 + 1) * T] = x[p, pl.ds(at, 1), :][:, z.base :]


def put_ring_sums(z, msg, *rows):
    for d, row in enumerate(rows):
        for t in range(z.tiles):
            at = (d * z.extra + t // z.R) * LANES
            msg[t % z.R : t % z.R + 1, at : at + LANES] = row[:, t * LANES : (t + 1) * LANES]


def ring_sum(z, w):
    south = w[0:1]
    north = w[z.L : z.L + 1]
    for l in range(1, z.L):
        south = south + w[l : l + 1]
        north = north + w[z.L + l : z.L + l + 1]
    return south, north


def unfold(z, r1, r2, ring, ring_surface):
    lat_odd = lax.axis_index("lat") % 2 == 1
    L, B = z.L, z.base
    fold = z.fold * LANES

    def place(d, source):
        here = slice(d * L, (d + 1) * L)
        for k in range(6):
            at = (k % 2) * L
            ring[k, here, 0:B] = source[at : at + L, k // 2 * B : (k // 2 + 1) * B]
        ring[6, here, 0:fold] = source[0:L, 3 * B : 3 * B + fold]
        ring[6, here, fold:B] = source[L : 2 * L, 3 * B : 4 * B - fold]
        for t in range(B // LANES):
            at = 3 * B + fold + t // z.R * LANES
            part = source[t % z.R : t % z.R + 1, at : at + LANES]
            ring_surface[here, t * LANES : (t + 1) * LANES] = jnp.broadcast_to(part, (L, LANES))

    @pl.when(lat_odd)
    def _():
        place(0, r2)
        place(1, r1)

    @pl.when(jnp.logical_not(lat_odd))
    def _():
        place(0, r1)
        place(1, r2)


def halo_rows(z, ring_in, surface_in, sums, t1, t2, ring, ring_surface, msg):
    del ring_in, surface_in
    lat_odd = lax.axis_index("lat") % 2 == 1
    L, B, T = z.L, z.base, z.W - z.base
    msg[:, 0 : z.W] = sums[...]
    msg[:, z.W :] = jnp.zeros((z.R, 2 * z.extra * LANES), jnp.float32)

    def place(d, tail):
        here = slice(d * L, (d + 1) * L)
        for k in range(7):
            at = (k % 2) * L
            ring[k, here, B:] = tail[at : at + L, k // 2 * T : (k // 2 + 1) * T]
        ring_surface[here, B:] = tail[L : 2 * L, 3 * T :]

    @pl.when(lat_odd)
    def _():
        place(0, t2)
        place(1, t1)

    @pl.when(jnp.logical_not(lat_odd))
    def _():
        place(0, t1)
        place(1, t2)

    south, north = ring_sum(z, layer_weight(ring[2], ring[3]))
    put_ring_sums(z, msg.at[:, z.W :], north, south)


def in_band(z, shape):
    lat = lax.axis_index("lat")
    row = lax.broadcasted_iota(jnp.int32, shape, 0)
    south = jnp.where(lat > 0, 1.0, 0.0)
    north = jnp.where(lat < z.n_lat - 1, 1.0, 0.0)
    return jnp.where(row < z.L, south, north)


def ring_geopot(z, h, t):
    w = layer_weight(h, t)
    row = row_iota(w)
    level = jnp.where(row < z.L, row, row - z.L)
    q = 0.5 * w
    for s in range(1, z.L):
        q = q + jnp.where(level < z.L - s, pltpu.roll(w, 2 * z.L - s, 0), 0.0)
    return q * in_band(z, w.shape)


def tendencies(coef, u, v, h, t, un, vs, hn, hs, tn, ts, q, qn, which="uvht"):
    zonal, cor, corn, north, south = coef
    out = {}
    if "u" in which:
        a = v + vs
        out["u"] = u + cor * (a + east(a)) - zonal * (east(q) - q)
    if "v" in which:
        b = u + un
        out["v"] = v - corn * (b + west(b)) - NORTH_COEF * (qn - q)
    if "h" in which:
        flux = u * (2.0 + h + east(h)) * 0.5
        out["h"] = (
            h
            - zonal * (flux - west(flux))
            - (north * (v * (2.0 + h + hn) * 0.5) - south * (vs * (2.0 + hs + h) * 0.5))
        )
    if "t" in which:
        out["t"] = (
            t
            - 0.25 * (u + west(u)) * zonal * (east(t) - west(t))
            - (0.25 * NORTH_COEF) * (v + vs) * (tn - ts)
        )
    return out


def advance_tile(z, geom, get, un_row, vs_row, h_ring, t_ring, q_ring, put, qput=None):
    coef = [wide(geom, k, 0, z.R, z.W) for k in range(5)]
    below = None
    for l in reversed(range(z.L)):
        u, v, h, t = (get(f, l) for f in range(4))
        w = layer_weight(h, t)
        q = 0.5 * w if below is None else below + 0.5 * w
        below = w if below is None else below + w
        s, n = l, z.L + l
        new = tendencies(
            coef, u, v, h, t,
            with_last(u, un_row(l)), with_first(v, vs_row(l)),
            with_last(h, h_ring[n : n + 1, :]), with_first(h, h_ring[s : s + 1, :]),
            with_last(t, t_ring[n : n + 1, :]), with_first(t, t_ring[s : s + 1, :]),
            q, with_last(q, q_ring[n : n + 1, :]),
        )
        for f, name in enumerate("uvht"):
            put(f, l, new[name])
        if qput is not None:
            qput(l, q)


def first_step(z, x, ring, geom, y, yring, inner, q_ring):
    L = z.L
    q_ring[...] = ring_geopot(z, ring[2], ring[3])

    def get(f, l):
        return x[f * L + l]

    def put(f, l, value):
        y[f * L + l] = value

    def qput(l, q):
        inner[3, l : l + 1, :] = q[0:1]

    inner[3, L:, :] = jnp.zeros((L, z.W), jnp.float32)
    advance_tile(
        z, geom, get,
        lambda l: ring[0, L + l : L + l + 1, :], lambda l: ring[1, l : l + 1, :],
        ring.at[2], ring.at[3], q_ring, put, qput,
    )
    for l in range(L):
        inner[0, l : l + 1, :] = x[l, 0:1, :]
        inner[0, L + l : L + l + 1, :] = x[L + l, z.R - 1 : z.R, :]
        for k, f in ((1, 2), (2, 3)):
            inner[k, l : l + 1, :] = x[f * L + l, 0:1, :]
            inner[k, L + l : L + l + 1, :] = x[f * L + l, z.R - 1 : z.R, :]
    south = lax.broadcasted_iota(jnp.int32, (2 * L, z.W), 0) < L
    coef = [wide(geom, k, z.R, z.R + 2 * L, z.W) for k in range(5)]
    u, v, h, t = (ring[k] for k in range(4))
    new = tendencies(
        coef, u, v, h, t,
        inner[0], jnp.where(south, ring[4], inner[0]),
        jnp.where(south, inner[1], ring[5]), jnp.where(south, ring[5], inner[1]),
        jnp.where(south, inner[2], ring[6]), jnp.where(south, ring[6], inner[2]),
        q_ring[...], inner[3],
    )
    mask = in_band(z, (2 * L, z.W))
    yring[0] = jnp.where(south, new["v"], new["u"]) * mask
    yring[1] = new["h"] * mask
    yring[2] = new["t"] * mask


def level_part(z, surface, ring_surface, got):
    live = jnp.where(lax.axis_index("lev") < z.n_lev - 1, 1.0, 0.0)
    lat = lax.axis_index("lat")
    out = [surface + live * got[:, 0 : z.W]]
    for d in range((got.shape[1] - z.W) // (z.extra * LANES)):
        inside = lat < z.n_lat - 1 if d == 0 else lat > 0
        parts = []
        for t in range(z.tiles):
            at = z.W + (d * z.extra + t // z.R) * LANES
            parts.append(got[t % z.R : t % z.R + 1, at : at + LANES])
        sums = jnp.concatenate(parts, 1)
        row = (1 - d) * z.L
        out.append(jnp.where(inside, 1.0, 0.0) * (ring_surface[row : row + 1, :] + live * sums))
    return out


def dot(a, b, dims):
    return lax.dot_general(a, b, (dims, ((), ())), preferred_element_type=jnp.float32)


def product(x, wh, wl, dims):
    high = x.astype(jnp.bfloat16)
    wide = high.astype(jnp.float32)
    both = dot(jnp.concatenate([wide, x - wide], 0).astype(jnp.bfloat16), wh[...], dims)
    m = x.shape[0]
    return both[0:m] + both[m:] + dot(high, wl[...], dims)


def masked(z, x):
    tail = x[:, z.base :]
    lane = lax.broadcasted_iota(jnp.int32, tail.shape, 1)
    tail = jnp.where(lane < z.C - z.base, tail, 0.0)
    return jnp.concatenate([x[:, : z.base], tail], 1) if z.base else tail


def spectra(z, x, wh, wl, phase):
    s = product(x, wh, wl, ((1,), (0,)))
    a, b = s[:, :KMAX], s[:, KMAX:]
    c, d = phase[0:1, :], phase[1:2, :]
    return jnp.concatenate([a * c - b * d, a * d + b * c], 1)


def twice(x):
    return jnp.concatenate([x, x], 1)


def code_bit(code, k):
    return twice((code >> k) & 1) == 1


def compress(z, tile, code):
    for b in range(z.bits):
        tile = jnp.where(code_bit(code, b), pltpu.roll(tile, z.R - (1 << b), 0), tile)
    return tile


def expand(z, tile, code):
    for b in reversed(range(z.bits)):
        tile = jnp.where(code_bit(code, z.bits + b), pltpu.roll(tile, 1 << b, 0), tile)
    return tile


def pick_spectra(z, full, code, out):
    code = code[0 : z.R, :]
    row = lax.broadcasted_iota(jnp.int32, (z.R, 2 * KMAX), 0)
    for i in range(2 * z.L):
        a = compress(z, full[2 * i * z.R : (2 * i + 1) * z.R], code)
        b = compress(z, full[(2 * i + 1) * z.R : (2 * i + 2) * z.R], code)
        out[i * z.R : (i + 1) * z.R, :] = jnp.where(row < z.slots, a, pltpu.roll(b, z.slots, 0))


def tile_spectra(z, y, wh, wl, phase, code, out):
    x = masked(z, y[...].reshape(4 * z.L * z.R, z.W))
    pick_spectra(z, spectra(z, x, wh, wl, phase), code, out)


def tile_and_ring_spectra(z, y, yring, wh, wl, phase, code, out):
    m = 4 * z.L * z.R
    x = jnp.concatenate([y[...].reshape(m, z.W), yring[...].reshape(6 * z.L, z.W)], 0)
    full = spectra(z, masked(z, x), wh, wl, phase)
    pick_spectra(z, full, code, out)
    out[4 * z.L * z.slots :, :] = full[m:, :]


def pick_level_part(z, full, code):
    code = code[0 : z.R, :]
    row = lax.broadcasted_iota(jnp.int32, (z.R, 2 * KMAX), 0)
    a = compress(z, full[0 : z.R], code)
    b = compress(z, full[z.R : 2 * z.R], code)
    return jnp.where(row < z.slots, a, pltpu.roll(b, z.slots, 0))


def first_level_spectra(
    z, surface, ring_surface, got, part, part_got, geom, wh, wl, phase, code, sent, own, change, ring_change
):
    L = z.L
    g, gn, gs = level_part(z, surface[...], ring_surface, got)
    du = wide(geom, 0, 0, z.R, z.W) * (east(g) - g)
    dv = NORTH_COEF * (with_last(g, gn) - g)
    shape = (2 * L, z.W)
    south = lax.broadcasted_iota(jnp.int32, shape, 0) < L
    gn = jnp.broadcast_to(gn, shape)
    du_north = wide(geom, 0, z.R, z.R + 2 * L, z.W) * (east(gn) - gn)
    dv_south = NORTH_COEF * jnp.broadcast_to(g[0:1] - gs, shape)
    ring = jnp.where(south, dv_south, du_north) * in_band(z, shape)
    change[0] = du
    change[1] = dv
    ring_change[...] = ring
    full = spectra(z, masked(z, jnp.concatenate([du, dv, ring], 0)), wh, wl, phase)
    own[0 : z.R, :] = pick_level_part(z, full, code)
    own[z.R :, :] = full[2 * z.R :]
    n = part.shape[0]
    sent[0:n, :] = part[...] + part_got[...]
    sent[n:, :] = own[...]


def second_level_spectra(
    z, surface, ring_surface, got, part, part_got, geom, wh, wl, phase, code, sent, own, change
):
    g, gn = level_part(z, surface[...], ring_surface, got)
    du = wide(geom, 0, 0, z.R, z.W) * (east(g) - g)
    dv = NORTH_COEF * (with_last(g, gn) - g)
    change[0] = du
    change[1] = dv
    full = spectra(z, masked(z, jnp.concatenate([du, dv], 0)), wh, wl, phase)
    own[...] = pick_level_part(z, full, code)
    n = part.shape[0]
    sent[0:n, :] = part[...] + part_got[...]
    sent[n:, :] = own[...]


def total_modes(z, parts):
    if len(parts) == 2:
        return parts[0][...] + parts[1][...]
    mine, got, core, across = parts
    n = mine.shape[0] - core.shape[0]
    total = mine[0:n, :] + got[0:n, :]
    level = (mine[n:, :] + core[...]) + (got[n:, :] + across[...])
    both = level[0 : z.R]
    row = lax.broadcasted_iota(jnp.int32, both.shape, 0)
    other = pltpu.roll(both, z.slots, 0)
    du = jnp.where(row < z.slots, both, other)
    dv = jnp.where(row < z.slots, other, both)
    pairs = z.L // 2
    m = 4 * z.L * z.slots
    tiles = [total[i * z.R : (i + 1) * z.R] - (du if i < pairs else dv) for i in range(z.L)]
    tiles.append(total[z.L * z.R : m])
    if n > m:
        tiles += [total[m : m + 2 * z.L] - level[z.R :], total[m + 2 * z.L :]]
    return jnp.concatenate(tiles, 0)


def join(z, mine, got, core, across, out):
    out[...] = total_modes(z, (mine, got, core, across))


def mode_weight(z, keep):
    keep = twice(keep)
    k = lax.broadcasted_iota(jnp.int32, keep.shape, 1)
    k = jnp.where(k < KMAX, k, k - KMAX)
    scale = jnp.where(k == 0, 1.0 / z.N, 2.0 / z.N)
    return jnp.where(k < keep, scale, 0.0)


def keeps(z, code):
    keep = code[...] >> (2 * z.bits)
    return keep[0 : z.R], keep[z.R :]


def damping(z, keep, width):
    value = jnp.where(keep > 0, 1.0 - DAMPING, 0.0)
    return jnp.concatenate([value] * (width // LANES), 1)


def local_modes(total, phase):
    a, b = total[:, :KMAX], total[:, KMAX:]
    c, d = phase[0:1, :], phase[1:2, :]
    return jnp.concatenate([a * c + b * d, b * c - a * d], 1)


def tile_modes(z, modes, code, weight):
    code = code[0 : z.R, :]
    out = []
    for i in range(2 * z.L):
        pair = modes[i * z.R : (i + 1) * z.R]
        out.append(expand(z, pair, code) * weight)
        out.append(expand(z, pltpu.roll(pair, z.R - z.slots, 0), code) * weight)
    return out


def smooth(modes, wh, wl):
    return product(modes, wh, wl, ((1,), (0,)))


def filter_mass(z, *refs):
    parts, refs = refs[:-10], refs[-10:]
    state, sring, wh, wl, phase, code, ht, htring, uvmodes, msg = refs
    L, m = z.L, 4 * z.L * z.slots
    modes = local_modes(total_modes(z, parts), phase)
    keep, rkeep = keeps(z, code)
    weight, rweight = mode_weight(z, keep), mode_weight(z, rkeep)
    ring = [modes[m + k * 2 * L : m + (k + 1) * 2 * L] * rweight for k in range(3)]
    tiles = tile_modes(z, modes, code, weight)
    uvmodes[...] = jnp.concatenate(tiles[: 2 * L] + [ring[0]], 0)
    s = smooth(jnp.concatenate(tiles[2 * L :] + ring[1:], 0), wh, wl)
    damp, rdamp = damping(z, keep, z.W), damping(z, rkeep, z.W)
    for p in range(2 * L):
        x = state[2 * L + p]
        ht[p] = x + damp * (s[p * z.R : (p + 1) * z.R] - x)
    for k in range(2):
        x = sring[1 + k]
        at = 2 * L * z.R + k * 2 * L
        htring[k] = x + rdamp * (s[at : at + 2 * L] - x)
    total = layer_weight(ht[0], ht[L])
    for l in range(1, L):
        total = total + layer_weight(ht[l], ht[L + l])
    _, north = ring_sum(z, layer_weight(htring[0], htring[1]))
    msg[:, 0 : z.W] = total
    msg[:, z.W :] = jnp.zeros((z.R, z.extra * LANES), jnp.float32)
    put_ring_sums(z, msg.at[:, z.W :], north)


def second_step(z, state, sring, change, ring_change, uvmodes, ht, htring, geom, wh, wl, code, y, uv, uvring, q_ring):
    L = z.L
    m = 2 * L * z.R
    s = smooth(uvmodes[...], wh, wl)
    keep, rkeep = keeps(z, code)
    damp, rdamp = damping(z, keep, z.W), damping(z, rkeep, z.W)
    for p in range(2 * L):
        x = state[p] - change[p // L]
        uv[p] = x + damp * (s[p * z.R : (p + 1) * z.R] - x)
    x = sring[0] - ring_change[...]
    uvring[...] = x + rdamp * (s[m:] - x)
    q_ring[...] = ring_geopot(z, htring[0], htring[1])

    def get(f, l):
        return uv[f * L + l] if f < 2 else ht[(f - 2) * L + l]

    def put(f, l, value):
        y[f * L + l] = value

    advance_tile(
        z, geom, get,
        lambda l: uvring[L + l : L + l + 1, :], lambda l: uvring[l : l + 1, :],
        htring.at[0], htring.at[1], q_ring, put,
    )


def filter_all(z, *refs):
    parts, refs = refs[:-9], refs[-9:]
    state, change, wh, wl, phase, code, out, held, sem = refs
    L = z.L
    modes = local_modes(total_modes(z, parts), phase)
    keep, _ = keeps(z, code)
    modes = jnp.concatenate(tile_modes(z, modes, code, mode_weight(z, keep)), 0)
    high = modes.astype(jnp.bfloat16)
    wide_high = high.astype(jnp.float32)
    both = jnp.concatenate([wide_high, modes - wide_high], 0).astype(jnp.bfloat16)
    m = modes.shape[0]
    across = ((1,), (0,))
    copies = []
    for i, (lo, hi) in enumerate(z.chunks):
        top = min(-(-hi // LANES) * LANES, z.W)
        w, v = wh[:, lo:top], wl[:, lo:top]
        s = dot(both, w, across)
        s = s[0:m] + s[m:] + dot(high, v, across)
        d = damping(z, keep, top - lo)
        for p in range(4 * L):
            x = state[p, :, lo:top]
            if p < 2 * L:
                x = x - change[p // L, :, lo:top]
            new = x + d * (s[p * z.R : (p + 1) * z.R] - x)
            held[p // L, p % L, :, lo:hi] = new[:, : hi - lo]
        copies.append(
            pltpu.make_async_copy(held.at[:, :, :, lo:hi], out.at[:, :, :, lo:hi], sem.at[i])
        )
        copies[-1].start()
    for copy in copies:
        copy.wait()


def row_code(z, rows, counts, out):
    row = lax.broadcasted_iota(jnp.int32, (z.R + 2 * z.L, LANES), 0)
    lat = lax.axis_index("lat")
    code = jnp.zeros(row.shape, jnp.int32)
    for s in range(z.slots):
        at = rows[lat * z.slots + s] - lat * z.R
        far = at - s
        code = code + jnp.where(row == at, counts[lat * z.slots + s] << (2 * z.bits), 0)
        for b in range(z.bits):
            bit = (far >> b) & 1
            to = at - (bit << b)
            code = code + jnp.where((row == to) & (bit == 1), 1 << b, 0)
            code = code + jnp.where((row == at) & (bit == 1), 1 << (z.bits + b), 0)
            at = to
    before = jnp.maximum(lat * z.slots - 1, 0)
    after = jnp.minimum((lat + 1) * z.slots, z.filters - 1)
    south = jnp.where((lat > 0) & (rows[before] == lat * z.R - 1), counts[before], 0)
    north = jnp.where(
        (lat < z.n_lat - 1) & (rows[after] == (lat + 1) * z.R), counts[after], 0
    )
    ring = jnp.where(row < z.R + z.L, south, north) << (2 * z.bits)
    out[...] = jnp.where(row < z.R, code, ring)


def local(z, tables, fields, surface, filter_rows, keep_counts):
    L, R, W = z.L, z.R, z.W
    f32 = jnp.float32
    wave_high, wave_low, back_high, back_low = tables
    vmem = pl.BlockSpec(memory_space=pltpu.VMEM)

    def call(kernel, outs, ins, scratch=(), flops=1_000_000, aliases={}):
        size = sum(int(np.prod(s)) for s in outs) * 4 + sum(i.size * i.dtype.itemsize for i in ins)
        return pl.pallas_call(
            functools.partial(kernel, z),
            out_shape=[jax.ShapeDtypeStruct(s, f32) for s in outs],
            in_specs=[vmem] * len(ins),
            out_specs=[vmem] * len(outs),
            scratch_shapes=[pltpu.VMEM(s, f32) for s in scratch],
            input_output_aliases=aliases,
            compiler_params=pltpu.CompilerParams(vmem_limit_bytes=VMEM_LIMIT),
            cost_estimate=pl.CostEstimate(flops=flops, bytes_accessed=size, transcendentals=0),
            name=kernel.__name__,
        )(*ins)

    lat, lon = lax.axis_index("lat"), lax.axis_index("lon")
    index = lax.broadcasted_iota(jnp.int32, (R + 2 * L, LANES), 0)
    index = jnp.where(index < R, index, jnp.where(index < R + L, -1, R))
    based = (lat * R + index).astype(f32)
    to_radian = jnp.pi / 180.0
    middle = (FIRST_LAT + (based + 0.5) * ROW_STEP) * to_radian
    northern = (FIRST_LAT + (based + 1.0) * ROW_STEP) * to_radian
    southern = (FIRST_LAT + based * ROW_STEP) * to_radian
    cos_mid = jnp.cos(middle)
    geom = jnp.stack(
        [
            ZONAL_COEF / cos_mid,
            (0.25 * CORIOLIS) * jnp.sin(middle),
            (0.25 * CORIOLIS) * jnp.sin(northern),
            NORTH_COEF * jnp.cos(northern) / cos_mid,
            NORTH_COEF * jnp.cos(southern) / cos_mid,
        ]
    )
    turn = (lon * z.C * jnp.arange(KMAX, dtype=jnp.int32)) % z.N
    angle = turn.astype(f32) * (2.0 * jnp.pi / z.N)
    phase = jnp.stack([jnp.cos(angle), jnp.sin(angle)])

    smem = pl.BlockSpec(memory_space=pltpu.SMEM)
    code = pl.pallas_call(
        functools.partial(row_code, z),
        out_shape=jax.ShapeDtypeStruct((R + 2 * L, LANES), jnp.int32),
        in_specs=[smem] * 2,
        out_specs=vmem,
        name="row_code",
    )(filter_rows, keep_counts)

    lon_one = [(i, i ^ 1) for i in range(z.n_lon)]
    lon_two = [(i, (((i + 1) % z.n_lon ^ 1) - 1) % z.n_lon) for i in range(z.n_lon)]
    lat_two = [(i, i ^ 1) for i in range(z.n_lat) if i ^ 1 < z.n_lat]
    lat_one = [(i, ((i + 1) ^ 1) - 1) for i in range(1, z.n_lat) if ((i + 1) ^ 1) - 1 < z.n_lat]

    def from_below(column):
        if z.n_lev == 2:
            return lax.ppermute(column, "lev", [(0, 1), (1, 0)])
        place = lax.axis_index("lev")
        total = jnp.zeros_like(column)
        for s in range(1, z.n_lev):
            got = lax.ppermute(column, "lev", [(i, i - s) for i in range(s, z.n_lev)])
            total = total + jnp.where(place + s < z.n_lev, got, 0.0)
        return total

    def lon_swap(value, step):
        return lax.ppermute(value, "lon", [(i, i ^ step) for i in range(z.n_lon)])

    def over_lon(sent, own, rows):
        parts = [sent, lon_swap(sent, 2), lon_swap(own, 1), lon_swap(own, 3)]
        if z.n_lon == 4:
            return parts
        (part,) = call(join, [(rows, 2 * KMAX)], parts)
        got, step = lon_swap(part, 4), 8
        while step < z.n_lon:
            part = part + got
            got, step = lon_swap(part, step), step * 2
        return [part, got]

    tile = (R, LANES)
    x = jnp.concatenate([fields.reshape(4 * L, R, z.C), surface[None]], 0)
    x = jnp.pad(x, ((0, 0), (0, 0), (0, W - z.C)))
    m1, m2, e1, e2 = call(edges, [(R, z.lat_lanes)] * 2 + [tile] * 2, [x])
    m1 = lax.ppermute(m1, "lat", lat_one)
    m2 = lax.ppermute(m2, "lat", lat_two)
    e1 = lax.ppermute(e1, "lon", lon_one)
    e2 = lax.ppermute(e2, "lon", lon_two)
    tails = (R, 4 * (W - z.base))
    x, sums, t1, t2 = call(
        widen,
        [(z.planes, R, W), (R, W), tails, tails],
        [x, e1, e2],
        [tile] * 2,
        aliases={0: 0},
    )
    t1 = lax.ppermute(t1, "lat", lat_one)
    t2 = lax.ppermute(t2, "lat", lat_two)
    ring_lanes = 2 * z.extra * LANES
    ring, ring_surface = call(unfold, [(7, 2 * L, W), (2 * L, W)], [m1, m2], flops=2_000_000)
    ring, ring_surface, msg = call(
        halo_rows,
        [(7, 2 * L, W), (2 * L, W), (R, W + ring_lanes)],
        [ring, ring_surface, sums, t1, t2],
        aliases={0: 0, 1: 1},
    )
    got = from_below(msg)
    y, yring = call(
        first_step,
        [(4 * L, R, W), (3, 2 * L, W)],
        [x, ring, geom],
        [(4, 2 * L, W), (2 * L, W)],
        flops=10_000_000,
    )
    waves = [wave_high, wave_low, phase, code]
    back = [back_high, back_low, phase, code]
    rows = 4 * L * z.slots
    (part,) = call(tile_and_ring_spectra, [(rows + 6 * L, 2 * KMAX)], [y, yring, *waves])
    surface_tile = x[4 * L]
    sent, own, change, ring_change = call(
        first_level_spectra,
        [(rows + 8 * L + R, 2 * KMAX), (2 * L + R, 2 * KMAX), (2, R, W), (2 * L, W)],
        [surface_tile, ring_surface, got, part, lon_swap(part, 1), geom, *waves],
    )
    parts = over_lon(sent, own, rows + 6 * L)
    ht, htring, uvmodes, msg = call(
        filter_mass,
        [(2 * L, R, W), (2, 2 * L, W), (2 * L * R + 2 * L, 2 * KMAX), (R, W + ring_lanes // 2)],
        [*parts, y, yring, *back],
    )
    got = from_below(msg)
    (y,) = call(
        second_step,
        [(4 * L, R, W)],
        [y, yring, change, ring_change, uvmodes, ht, htring, geom, back_high, back_low, code],
        [(2 * L, R, W), (2 * L, W), (2 * L, W)],
        flops=10_000_000,
    )
    (part,) = call(tile_spectra, [(rows, 2 * KMAX)], [y, *waves])
    sent, own, change = call(
        second_level_spectra,
        [(rows + R, 2 * KMAX), (R, 2 * KMAX), (2, R, W)],
        [surface_tile, ring_surface, got, part, lon_swap(part, 1), geom, *waves],
    )
    parts = over_lon(sent, own, rows)
    return pl.pallas_call(
        functools.partial(filter_all, z),
        out_shape=jax.ShapeDtypeStruct((4, L, R, z.C), f32),
        in_specs=[vmem] * (len(parts) + 6),
        out_specs=pl.BlockSpec(memory_space=pl.ANY),
        scratch_shapes=[
            pltpu.VMEM((4, L, R, z.C), f32),
            pltpu.SemaphoreType.DMA((len(z.chunks),)),
        ],
        compiler_params=pltpu.CompilerParams(vmem_limit_bytes=VMEM_LIMIT),
        name="filter_all",
    )(*parts, y, change, *back)


def wave_tables(z):
    lane = np.arange(z.W)
    j = np.where(lane >= z.W - 2, lane - z.W, lane)
    angle = 2.0 * np.pi * ((j[:, None] * np.arange(KMAX)[None, :]) % z.N) / z.N
    table = np.concatenate([np.cos(angle), np.sin(angle)], 1).astype(np.float32)
    high = table.astype(ml_dtypes.bfloat16)
    low = (table - high.astype(np.float32)).astype(ml_dtypes.bfloat16)
    return high, low


def solution(mesh):
    def run(fields, surface, filter_rows, keep_counts):
        z = Sizes(mesh, fields.shape, filter_rows.shape[0])
        high, low = wave_tables(z)
        tables = [high, low, np.ascontiguousarray(high.T), np.ascontiguousarray(low.T)]

        def body(fields, surface, filter_rows, keep_counts):
            return local(
                z, [jnp.asarray(t) for t in tables], fields, surface, filter_rows, keep_counts
            )

        spec = P(None, "lev", "lat", "lon")
        return jax.shard_map(
            body,
            mesh=mesh,
            in_specs=(spec, P("lat", "lon"), P(), P()),
            out_specs=spec,
            check_vma=False,
        )(fields, surface, filter_rows, keep_counts)

    return run
```

```python
import functools

import jax
import jax.numpy as jnp
import ml_dtypes
import numpy as np
from jax import lax
from jax.experimental import pallas as pl
from jax.experimental.pallas import tpu as pltpu
from jax.sharding import PartitionSpec as P

KMAX = 128
GRAVITY_SCALE = 0.05
BUOYANCY = 0.5
CORIOLIS = 0.3
ZONAL_COEF = 0.08
NORTH_COEF = 0.2
DAMPING = 0.25
FIRST_LAT = -70.0
ROW_STEP = 0.05
LANES = 128
VMEM_LIMIT = 24 * 1024 * 1024


def layer_weight(h, t):
    return GRAVITY_SCALE * (1.0 + h) * (1.0 + BUOYANCY * t)


def east(x):
    return pltpu.roll(x, x.shape[1] - 1, 1)


def west(x):
    return pltpu.roll(x, 1, 1)


def rows_up(x):
    return pltpu.roll(x, x.shape[0] - 1, 0)


def rows_down(x):
    return pltpu.roll(x, 1, 0)


def row_iota(x):
    return lax.broadcasted_iota(jnp.int32, x.shape, 0)


def with_last(x, row):
    return jnp.where(row_iota(x) == x.shape[0] - 1, jnp.broadcast_to(row, x.shape), rows_up(x))


def with_first(x, row):
    return jnp.where(row_iota(x) == 0, jnp.broadcast_to(row, x.shape), rows_down(x))


def wide(geom, k, lo, hi, width):
    return jnp.concatenate([geom[k, lo:hi, :]] * (width // LANES), 1)


class Sizes:
    def __init__(self, mesh, fields_shape, filter_count):
        _, levels, rows, columns = fields_shape
        self.n_lon, self.n_lat, self.n_lev = (mesh.shape[a] for a in ("lon", "lat", "lev"))
        self.L = levels // self.n_lev
        self.R = rows // self.n_lat
        self.C = columns // self.n_lon
        self.N = columns
        self.W = -(-(self.C + 4) // LANES) * LANES
        self.slots = filter_count // self.n_lat
        self.filters = filter_count
        self.planes = 4 * self.L + 1
        self.base = (self.C - 1) // LANES * LANES
        self.tiles = self.W // LANES
        self.extra = -(-self.tiles // self.R)
        whole = self.base // LANES
        self.fold = -(-whole // 2)
        self.lat_lanes = 3 * self.base + (self.fold + -(-whole // self.R)) * LANES
        width = -(-self.base // LANES // 4) * LANES if self.base else self.W
        cuts = [c for c in range(0, self.base + 1, width)] if self.base else [0]
        if self.C - cuts[-1] <= LANES and len(cuts) > 1:
            cuts.pop()
        self.chunks = list(zip(cuts, cuts[1:] + [self.C]))
        self.bits = (self.R - self.slots).bit_length()
        assert self.R == 2 * self.slots and self.base > 0
        assert self.R == 2 * self.L and self.n_lon % 4 == 0 and self.L % 2 == 0
        assert 2 <= self.C - self.base <= LANES - 2 and 2 * self.planes <= LANES


def edge_tiles(z, count, head, tail, width):
    lane = lax.broadcasted_iota(jnp.int32, (z.R, LANES), 1)
    left = jnp.zeros((z.R, LANES), jnp.float32)
    right = left
    first = z.C - width - z.base
    for p in range(count):
        here = (lane >= width * p) & (lane < width * (p + 1))
        left = jnp.where(here, moved(head(p), width * p), left)
        right = jnp.where(here, moved(tail(p), width * p - first), right)
    return left, right


def moved(x, shift):
    shift = shift % x.shape[1]
    return pltpu.roll(x, shift, 1) if shift else x


def by_parity(axis, first, second, even, odd):
    is_even = lax.axis_index(axis) % 2 == 0

    @pl.when(is_even)
    def _():
        first[...] = even
        second[...] = odd

    @pl.when(jnp.logical_not(is_even))
    def _():
        first[...] = odd
        second[...] = even


def patch(z, ref, p, count, width, from_right, from_left):
    lane = lax.broadcasted_iota(jnp.int32, (z.R, LANES), 1)
    last = z.C - z.base
    right = moved(from_right, last - width * p)
    left = moved(from_left, LANES - width - width * p)
    for start in sorted({z.base, z.W - LANES}):
        tile = ref[:, start : start + LANES]
        if start == z.base:
            tile = jnp.where((lane >= last) & (lane < last + width), right, tile)
        if start == z.W - LANES:
            tile = jnp.where(lane >= LANES - width, left, tile)
        ref[:, start : start + LANES] = tile


def near_and_far(z):
    lat_even = lax.axis_index("lat") % 2 == 0
    near = jnp.where(lat_even, z.R - 1, 0)
    far = jnp.where(lat_even, z.R - 2, 1)
    return (near, far), (z.R - 1 - near, z.R - 1 - far)


def edges(z, x, m1, m2, e1, e2):
    L, B = z.L, z.base
    fold = z.fold * LANES
    for msg, (near, far) in zip((m1, m2), near_and_far(z)):
        msg[:, 3 * B :] = jnp.zeros((z.R, z.lat_lanes - 3 * B), jnp.float32)
        for k in range(7):
            f, at = (k, near) if k < 4 else (k - 3, far)
            for l in range(L):
                row = x[f * L + l, pl.ds(at, 1), 0:B]
                to = (k % 2) * L + l
                if k < 6:
                    msg[to : to + 1, k // 2 * B : (k // 2 + 1) * B] = row
                else:
                    msg[l : l + 1, 3 * B : 3 * B + fold] = row[:, 0:fold]
                    msg[L + l : L + l + 1, 3 * B : 4 * B - fold] = row[:, fold:]
        row = x[4 * L, pl.ds(near, 1), 0:B]
        for t in range(B // LANES):
            at = 3 * B + fold + t // z.R * LANES
            msg[t % z.R : t % z.R + 1, at : at + LANES] = row[:, t * LANES : (t + 1) * LANES]
    left, right = edge_tiles(
        z,
        z.planes,
        lambda p: x[p, :, 0:LANES],
        lambda p: x[p, :, z.base : z.base + LANES],
        2,
    )
    by_parity("lon", e1, e2, right, left)


def widen(z, x_in, r1, r2, x, sums, k1, k2, from_right, from_left):
    del x_in
    L, T = z.L, z.W - z.base
    by_parity("lon", from_right, from_left, r1[...], r2[...])
    right, left = from_right[...], from_left[...]
    for p in range(z.planes):
        patch(z, x.at[p], p, z.planes, 2, right, left)
    total = layer_weight(x[2 * L], x[3 * L])
    for l in range(1, L):
        total = total + layer_weight(x[2 * L + l], x[3 * L + l])
    sums[...] = total
    for msg, (near, far) in zip((k1, k2), near_and_far(z)):
        for k in range(8):
            f, at = (k, near) if k < 4 else (k - 3, far) if k < 7 else (4, near)
            for l in range(L):
                p = f * L + l if k < 7 else 4 * L
                to = (k % 2) * L + l
                msg[to : to + 1, k // 2 * T : (k // 2 + 1) * T] = x[p, pl.ds(at, 1), :][:, z.base :]


def put_ring_sums(z, msg, *rows):
    for d, row in enumerate(rows):
        for t in range(z.tiles):
            at = (d * z.extra + t // z.R) * LANES
            msg[t % z.R : t % z.R + 1, at : at + LANES] = row[:, t * LANES : (t + 1) * LANES]


def ring_sum(z, w):
    south = w[0:1]
    north = w[z.L : z.L + 1]
    for l in range(1, z.L):
        south = south + w[l : l + 1]
        north = north + w[z.L + l : z.L + l + 1]
    return south, north


def unfold(z, r1, r2, ring, ring_surface):
    lat_even = lax.axis_index("lat") % 2 == 0
    L, B = z.L, z.base
    fold = z.fold * LANES

    def place(d, source):
        here = slice(d * L, (d + 1) * L)
        for k in range(6):
            at = (k % 2) * L
            ring[k, here, 0:B] = source[at : at + L, k // 2 * B : (k // 2 + 1) * B]
        ring[6, here, 0:fold] = source[0:L, 3 * B : 3 * B + fold]
        ring[6, here, fold:B] = source[L : 2 * L, 3 * B : 4 * B - fold]
        for t in range(B // LANES):
            at = 3 * B + fold + t // z.R * LANES
            part = source[t % z.R : t % z.R + 1, at : at + LANES]
            ring_surface[here, t * LANES : (t + 1) * LANES] = jnp.broadcast_to(part, (L, LANES))

    @pl.when(lat_even)
    def _():
        place(0, r2)
        place(1, r1)

    @pl.when(jnp.logical_not(lat_even))
    def _():
        place(0, r1)
        place(1, r2)


def halo_rows(z, ring_in, surface_in, sums, t1, t2, ring, ring_surface, msg):
    del ring_in, surface_in
    lat_even = lax.axis_index("lat") % 2 == 0
    L, B, T = z.L, z.base, z.W - z.base
    msg[:, 0 : z.W] = sums[...]
    msg[:, z.W :] = jnp.zeros((z.R, 2 * z.extra * LANES), jnp.float32)

    def place(d, tail):
        here = slice(d * L, (d + 1) * L)
        for k in range(7):
            at = (k % 2) * L
            ring[k, here, B:] = tail[at : at + L, k // 2 * T : (k // 2 + 1) * T]
        ring_surface[here, B:] = tail[L : 2 * L, 3 * T :]

    @pl.when(lat_even)
    def _():
        place(0, t2)
        place(1, t1)

    @pl.when(jnp.logical_not(lat_even))
    def _():
        place(0, t1)
        place(1, t2)

    south, north = ring_sum(z, layer_weight(ring[2], ring[3]))
    put_ring_sums(z, msg.at[:, z.W :], north, south)


def in_band(z, shape):
    lat = lax.axis_index("lat")
    row = lax.broadcasted_iota(jnp.int32, shape, 0)
    south = jnp.where(lat > 0, 1.0, 0.0)
    north = jnp.where(lat < z.n_lat - 1, 1.0, 0.0)
    return jnp.where(row < z.L, south, north)


def ring_geopot(z, h, t):
    w = layer_weight(h, t)
    row = row_iota(w)
    level = jnp.where(row < z.L, row, row - z.L)
    q = 0.5 * w
    for s in range(1, z.L):
        q = q + jnp.where(level < z.L - s, pltpu.roll(w, 2 * z.L - s, 0), 0.0)
    return q * in_band(z, w.shape)


def tendencies(coef, u, v, h, t, un, vs, hn, hs, tn, ts, q, qn, which="uvht"):
    zonal, cor, corn, north, south = coef
    out = {}
    if "u" in which:
        a = v + vs
        out["u"] = u + cor * (a + east(a)) - zonal * (east(q) - q)
    if "v" in which:
        b = u + un
        out["v"] = v - corn * (b + west(b)) - NORTH_COEF * (qn - q)
    if "h" in which:
        flux = u * (2.0 + h + east(h)) * 0.5
        out["h"] = (
            h
            - zonal * (flux - west(flux))
            - (north * (v * (2.0 + h + hn) * 0.5) - south * (vs * (2.0 + hs + h) * 0.5))
        )
    if "t" in which:
        out["t"] = (
            t
            - 0.25 * (u + west(u)) * zonal * (east(t) - west(t))
            - (0.25 * NORTH_COEF) * (v + vs) * (tn - ts)
        )
    return out


def advance_tile(z, geom, get, un_row, vs_row, h_ring, t_ring, q_ring, put, qput=None):
    coef = [wide(geom, k, 0, z.R, z.W) for k in range(5)]
    below = None
    for l in reversed(range(z.L)):
        u, v, h, t = (get(f, l) for f in range(4))
        w = layer_weight(h, t)
        q = 0.5 * w if below is None else below + 0.5 * w
        below = w if below is None else below + w
        s, n = l, z.L + l
        new = tendencies(
            coef, u, v, h, t,
            with_last(u, un_row(l)), with_first(v, vs_row(l)),
            with_last(h, h_ring[n : n + 1, :]), with_first(h, h_ring[s : s + 1, :]),
            with_last(t, t_ring[n : n + 1, :]), with_first(t, t_ring[s : s + 1, :]),
            q, with_last(q, q_ring[n : n + 1, :]),
        )
        for f, name in enumerate("uvht"):
            put(f, l, new[name])
        if qput is not None:
            qput(l, q)


def first_step(z, x, ring, geom, y, yring, inner, q_ring):
    L = z.L
    q_ring[...] = ring_geopot(z, ring[2], ring[3])

    def get(f, l):
        return x[f * L + l]

    def put(f, l, value):
        y[f * L + l] = value

    def qput(l, q):
        inner[3, l : l + 1, :] = q[0:1]

    inner[3, L:, :] = jnp.zeros((L, z.W), jnp.float32)
    advance_tile(
        z, geom, get,
        lambda l: ring[0, L + l : L + l + 1, :], lambda l: ring[1, l : l + 1, :],
        ring.at[2], ring.at[3], q_ring, put, qput,
    )
    for l in range(L):
        inner[0, l : l + 1, :] = x[l, 0:1, :]
        inner[0, L + l : L + l + 1, :] = x[L + l, z.R - 1 : z.R, :]
        for k, f in ((1, 2), (2, 3)):
            inner[k, l : l + 1, :] = x[f * L + l, 0:1, :]
            inner[k, L + l : L + l + 1, :] = x[f * L + l, z.R - 1 : z.R, :]
    south = lax.broadcasted_iota(jnp.int32, (2 * L, z.W), 0) < L
    coef = [wide(geom, k, z.R, z.R + 2 * L, z.W) for k in range(5)]
    u, v, h, t = (ring[k] for k in range(4))
    new = tendencies(
        coef, u, v, h, t,
        inner[0], jnp.where(south, ring[4], inner[0]),
        jnp.where(south, inner[1], ring[5]), jnp.where(south, ring[5], inner[1]),
        jnp.where(south, inner[2], ring[6]), jnp.where(south, ring[6], inner[2]),
        q_ring[...], inner[3],
    )
    mask = in_band(z, (2 * L, z.W))
    yring[0] = jnp.where(south, new["v"], new["u"]) * mask
    yring[1] = new["h"] * mask
    yring[2] = new["t"] * mask


def level_part(z, surface, ring_surface, got):
    live = jnp.where(lax.axis_index("lev") < z.n_lev - 1, 1.0, 0.0)
    lat = lax.axis_index("lat")
    out = [surface + live * got[:, 0 : z.W]]
    for d in range((got.shape[1] - z.W) // (z.extra * LANES)):
        inside = lat < z.n_lat - 1 if d == 0 else lat > 0
        parts = []
        for t in range(z.tiles):
            at = z.W + (d * z.extra + t // z.R) * LANES
            parts.append(got[t % z.R : t % z.R + 1, at : at + LANES])
        sums = jnp.concatenate(parts, 1)
        row = (1 - d) * z.L
        out.append(jnp.where(inside, 1.0, 0.0) * (ring_surface[row : row + 1, :] + live * sums))
    return out


def dot(a, b, dims):
    return lax.dot_general(a, b, (dims, ((), ())), preferred_element_type=jnp.float32)


def product(x, wh, wl, dims):
    high = x.astype(jnp.bfloat16)
    wide = high.astype(jnp.float32)
    both = dot(jnp.concatenate([wide, x - wide], 0).astype(jnp.bfloat16), wh[...], dims)
    m = x.shape[0]
    return both[0:m] + both[m:] + dot(high, wl[...], dims)


def masked(z, x):
    tail = x[:, z.base :]
    lane = lax.broadcasted_iota(jnp.int32, tail.shape, 1)
    tail = jnp.where(lane < z.C - z.base, tail, 0.0)
    return jnp.concatenate([x[:, : z.base], tail], 1) if z.base else tail


def spectra(z, x, wh, wl, phase):
    s = product(x, wh, wl, ((1,), (0,)))
    a, b = s[:, :KMAX], s[:, KMAX:]
    c, d = phase[0:1, :], phase[1:2, :]
    return jnp.concatenate([a * c - b * d, a * d + b * c], 1)


def twice(x):
    return jnp.concatenate([x, x], 1)


def code_bit(code, k):
    return twice((code >> k) & 1) == 1


def compress(z, tile, code):
    for b in range(z.bits):
        tile = jnp.where(code_bit(code, b), pltpu.roll(tile, z.R - (1 << b), 0), tile)
    return tile


def expand(z, tile, code):
    for b in reversed(range(z.bits)):
        tile = jnp.where(code_bit(code, z.bits + b), pltpu.roll(tile, 1 << b, 0), tile)
    return tile


def pick_spectra(z, full, code, out):
    code = code[0 : z.R, :]
    row = lax.broadcasted_iota(jnp.int32, (z.R, 2 * KMAX), 0)
    for i in range(2 * z.L):
        a = compress(z, full[2 * i * z.R : (2 * i + 1) * z.R], code)
        b = compress(z, full[(2 * i + 1) * z.R : (2 * i + 2) * z.R], code)
        out[i * z.R : (i + 1) * z.R, :] = jnp.where(row < z.slots, a, pltpu.roll(b, z.slots, 0))


def tile_spectra(z, y, wh, wl, phase, code, out):
    x = masked(z, y[...].reshape(4 * z.L * z.R, z.W))
    pick_spectra(z, spectra(z, x, wh, wl, phase), code, out)


def tile_and_ring_spectra(z, y, yring, wh, wl, phase, code, out):
    m = 4 * z.L * z.R
    x = jnp.concatenate([y[...].reshape(m, z.W), yring[...].reshape(6 * z.L, z.W)], 0)
    full = spectra(z, masked(z, x), wh, wl, phase)
    pick_spectra(z, full, code, out)
    out[4 * z.L * z.slots :, :] = full[m:, :]


def pick_level_part(z, full, code):
    code = code[0 : z.R, :]
    row = lax.broadcasted_iota(jnp.int32, (z.R, 2 * KMAX), 0)
    a = compress(z, full[0 : z.R], code)
    b = compress(z, full[z.R : 2 * z.R], code)
    return jnp.where(row < z.slots, a, pltpu.roll(b, z.slots, 0))


def first_level_spectra(
    z, surface, ring_surface, got, part, part_got, geom, wh, wl, phase, code, sent, own, change, ring_change
):
    L = z.L
    g, gn, gs = level_part(z, surface[...], ring_surface, got)
    du = wide(geom, 0, 0, z.R, z.W) * (east(g) - g)
    dv = NORTH_COEF * (with_last(g, gn) - g)
    shape = (2 * L, z.W)
    south = lax.broadcasted_iota(jnp.int32, shape, 0) < L
    gn = jnp.broadcast_to(gn, shape)
    du_north = wide(geom, 0, z.R, z.R + 2 * L, z.W) * (east(gn) - gn)
    dv_south = NORTH_COEF * jnp.broadcast_to(g[0:1] - gs, shape)
    ring = jnp.where(south, dv_south, du_north) * in_band(z, shape)
    change[0] = du
    change[1] = dv
    ring_change[...] = ring
    full = spectra(z, masked(z, jnp.concatenate([du, dv, ring], 0)), wh, wl, phase)
    own[0 : z.R, :] = pick_level_part(z, full, code)
    own[z.R :, :] = full[2 * z.R :]
    n = part.shape[0]
    sent[0:n, :] = part[...] + part_got[...]
    sent[n:, :] = own[...]


def second_level_spectra(
    z, surface, ring_surface, got, part, part_got, geom, wh, wl, phase, code, sent, own, change
):
    g, gn = level_part(z, surface[...], ring_surface, got)
    du = wide(geom, 0, 0, z.R, z.W) * (east(g) - g)
    dv = NORTH_COEF * (with_last(g, gn) - g)
    change[0] = du
    change[1] = dv
    full = spectra(z, masked(z, jnp.concatenate([du, dv], 0)), wh, wl, phase)
    own[...] = pick_level_part(z, full, code)
    n = part.shape[0]
    sent[0:n, :] = part[...] + part_got[...]
    sent[n:, :] = own[...]


def total_modes(z, parts):
    if len(parts) == 2:
        return parts[0][...] + parts[1][...]
    mine, got, core, across = parts
    n = mine.shape[0] - core.shape[0]
    total = mine[0:n, :] + got[0:n, :]
    level = (mine[n:, :] + core[...]) + (got[n:, :] + across[...])
    both = level[0 : z.R]
    row = lax.broadcasted_iota(jnp.int32, both.shape, 0)
    other = pltpu.roll(both, z.slots, 0)
    du = jnp.where(row < z.slots, both, other)
    dv = jnp.where(row < z.slots, other, both)
    pairs = z.L // 2
    m = 4 * z.L * z.slots
    tiles = [total[i * z.R : (i + 1) * z.R] - (du if i < pairs else dv) for i in range(z.L)]
    tiles.append(total[z.L * z.R : m])
    if n > m:
        tiles += [total[m : m + 2 * z.L] - level[z.R :], total[m + 2 * z.L :]]
    return jnp.concatenate(tiles, 0)


def join(z, mine, got, core, across, out):
    out[...] = total_modes(z, (mine, got, core, across))


def mode_weight(z, keep):
    keep = twice(keep)
    k = lax.broadcasted_iota(jnp.int32, keep.shape, 1)
    k = jnp.where(k < KMAX, k, k - KMAX)
    scale = jnp.where(k == 0, 1.0 / z.N, 2.0 / z.N)
    return jnp.where(k < keep, scale, 0.0)


def keeps(z, code):
    keep = code[...] >> (2 * z.bits)
    return keep[0 : z.R], keep[z.R :]


def damping(z, keep, width):
    value = jnp.where(keep > 0, 1.0 - DAMPING, 0.0)
    return jnp.concatenate([value] * (width // LANES), 1)


def local_modes(total, phase):
    a, b = total[:, :KMAX], total[:, KMAX:]
    c, d = phase[0:1, :], phase[1:2, :]
    return jnp.concatenate([a * c + b * d, b * c - a * d], 1)


def tile_modes(z, modes, code, weight):
    code = code[0 : z.R, :]
    out = []
    for i in range(2 * z.L):
        pair = modes[i * z.R : (i + 1) * z.R]
        out.append(expand(z, pair, code) * weight)
        out.append(expand(z, pltpu.roll(pair, z.R - z.slots, 0), code) * weight)
    return out


def smooth(modes, wh, wl):
    return product(modes, wh, wl, ((1,), (0,)))


def filter_mass(z, *refs):
    parts, refs = refs[:-10], refs[-10:]
    state, sring, wh, wl, phase, code, ht, htring, uvmodes, msg = refs
    L, m = z.L, 4 * z.L * z.slots
    modes = local_modes(total_modes(z, parts), phase)
    keep, rkeep = keeps(z, code)
    weight, rweight = mode_weight(z, keep), mode_weight(z, rkeep)
    ring = [modes[m + k * 2 * L : m + (k + 1) * 2 * L] * rweight for k in range(3)]
    tiles = tile_modes(z, modes, code, weight)
    uvmodes[...] = jnp.concatenate(tiles[: 2 * L] + [ring[0]], 0)
    s = smooth(jnp.concatenate(tiles[2 * L :] + ring[1:], 0), wh, wl)
    damp, rdamp = damping(z, keep, z.W), damping(z, rkeep, z.W)
    for p in range(2 * L):
        x = state[2 * L + p]
        ht[p] = x + damp * (s[p * z.R : (p + 1) * z.R] - x)
    for k in range(2):
        x = sring[1 + k]
        at = 2 * L * z.R + k * 2 * L
        htring[k] = x + rdamp * (s[at : at + 2 * L] - x)
    total = layer_weight(ht[0], ht[L])
    for l in range(1, L):
        total = total + layer_weight(ht[l], ht[L + l])
    _, north = ring_sum(z, layer_weight(htring[0], htring[1]))
    msg[:, 0 : z.W] = total
    msg[:, z.W :] = jnp.zeros((z.R, z.extra * LANES), jnp.float32)
    put_ring_sums(z, msg.at[:, z.W :], north)


def second_step(z, state, sring, change, ring_change, uvmodes, ht, htring, geom, wh, wl, code, y, uv, uvring, q_ring):
    L = z.L
    m = 2 * L * z.R
    s = smooth(uvmodes[...], wh, wl)
    keep, rkeep = keeps(z, code)
    damp, rdamp = damping(z, keep, z.W), damping(z, rkeep, z.W)
    for p in range(2 * L):
        x = state[p] - change[p // L]
        uv[p] = x + damp * (s[p * z.R : (p + 1) * z.R] - x)
    x = sring[0] - ring_change[...]
    uvring[...] = x + rdamp * (s[m:] - x)
    q_ring[...] = ring_geopot(z, htring[0], htring[1])

    def get(f, l):
        return uv[f * L + l] if f < 2 else ht[(f - 2) * L + l]

    def put(f, l, value):
        y[f * L + l] = value

    advance_tile(
        z, geom, get,
        lambda l: uvring[L + l : L + l + 1, :], lambda l: uvring[l : l + 1, :],
        htring.at[0], htring.at[1], q_ring, put,
    )


def filter_all(z, *refs):
    parts, refs = refs[:-9], refs[-9:]
    state, change, wh, wl, phase, code, out, held, sem = refs
    L = z.L
    modes = local_modes(total_modes(z, parts), phase)
    keep, _ = keeps(z, code)
    modes = jnp.concatenate(tile_modes(z, modes, code, mode_weight(z, keep)), 0)
    high = modes.astype(jnp.bfloat16)
    wide_high = high.astype(jnp.float32)
    both = jnp.concatenate([wide_high, modes - wide_high], 0).astype(jnp.bfloat16)
    m = modes.shape[0]
    across = ((1,), (0,))
    copies = []
    for i, (lo, hi) in enumerate(z.chunks):
        top = min(-(-hi // LANES) * LANES, z.W)
        w, v = wh[:, lo:top], wl[:, lo:top]
        s = dot(both, w, across)
        s = s[0:m] + s[m:] + dot(high, v, across)
        d = damping(z, keep, top - lo)
        for p in range(4 * L):
            x = state[p, :, lo:top]
            if p < 2 * L:
                x = x - change[p // L, :, lo:top]
            new = x + d * (s[p * z.R : (p + 1) * z.R] - x)
            held[p // L, p % L, :, lo:hi] = new[:, : hi - lo]
        copies.append(
            pltpu.make_async_copy(held.at[:, :, :, lo:hi], out.at[:, :, :, lo:hi], sem.at[i])
        )
        copies[-1].start()
    for copy in copies:
        copy.wait()


def row_code(z, rows, counts, out):
    row = lax.broadcasted_iota(jnp.int32, (z.R + 2 * z.L, LANES), 0)
    lat = lax.axis_index("lat")
    code = jnp.zeros(row.shape, jnp.int32)
    for s in range(z.slots):
        at = rows[lat * z.slots + s] - lat * z.R
        far = at - s
        code = code + jnp.where(row == at, counts[lat * z.slots + s] << (2 * z.bits), 0)
        for b in range(z.bits):
            bit = (far >> b) & 1
            to = at - (bit << b)
            code = code + jnp.where((row == to) & (bit == 1), 1 << b, 0)
            code = code + jnp.where((row == at) & (bit == 1), 1 << (z.bits + b), 0)
            at = to
    before = jnp.maximum(lat * z.slots - 1, 0)
    after = jnp.minimum((lat + 1) * z.slots, z.filters - 1)
    south = jnp.where((lat > 0) & (rows[before] == lat * z.R - 1), counts[before], 0)
    north = jnp.where(
        (lat < z.n_lat - 1) & (rows[after] == (lat + 1) * z.R), counts[after], 0
    )
    ring = jnp.where(row < z.R + z.L, south, north) << (2 * z.bits)
    out[...] = jnp.where(row < z.R, code, ring)


def local(z, tables, fields, surface, filter_rows, keep_counts):
    L, R, W = z.L, z.R, z.W
    f32 = jnp.float32
    wave_high, wave_low, back_high, back_low = tables
    vmem = pl.BlockSpec(memory_space=pltpu.VMEM)

    def call(kernel, outs, ins, scratch=(), flops=1_000_000, aliases={}):
        size = sum(int(np.prod(s)) for s in outs) * 4 + sum(i.size * i.dtype.itemsize for i in ins)
        return pl.pallas_call(
            functools.partial(kernel, z),
            out_shape=[jax.ShapeDtypeStruct(s, f32) for s in outs],
            in_specs=[vmem] * len(ins),
            out_specs=[vmem] * len(outs),
            scratch_shapes=[pltpu.VMEM(s, f32) for s in scratch],
            input_output_aliases=aliases,
            compiler_params=pltpu.CompilerParams(vmem_limit_bytes=VMEM_LIMIT),
            cost_estimate=pl.CostEstimate(flops=flops, bytes_accessed=size, transcendentals=0),
            name=kernel.__name__,
        )(*ins)

    lat, lon = lax.axis_index("lat"), lax.axis_index("lon")
    index = lax.broadcasted_iota(jnp.int32, (R + 2 * L, LANES), 0)
    index = jnp.where(index < R, index, jnp.where(index < R + L, -1, R))
    based = (lat * R + index).astype(f32)
    to_radian = jnp.pi / 180.0
    middle = (FIRST_LAT + (based + 0.5) * ROW_STEP) * to_radian
    northern = (FIRST_LAT + (based + 1.0) * ROW_STEP) * to_radian
    southern = (FIRST_LAT + based * ROW_STEP) * to_radian
    cos_mid = jnp.cos(middle)
    geom = jnp.stack(
        [
            ZONAL_COEF / cos_mid,
            (0.25 * CORIOLIS) * jnp.sin(middle),
            (0.25 * CORIOLIS) * jnp.sin(northern),
            NORTH_COEF * jnp.cos(northern) / cos_mid,
            NORTH_COEF * jnp.cos(southern) / cos_mid,
        ]
    )
    turn = (lon * z.C * jnp.arange(KMAX, dtype=jnp.int32)) % z.N
    angle = turn.astype(f32) * (2.0 * jnp.pi / z.N)
    phase = jnp.stack([jnp.cos(angle), jnp.sin(angle)])

    smem = pl.BlockSpec(memory_space=pltpu.SMEM)
    code = pl.pallas_call(
        functools.partial(row_code, z),
        out_shape=jax.ShapeDtypeStruct((R + 2 * L, LANES), jnp.int32),
        in_specs=[smem] * 2,
        out_specs=vmem,
        name="row_code",
    )(filter_rows, keep_counts)

    lon_one = [(i, i ^ 1) for i in range(z.n_lon)]
    lon_two = [(i, (((i + 1) % z.n_lon ^ 1) - 1) % z.n_lon) for i in range(z.n_lon)]
    lat_one = [(i, i ^ 1) for i in range(z.n_lat) if i ^ 1 < z.n_lat]
    lat_two = [(i, ((i + 1) ^ 1) - 1) for i in range(1, z.n_lat) if ((i + 1) ^ 1) - 1 < z.n_lat]

    def from_below(column):
        if z.n_lev == 2:
            return lax.ppermute(column, "lev", [(0, 1), (1, 0)])
        place = lax.axis_index("lev")
        total = jnp.zeros_like(column)
        for s in range(1, z.n_lev):
            got = lax.ppermute(column, "lev", [(i, i - s) for i in range(s, z.n_lev)])
            total = total + jnp.where(place + s < z.n_lev, got, 0.0)
        return total

    def lon_swap(value, step):
        return lax.ppermute(value, "lon", [(i, i ^ step) for i in range(z.n_lon)])

    def over_lon(sent, own, rows):
        parts = [sent, lon_swap(sent, 2), lon_swap(own, 1), lon_swap(own, 3)]
        if z.n_lon == 4:
            return parts
        (part,) = call(join, [(rows, 2 * KMAX)], parts)
        got, step = lon_swap(part, 4), 8
        while step < z.n_lon:
            part = part + got
            got, step = lon_swap(part, step), step * 2
        return [part, got]

    tile = (R, LANES)
    x = jnp.concatenate([fields.reshape(4 * L, R, z.C), surface[None]], 0)
    x = jnp.pad(x, ((0, 0), (0, 0), (0, W - z.C)))
    m1, m2, e1, e2 = call(edges, [(R, z.lat_lanes)] * 2 + [tile] * 2, [x])
    m1 = lax.ppermute(m1, "lat", lat_one)
    m2 = lax.ppermute(m2, "lat", lat_two)
    e1 = lax.ppermute(e1, "lon", lon_one)
    e2 = lax.ppermute(e2, "lon", lon_two)
    tails = (R, 4 * (W - z.base))
    x, sums, t1, t2 = call(
        widen,
        [(z.planes, R, W), (R, W), tails, tails],
        [x, e1, e2],
        [tile] * 2,
        aliases={0: 0},
    )
    t1 = lax.ppermute(t1, "lat", lat_one)
    t2 = lax.ppermute(t2, "lat", lat_two)
    ring_lanes = 2 * z.extra * LANES
    ring, ring_surface = call(unfold, [(7, 2 * L, W), (2 * L, W)], [m1, m2], flops=2_000_000)
    ring, ring_surface, msg = call(
        halo_rows,
        [(7, 2 * L, W), (2 * L, W), (R, W + ring_lanes)],
        [ring, ring_surface, sums, t1, t2],
        aliases={0: 0, 1: 1},
    )
    got = from_below(msg)
    y, yring = call(
        first_step,
        [(4 * L, R, W), (3, 2 * L, W)],
        [x, ring, geom],
        [(4, 2 * L, W), (2 * L, W)],
        flops=10_000_000,
    )
    waves = [wave_high, wave_low, phase, code]
    back = [back_high, back_low, phase, code]
    rows = 4 * L * z.slots
    (part,) = call(tile_and_ring_spectra, [(rows + 6 * L, 2 * KMAX)], [y, yring, *waves])
    surface_tile = x[4 * L]
    sent, own, change, ring_change = call(
        first_level_spectra,
        [(rows + 8 * L + R, 2 * KMAX), (2 * L + R, 2 * KMAX), (2, R, W), (2 * L, W)],
        [surface_tile, ring_surface, got, part, lon_swap(part, 1), geom, *waves],
    )
    parts = over_lon(sent, own, rows + 6 * L)
    ht, htring, uvmodes, msg = call(
        filter_mass,
        [(2 * L, R, W), (2, 2 * L, W), (2 * L * R + 2 * L, 2 * KMAX), (R, W + ring_lanes // 2)],
        [*parts, y, yring, *back],
    )
    got = from_below(msg)
    (y,) = call(
        second_step,
        [(4 * L, R, W)],
        [y, yring, change, ring_change, uvmodes, ht, htring, geom, back_high, back_low, code],
        [(2 * L, R, W), (2 * L, W), (2 * L, W)],
        flops=10_000_000,
    )
    (part,) = call(tile_spectra, [(rows, 2 * KMAX)], [y, *waves])
    sent, own, change = call(
        second_level_spectra,
        [(rows + R, 2 * KMAX), (R, 2 * KMAX), (2, R, W)],
        [surface_tile, ring_surface, got, part, lon_swap(part, 1), geom, *waves],
    )
    parts = over_lon(sent, own, rows)
    return pl.pallas_call(
        functools.partial(filter_all, z),
        out_shape=jax.ShapeDtypeStruct((4, L, R, z.C), f32),
        in_specs=[vmem] * (len(parts) + 6),
        out_specs=pl.BlockSpec(memory_space=pl.ANY),
        scratch_shapes=[
            pltpu.VMEM((4, L, R, z.C), f32),
            pltpu.SemaphoreType.DMA((len(z.chunks),)),
        ],
        compiler_params=pltpu.CompilerParams(vmem_limit_bytes=VMEM_LIMIT),
        name="filter_all",
    )(*parts, y, change, *back)


def wave_tables(z):
    lane = np.arange(z.W)
    j = np.where(lane >= z.W - 2, lane - z.W, lane)
    angle = 2.0 * np.pi * ((j[:, None] * np.arange(KMAX)[None, :]) % z.N) / z.N
    table = np.concatenate([np.cos(angle), np.sin(angle)], 1).astype(np.float32)
    high = table.astype(ml_dtypes.bfloat16)
    low = (table - high.astype(np.float32)).astype(ml_dtypes.bfloat16)
    return high, low


def solution(mesh):
    def run(fields, surface, filter_rows, keep_counts):
        z = Sizes(mesh, fields.shape, filter_rows.shape[0])
        high, low = wave_tables(z)
        tables = [high, low, np.ascontiguousarray(high.T), np.ascontiguousarray(low.T)]

        def body(fields, surface, filter_rows, keep_counts):
            return local(
                z, [jnp.asarray(t) for t in tables], fields, surface, filter_rows, keep_counts
            )

        spec = P(None, "lev", "lat", "lon")
        return jax.shard_map(
            body,
            mesh=mesh,
            in_specs=(spec, P("lat", "lon"), P(), P()),
            out_specs=spec,
            check_vma=False,
        )(fields, surface, filter_rows, keep_counts)

    return run
```
